32 devices in a mesh: seq: 8 (over z, y), wsh: 4 (over x, core).
Axes of the slice: x: 2, y: 2, z: 4, core: 2. Of those that a mesh axis runs over, the one named last changes fastest.
Arguments:
- tokens: bfloat16 [2, 4, 8192, 768], P(None, 'wsh', 'seq'), may hold values from -6 to 6
- cotangent: bfloat16 [2, 4, 8192, 768], P(None, 'wsh', 'seq'), may hold values from -6 to 6
- lengths: int32 [2, 4], P(None, 'wsh'), may hold values from 2048 to 8192, as said below
- ema_alpha: bfloat16 [768, 16], P('wsh'), may hold values from -7 to -1
- ema_delta: bfloat16 [768, 16], P('wsh'), may hold values from -7 to -2
- ema_beta: bfloat16 [768, 16], P('wsh'), may hold values from -1.5 to 1.5
- ema_eta: bfloat16 [768, 16], P('wsh'), may hold values from -1.5 to 1.5
- ema_omega: bfloat16 [768], P('wsh'), may hold values from -4 to 4
- mix_weight: bfloat16 [768, 3200], P('wsh'), may hold values from -0.4375 to 0.4375
- mix_bias: bfloat16 [3200], P('wsh'), may hold values from -1.796875 to 1.796875
- value_weight: bfloat16 [768, 1536], P('wsh'), may hold values from -0.21875 to 0.21875
- value_bias: bfloat16 [1536], P('wsh'), may hold values from -1.796875 to 1.796875
- qk_gain: bfloat16 [128, 2], P('wsh'), may hold values from 0.5 to 1.5
- qk_bias: bfloat16 [128], P('wsh'), may hold values from -1.796875 to 1.796875
- rel_bias: bfloat16 [256], P('wsh'), may hold values from -5 to 5
- out_weight: bfloat16 [1536, 768], P('wsh'), may hold values from -0.625 to 0.625
- norm_gain: bfloat16 [768, 2], P('wsh'), may hold values from 0.5 to 1.5
- norm_bias: bfloat16 [768, 2], P('wsh'), may hold values from -1.796875 to 1.796875
- ffn_in: bfloat16 [768, 1536], P('wsh'), may hold values from -0.21875 to 0.21875
- ffn_in_bias: bfloat16 [1536], P('wsh'), may hold values from -1.796875 to 1.796875
- ffn_out: bfloat16 [1536, 768], P('wsh'), may hold values from -0.15625 to 0.15625
- ffn_out_bias: bfloat16 [768], P('wsh'), may hold values from -1.796875 to 1.796875
Outputs:
- output: bfloat16 [2, 4, 8192, 768], P(None, 'wsh', 'seq')
- input_grad: bfloat16 [2, 4, 8192, 768], P(None, 'wsh', 'seq')
- alpha_grad: float32 [768, 16], P('wsh')
- delta_grad: float32 [768, 16], P('wsh')
- beta_grad: float32 [768, 16], P('wsh')
- eta_grad: float32 [768, 16], P('wsh')
- omega_grad: float32 [768], P('wsh')
- mix_weight_grad: float32 [768, 3200], P('wsh')
- mix_bias_grad: float32 [3200], P('wsh')
- value_weight_grad: float32 [768, 1536], P('wsh')
- value_bias_grad: float32 [1536], P('wsh')
- qk_gain_grad: float32 [128, 2], P('wsh')
- qk_bias_grad: float32 [128], P('wsh')
- rel_bias_grad: float32 [256], P('wsh')
- out_weight_grad: float32 [1536, 768], P('wsh')
- norm_gain_grad: float32 [768, 2], P('wsh')
- norm_bias_grad: float32 [768, 2], P('wsh')
- ffn_in_grad: float32 [768, 1536], P('wsh')
- ffn_in_bias_grad: float32 [1536], P('wsh')
- ffn_out_grad: float32 [1536, 768], P('wsh')
- ffn_out_bias_grad: float32 [768], P('wsh')
The draws below stay inside these ranges and needn't reach their ends.
Inputs may be any that keep to these rules, and one draw needn't show every extreme that they name: `lengths`: in every micro-batch some sequence uses all 8192 positions.
All inputs are finite; a program needn't handle non-finite values.
Results may differ from the reference program's by a relative error of at most 0.015.
Values may be sent and summed in bfloat16 or wider, within the bound.
A program may use at most 1.125 GiB of HBM per device.

```python
import jax
import jax.numpy as jnp
from jax import lax

D = 768
H = 16
Z = 128
V = 1536
FF = 1536
BLOCK = 128
MICRO = 2
SEQ_LEN = 8192
SEQS = 4
E = 3200


def draw_lengths(key, part):
    key_len, key_full = jax.random.split(key)
    shorter = jax.random.randint(key_len, (MICRO, SEQS), SEQ_LEN // 4, SEQ_LEN + 1, dtype=jnp.int32)
    filled = jax.random.randint(key_full, (MICRO,), 0, SEQS, dtype=jnp.int32)
    column = jnp.arange(SEQS, dtype=jnp.int32)
    return jnp.where(column[None, :] == filled[:, None], SEQ_LEN, shorter).astype(jnp.int32)


def level_of(own_key, dims, shards, smallest, largest):
    loudness = 1.0
    for axis_at, blocks in shards:
        steps = jax.random.uniform(jax.random.fold_in(jax.random.fold_in(own_key, 6), axis_at), (blocks,), jnp.float32, smallest / len(shards), largest / len(shards))
        loudness = loudness * jnp.repeat(jnp.exp(steps), dims[axis_at] // blocks).reshape((-1,) + (1,) * (len(dims) - 1 - axis_at))
    return loudness


def bell_draw(rng, shape, width, limit, shards=(), kind=jnp.bfloat16):
    entries = width * jax.random.normal(rng, shape, jnp.float32)
    if shards:
        entries = entries * level_of(rng, shape, shards, -0.22, 0.18)
    return jnp.clip(entries, -limit, limit).astype(kind)


def setup_inputs(seed: int = 0) -> dict:
    arg_keys = jax.random.split(jax.random.key(seed), 23)
    tokens = bell_draw(arg_keys[0], (MICRO, SEQS, SEQ_LEN, D), 1.0, 6.0, ((1, 4), (2, 8)))
    cotangent = bell_draw(arg_keys[1], (MICRO, SEQS, SEQ_LEN, D), 1.0, 6.0, ((1, 4), (2, 8)))
    lengths = draw_lengths(jax.random.fold_in(arg_keys[22], 71), 0)
    ema_alpha = jnp.clip(-7.0 + 6.0 * jax.random.uniform(arg_keys[3], (D, H), jnp.float32) ** level_of(arg_keys[3], (D, H), ((0, 4),), -0.2, 0.2), -7.0, -1.0).astype(jnp.bfloat16)
    ema_delta = jnp.clip(-7.0 + 5.0 * jax.random.uniform(arg_keys[4], (D, H), jnp.float32) ** level_of(arg_keys[4], (D, H), ((0, 4),), -0.2, 0.2), -7.0, -2.0).astype(jnp.bfloat16)
    ema_beta = bell_draw(arg_keys[5], (D, H), H ** -0.5, 1.5, ((0, 4),))
    ema_eta = bell_draw(arg_keys[6], (D, H), H ** -0.5, 1.5, ((0, 4),))
    ema_omega = bell_draw(arg_keys[7], (D,), 1.0, 4.0, ((0, 4),))
    mix_weight = bell_draw(arg_keys[8], (D, E), (D // 4) ** -0.5, 0.4375, ((0, 4),))
    mix_bias = bell_draw(arg_keys[9], (E,), 0.3, 1.796875, ((0, 4),))
    value_weight = bell_draw(arg_keys[10], (D, V), D ** -0.5, 0.21875, ((0, 4),))
    value_bias = bell_draw(arg_keys[11], (V,), 0.3, 1.796875, ((0, 4),))
    qk_gain = jnp.clip(1.0 + 0.1 * jax.random.normal(arg_keys[12], (Z, 2), jnp.float32), 0.5, 1.5).astype(jnp.bfloat16)
    qk_bias = bell_draw(arg_keys[13], (Z,), 0.3, 1.796875, ((0, 4),))
    rel_bias = bell_draw(arg_keys[14], (2 * BLOCK,), 1.0, 5.0, ((0, 4),))
    out_weight = bell_draw(arg_keys[15], (V, D), (V // 16) ** -0.5, 0.625, ((0, 4),))
    norm_gain = jnp.clip(1.0 + 0.1 * jax.random.normal(arg_keys[16], (D, 2), jnp.float32), 0.5, 1.5).astype(jnp.bfloat16)
    norm_bias = bell_draw(arg_keys[17], (D, 2), 0.3, 1.796875, ((0, 4),))
    ffn_in = bell_draw(arg_keys[18], (D, FF), D ** -0.5, 0.21875, ((0, 4),))
    ffn_in_bias = bell_draw(arg_keys[19], (FF,), 0.3, 1.796875, ((0, 4),))
    ffn_out = bell_draw(arg_keys[20], (FF, D), FF ** -0.5, 0.15625, ((0, 4),))
    ffn_out_bias = bell_draw(arg_keys[21], (D,), 0.3, 1.796875, ((0, 4),))
    return dict(tokens=tokens, cotangent=cotangent, lengths=lengths, ema_alpha=ema_alpha, ema_delta=ema_delta, ema_beta=ema_beta, ema_eta=ema_eta, ema_omega=ema_omega, mix_weight=mix_weight, mix_bias=mix_bias, value_weight=value_weight, value_bias=value_bias, qk_gain=qk_gain, qk_bias=qk_bias, rel_bias=rel_bias, out_weight=out_weight, norm_gain=norm_gain, norm_bias=norm_bias, ffn_in=ffn_in, ffn_in_bias=ffn_in_bias, ffn_out=ffn_out, ffn_out_bias=ffn_out_bias)


HIGHEST = lax.Precision.HIGHEST

@jax.custom_vjp
def low(v):
    return lax.optimization_barrier(v.astype(jnp.bfloat16)).astype(jnp.float32)

@jax.custom_vjp
def low_back(v):
    return v

def low_keep(v):
    return (low(v), None)

def low_pass(kept, grad):
    return (grad,)

def back_keep(v):
    return (v, None)

def back_low(kept, grad):
    return (low(grad),)
low.defvjp(low_keep, low_pass)
low_back.defvjp(back_keep, back_low)

def matmul(left_op, right_op):
    return jnp.dot(left_op, right_op, precision=HIGHEST, preferred_element_type=jnp.float32)

def layer_norm(values, scale, shift):
    center = values - lax.optimization_barrier(jnp.mean(values, axis=-1, keepdims=True))
    inverse = lax.rsqrt(lax.optimization_barrier(jnp.mean(center * center, axis=-1, keepdims=True)) + 1e-05)
    return center * inverse * scale + shift

def ema_filter(rate_logit, damp_logit, in_scale, out_scale, skip_scale, chan_x):
    length = chan_x.shape[0]
    rate_in = jax.nn.sigmoid(rate_logit)
    damping = jax.nn.sigmoid(damp_logit)
    log_keep = jnp.log(1.0 - rate_in * damping)
    kernel_weight = out_scale * (in_scale * rate_in)
    steps_float = jnp.arange(length, dtype=jnp.float32)
    kernel = jnp.zeros((chan_x.shape[1], length), jnp.float32)
    for head_index in range(rate_logit.shape[1]):
        kernel = kernel + kernel_weight[:, head_index:head_index + 1] * jnp.exp(steps_float[None, :] * log_keep[:, head_index:head_index + 1])
    fft_len = 2 * length
    product = jnp.fft.rfft(chan_x.T, n=fft_len, axis=1) * jnp.fft.rfft(kernel, n=fft_len, axis=1)
    smoothed = jnp.fft.irfft(product, n=fft_len, axis=1)[:, :length].T
    return jax.nn.silu(smoothed + skip_scale * chan_x)

def sequence_forward(params, inputs):
    rate_logit, damp_logit, in_scale, out_scale, skip_scale, w_mix, b_mix, w_value, b_value, qk_scale, qk_shift, rel_full, w_out, norm_scale, norm_shift, w_ffn_in, b_ffn_in, w_ffn_out, b_ffn_out = params
    seq_x, live_mask = inputs
    length = seq_x.shape[0]
    model_width = seq_x.shape[1]
    z_width = qk_scale.shape[0]
    v_width = w_value.shape[1]
    chan_x = low_back(seq_x)
    xp_rows = low_back(low(ema_filter(rate_logit, damp_logit, in_scale, out_scale, skip_scale, chan_x)))
    base_rows = low_back(matmul(xp_rows, w_mix) + b_mix)
    update_gate = jax.nn.sigmoid(base_rows[:, :model_width])
    shared = jax.nn.silu(base_rows[:, model_width:model_width + z_width])
    reset_gate = jax.nn.silu(base_rows[:, model_width + z_width:model_width + z_width + v_width])
    h_lin = base_rows[:, model_width + z_width + v_width:]
    v_pre = low_back(matmul(seq_x, w_value) + b_value)
    values = low(jax.nn.silu(v_pre))
    queries = low(shared * qk_scale[:, 0] + qk_shift)
    key_rows = low(shared * qk_scale[:, 1])
    block_count = length // BLOCK
    within = jnp.arange(BLOCK, dtype=jnp.int32)
    rel_matrix = jnp.take(rel_full, within[:, None] - within[None, :] + BLOCK - 1, axis=0)
    raw_scores = jnp.einsum('nid,njd->nij', queries.reshape(block_count, BLOCK, z_width), key_rows.reshape(block_count, BLOCK, z_width), precision=HIGHEST)
    scores = low_back(raw_scores * z_width ** (-0.5) + rel_matrix)
    scores = jnp.where(within[:, None] >= within[None, :], scores, -1e+30)
    weights_low = low(jax.nn.softmax(scores, axis=-1))
    attended = low_back(jnp.einsum('nij,njd->nid', weights_low, values.reshape(block_count, BLOCK, v_width), precision=HIGHEST).reshape(length, v_width))
    mixed_rows = low(reset_gate * attended)
    hidden = jax.nn.silu(h_lin + low_back(matmul(mixed_rows, w_out)))
    residual = seq_x + update_gate * (hidden - seq_x)
    first_norm = layer_norm(residual, norm_scale[:, 0], norm_shift[:, 0])
    f_pre = low_back(matmul(low(first_norm), w_ffn_in) + b_ffn_in)
    branch = low_back(matmul(low(jax.nn.silu(f_pre)), w_ffn_out))
    second = first_norm + branch + b_ffn_out
    return layer_norm(second, norm_scale[:, 1], norm_shift[:, 1]) * live_mask[:, None]

def reference(tokens, cotangent, lengths, ema_alpha, ema_delta, ema_beta, ema_eta, ema_omega, mix_weight, mix_bias, value_weight, value_bias, qk_gain, qk_bias, rel_bias, out_weight, norm_gain, norm_bias, ffn_in, ffn_in_bias, ffn_out, ffn_out_bias):
    params = tuple((member.astype(jnp.float32) for member in (ema_alpha, ema_delta, ema_beta, ema_eta, ema_omega, mix_weight, mix_bias, value_weight, value_bias, qk_gain, qk_bias, rel_bias, out_weight, norm_gain, norm_bias, ffn_in, ffn_in_bias, ffn_out, ffn_out_bias)))
    seq_inputs = tokens.astype(jnp.float32).reshape(MICRO * SEQS, SEQ_LEN, D)
    position = jnp.arange(SEQ_LEN, dtype=jnp.int32)
    live_mask = (position[None, :] < lengths.reshape(-1)[:, None]).astype(jnp.float32)

    def whole(weights, inputs):

        def visit(seq_item):
            return jax.checkpoint(sequence_forward)(weights, seq_item)
        return lax.map(visit, (inputs, live_mask))
    outputs, pullback = jax.vjp(whole, params, seq_inputs)
    param_grads, input_grad = pullback(cotangent.astype(jnp.float32).reshape(MICRO * SEQS, SEQ_LEN, D))
    shape_out = (MICRO, SEQS, SEQ_LEN, D)
    return (outputs.reshape(shape_out).astype(jnp.bfloat16), input_grad.reshape(shape_out).astype(jnp.bfloat16), param_grads[0], param_grads[1], param_grads[2], param_grads[3], param_grads[4], param_grads[5], param_grads[6], param_grads[7], param_grads[8], param_grads[9], param_grads[10], param_grads[11], param_grads[12], param_grads[13], param_grads[14], param_grads[15], param_grads[16], param_grads[17], param_grads[18])
```

```python
import functools

import jax
import jax.numpy as jnp
from jax import lax
from jax.experimental import pallas as pl
from jax.experimental.pallas import tpu as pltpu
from jax.sharding import PartitionSpec as P

BLOCK = 128
LANES = 128
CH = 8
PAD = 8
CHUNK = 768
STRIP = 32
EPSILON = 1e-05
VMEM_LIMIT = 62 * 1024 * 1024
F32 = jnp.float32
BF16 = jnp.bfloat16


def dot_rows(left_op, right_op):
    return jnp.einsum("ri,rj->ij", left_op, right_op, preferred_element_type=jnp.float32)


def skew_matrix(wrapped):
    lead = wrapped.shape[:-1]
    flat = jnp.tile(wrapped, (1,) * len(lead) + (BLOCK,))[..., : BLOCK * (2 * BLOCK - 1)]
    return flat.reshape(lead + (BLOCK, 2 * BLOCK - 1))[..., :BLOCK]


def power(v, n):
    k = 1
    while k < n:
        v = v * v
        k *= 2
    return v

def rows_of(scr, s, T):
    return scr[pl.ds(s, CH, stride=T+PAD), :]

def spread(scr, v, T):
    for k in range(CH):
        scr[k*(T+PAD):k*(T+PAD)+T, :] = v[k*T:(k+1)*T, :]

def collect(scr, T):
    return jnp.concatenate([scr[k*(T+PAD):k*(T+PAD)+T, :] for k in range(CH)], axis=0)

def ends_kernel(H, T, x_ref, q_ref, e_ref, s_ref, scr):
    spread(scr, x_ref[0].astype(F32), T)
    q = [jnp.broadcast_to(q_ref[h:h+1, :], (CH, LANES)) for h in range(H)]
    def step(s, st):
        xs = rows_of(scr, s, T)
        return tuple(q[h]*st[h] + xs for h in range(H))
    st = lax.fori_loop(0, T, step, tuple(jnp.zeros((CH,LANES),F32) for _ in range(H)), unroll=8)
    for h in range(H):
        e_ref[0, h*CH:(h+1)*CH, :] = st[h]
    qT = power(q_ref[...], T)
    c = jnp.zeros((H,LANES),F32)
    for k in range(CH):
        c = qT*c + e_ref[0, pl.ds(k,H,stride=CH), :]
    s_ref[0] = c

def fwd_kernel(H, T, x_ref, q_ref, w_ref, om_ref, e_ref, c_ref, xp_ref, p_ref, f_ref, scr, cs, ps):
    spread(scr, x_ref[0].astype(F32), T)
    qT = power(q_ref[...], T)
    c = c_ref[0]
    for k in range(CH):
        cs[pl.ds(k,H,stride=CH), :] = c
        c = qT*c + e_ref[0, pl.ds(k,H,stride=CH), :]
    q = [jnp.broadcast_to(q_ref[h:h+1, :], (CH, LANES)) for h in range(H)]
    w = [jnp.broadcast_to(w_ref[h:h+1, :], (CH, LANES)) for h in range(H)]
    om = jnp.broadcast_to(om_ref[...], (CH,LANES))
    def step(s, st):
        xs = rows_of(scr, s, T)
        st = tuple(q[h]*st[h] + xs for h in range(H))
        terms = [w[h]*st[h] for h in range(H)]
        while len(terms) > 1:
            terms = [terms[i]+terms[i+1] for i in range(0,len(terms)-1,2)] + ([terms[-1]] if len(terms)%2 else [])
        ps[pl.ds(s, CH, stride=T+PAD), :] = terms[0] + om*xs
        return st
    st = lax.fori_loop(0, T, step, tuple(cs[h*CH:(h+1)*CH, :] for h in range(H)), unroll=8)
    for h in range(H):
        f_ref[0, h*CH:(h+1)*CH, :] = st[h]
    p = collect(ps, T)
    p_ref[0] = p
    xp_ref[0] = (p*jax.nn.sigmoid(p)).astype(xp_ref.dtype)

def bends_kernel(H, T, dxp_ref, p_ref, q_ref, d_ref, e_ref, s_ref, ds):
    p = p_ref[0]
    sg = jax.nn.sigmoid(p)
    d = dxp_ref[0].astype(F32) * (sg*(1.0+p*(1.0-sg)))
    d_ref[0] = d
    spread(ds, d, T)
    q = [jnp.broadcast_to(q_ref[h:h+1, :], (CH, LANES)) for h in range(H)]
    def step(s, st):
        xs = rows_of(ds, T-1-s, T)
        return tuple(q[h]*st[h] + xs for h in range(H))
    st = lax.fori_loop(0, T, step, tuple(jnp.zeros((CH,LANES),F32) for _ in range(H)), unroll=8)
    for h in range(H):
        e_ref[0, h*CH:(h+1)*CH, :] = st[h]
    qT = power(q_ref[...], T)
    c = jnp.zeros((H,LANES),F32)
    for k in reversed(range(CH)):
        c = qT*c + e_ref[0, pl.ds(k,H,stride=CH), :]
    s_ref[0] = c

def bwd_kernel(H, T, d_ref, x_ref, q_ref, qi_ref, w_ref, om_ref, f_ref, e_ref, c_ref, dx_ref, s1_ref, s3_ref, go_ref, scr, cs, dx, ds):
    g = pl.program_id(1)
    x = x_ref[0].astype(F32)
    spread(scr, x, T)
    dv = d_ref[0]
    spread(ds, dv, T)
    qT = power(q_ref[...], T)
    c = c_ref[0]
    for k in reversed(range(CH)):
        cs[pl.ds(k,H,stride=CH), :] = c
        c = qT*c + e_ref[0, pl.ds(k,H,stride=CH), :]
    om = jnp.broadcast_to(om_ref[...], (CH,LANES))
    HH = H//2
    zero = jnp.zeros((CH,LANES),F32)
    @pl.when(g==0)
    def _():
        go_ref[...] = jnp.zeros_like(go_ref)
        s1_ref[...] = jnp.zeros_like(s1_ref)
        s3_ref[...] = jnp.zeros_like(s3_ref)
    go_ref[...] += jnp.sum(dv*x, axis=0, keepdims=True)
    for half in range(2):
        hs = range(half*HH, half*HH+HH)
        q = [jnp.broadcast_to(q_ref[h:h+1, :], (CH, LANES)) for h in hs]
        qi = [jnp.broadcast_to(qi_ref[h:h+1, :], (CH, LANES)) for h in hs]
        w = [jnp.broadcast_to(w_ref[h:h+1, :], (CH, LANES)) for h in hs]
        def step(s, carry):
            l, st, a1, a3 = carry
            at = pl.ds(T-1-s, CH, stride=T+PAD)
            d = ds[at, :]
            xs = scr[at, :]
            a1 = tuple(a1[i] + d*st[i] for i in range(HH))
            l = tuple(q[i]*l[i] + d for i in range(HH))
            st = tuple((st[i]-xs)*qi[i] for i in range(HH))
            a3 = tuple(a3[i] + l[i]*st[i] for i in range(HH))
            terms = [w[i]*l[i] for i in range(HH)]
            while len(terms) > 1:
                terms = [terms[i]+terms[i+1] for i in range(0,len(terms)-1,2)]
            if half == 0:
                dx[at, :] = terms[0] + om*d
            else:
                dx[at, :] = dx[at, :] + terms[0]
            return l, st, a1, a3
        init = (tuple(cs[h*CH:(h+1)*CH,:] for h in hs), tuple(f_ref[0,h*CH:(h+1)*CH,:] for h in hs), (zero,)*HH, (zero,)*HH)
        l, st, a1, a3 = lax.fori_loop(0, T, step, init, unroll=4)
        for i,h in enumerate(hs):
            s1_ref[h:h+1,:] += jnp.sum(a1[i],axis=0,keepdims=True)
            s3_ref[h:h+1,:] += jnp.sum(a3[i],axis=0,keepdims=True)
    dx_ref[0] = collect(dx, T).astype(dx_ref.dtype)

def specs(L,H):
    blk = pl.BlockSpec((1,L,LANES), lambda c,g:(g,0,c))
    par = pl.BlockSpec((H,LANES), lambda c,g:(0,c))
    one = pl.BlockSpec((1,LANES), lambda c,g:(0,c))
    st = pl.BlockSpec((1,H*CH,LANES), lambda c,g:(g,0,c))
    car = pl.BlockSpec((1,H,LANES), lambda c,g:(g,0,c))
    return blk,par,one,st,car

def ema_ends(x,q):
    G,L,C=x.shape; H=q.shape[0]
    blk,par,one,st,car=specs(L,H)
    return pl.pallas_call(functools.partial(ends_kernel,H,L//CH), grid=(C//LANES,G), in_specs=[blk,par], out_specs=[st,car],
      out_shape=[jax.ShapeDtypeStruct((G,H*CH,C),F32),jax.ShapeDtypeStruct((G,H,C),F32)], scratch_shapes=[pltpu.VMEM((L+CH*PAD,LANES),F32)], name="ema_ends")(x,q)

def ema_forward(x,q,w,om,e,c):
    G,L,C=x.shape; H=q.shape[0]
    blk,par,one,st,car=specs(L,H)
    return pl.pallas_call(functools.partial(fwd_kernel,H,L//CH), grid=(C//LANES,G), in_specs=[blk,par,par,one,st,car], out_specs=[blk,blk,st],
      out_shape=[jax.ShapeDtypeStruct((G,L,C),jnp.bfloat16),jax.ShapeDtypeStruct((G,L,C),F32),jax.ShapeDtypeStruct((G,H*CH,C),F32)],
      scratch_shapes=[pltpu.VMEM((L+CH*PAD,LANES),F32),pltpu.VMEM((H*CH,LANES),F32),pltpu.VMEM((L+CH*PAD,LANES),F32)], name="ema_fwd")(x,q,w,om,e,c)

def ema_back_ends(dxp,p,q):
    G,L,C=p.shape; H=q.shape[0]
    blk,par,one,st,car=specs(L,H)
    return pl.pallas_call(functools.partial(bends_kernel,H,L//CH), grid=(C//LANES,G), in_specs=[blk,blk,par], out_specs=[blk,st,car],
      out_shape=[jax.ShapeDtypeStruct((G,L,C),F32),jax.ShapeDtypeStruct((G,H*CH,C),F32),jax.ShapeDtypeStruct((G,H,C),F32)], scratch_shapes=[pltpu.VMEM((L+CH*PAD,LANES),F32)], name="ema_bends")(dxp,p,q)

def ema_backward(d,x,q,qi,w,om,f,e,c):
    G,L,C=x.shape; H=q.shape[0]
    blk,par,one,st,car=specs(L,H)
    return pl.pallas_call(functools.partial(bwd_kernel,H,L//CH), grid=(C//LANES,G), in_specs=[blk,blk,par,par,par,one,st,st,car], out_specs=[blk,par,par,one],
      out_shape=[jax.ShapeDtypeStruct((G,L,C),jnp.bfloat16),jax.ShapeDtypeStruct((H,C),F32),jax.ShapeDtypeStruct((H,C),F32),jax.ShapeDtypeStruct((1,C),F32)],
      scratch_shapes=[pltpu.VMEM((L+CH*PAD,LANES),F32),pltpu.VMEM((H*CH,LANES),F32),pltpu.VMEM((L+CH*PAD,LANES),F32),pltpu.VMEM((L+CH*PAD,LANES),F32)], name="ema_bwd")(d,x,q,qi,w,om,f,e,c)


def sig(v):
    return 0.5 * jnp.tanh(0.5 * v) + 0.5


def dot_nn(left_op, right_op):
    return jnp.dot(left_op, right_op, preferred_element_type=F32)


def dot_nt(left_op, right_op):
    return lax.dot_general(left_op, right_op, (((1,), (1,)), ((), ())), preferred_element_type=F32)


def dot_tn(left_op, right_op):
    return lax.dot_general(left_op, right_op, (((0,), (0,)), ((), ())), preferred_element_type=F32)


def piece_copies(pieces, target, sem, first):
    own, core, across, across_y, across_core, across_y_core = pieces
    rows = own.shape[0]
    half = across.shape[0]
    j = lax.axis_index("wsh")
    i = lax.axis_index("seq")
    bit = lax.rem(i, 2)
    spots = (
        (own, j * rows),
        (core, (j ^ 1) * rows),
        (across, (j ^ 2) * rows + bit * half),
        (across_y, (j ^ 2) * rows + (1 - bit) * half),
        (across_core, (j ^ 3) * rows + bit * half),
        (across_y_core, (j ^ 3) * rows + (1 - bit) * half),
    )
    copies = []
    for n, (piece, start) in enumerate(spots):
        size = piece.shape[0]
        copies.append(
            pltpu.make_async_copy(
                piece, target.at[pl.ds(pl.multiple_of(start, 32), size), :], sem.at[first + n]
            )
        )
    return copies


def bring(groups, sem):
    @pl.when(pl.program_id(0) == 0)
    def _():
        copies = []
        for n, (pieces, target) in enumerate(groups):
            copies.extend(piece_copies(pieces, target, sem, 6 * n))
        for copy in copies:
            copy.start()
        for copy in copies:
            copy.wait()


def fold(rows):
    total = rows[:8]
    for k in range(8, STRIP, 8):
        total = total + rows[k : k + 8]
    return total


def add_sums(ref, at, rows):
    ref[:, at] += jnp.sum(rows, axis=0, keepdims=True)


def mix_fwd_kernel(R, dims, x_ref, xp_ref, bm_ref, bv_ref, qk_ref, rel_ref, *refs):
    D, Z, V = dims
    pieces, refs = refs[:18], refs[18:]
    u_ref, h_ref, r_ref, v_ref, z_ref, p_ref, m_ref, wm, wv, wo, sem = refs
    bring(((pieces[:6], wm), (pieces[6:12], wv), (pieces[12:], wo)), sem)
    xp = xp_ref[...]
    x = x_ref[...]
    z = dot_nn(xp, wm[:, D : D + Z]) + bm_ref[:, D : D + Z]
    z_ref[...] = z
    shared = z * sig(z)
    query = (shared * qk_ref[0:1, :] + qk_ref[2:3, :]).astype(BF16)
    key = (shared * qk_ref[1:2, :]).astype(BF16)
    probs = []
    row = lax.broadcasted_iota(jnp.int32, (BLOCK, BLOCK), 0)
    col = lax.broadcasted_iota(jnp.int32, (BLOCK, BLOCK), 1)
    for b in range(R // BLOCK):
        at = slice(b * BLOCK, (b + 1) * BLOCK)
        score = dot_nt(query[at], key[at]) * Z ** (-0.5) + rel_ref[...]
        score = jnp.where(row >= col, score, -1e30)
        grown = jnp.exp(score - jnp.max(score, axis=-1, keepdims=True))
        prob = grown / jnp.sum(grown, axis=-1, keepdims=True)
        p_ref[at, :] = prob
        probs.append(prob.astype(BF16))
    for c in range(0, V, CHUNK):
        at = slice(c, c + CHUNK)
        rat = slice(D + Z + c, D + Z + c + CHUNK)
        v = dot_nn(x, wv[:, at]) + bv_ref[:, at]
        v_ref[:, at] = v
        value = (v * sig(v)).astype(BF16)
        r = dot_nn(xp, wm[:, rat]) + bm_ref[:, rat]
        r_ref[:, at] = r
        reset = r * sig(r)
        for b in range(R // BLOCK):
            rows = slice(b * BLOCK, (b + 1) * BLOCK)
            m_ref[rows, at] = (reset[rows] * dot_nn(probs[b], value[rows])).astype(BF16)
    u_ref[...] = dot_nn(xp, wm[:, :D]) + bm_ref[:, :D]
    h_ref[...] = dot_nn(xp, wm[:, D + Z + V :]) + bm_ref[:, D + Z + V :] + dot_nn(m_ref[...], wo[...])


def ffn_kernel(R, dims, x_ref, u_ref, h_ref, cot_ref, live_ref, gn_ref, bf_ref, bo_ref, *refs):
    D, FF = dims
    pieces, refs = refs[:12], refs[12:]
    (
        o_ref, h1_ref, act_ref, dg_ref, df_ref, dm_ref, du_ref, dt_ref, sd_ref, sf_ref,
        wi, wo, f_scr, n1_scr, a_scr, i1_scr, sem,
    ) = refs
    bring(((pieces[:6], wi), (pieces[6:], wo)), sem)

    @pl.when(pl.program_id(0) == 0)
    def _():
        sd_ref[...] = jnp.zeros_like(sd_ref)
        sf_ref[...] = jnp.zeros_like(sf_ref)

    g1, g2, b1, b2 = (gn_ref[k : k + 1, :] for k in range(4))

    def first(s, _):
        at = pl.ds(pl.multiple_of(s * STRIP, STRIP), STRIP)
        x = x_ref[at, :].astype(F32)
        h = h_ref[at, :]
        y = x + sig(u_ref[at, :]) * (h * sig(h) - x)
        center = y - jnp.mean(y, axis=-1, keepdims=True)
        inverse = lax.rsqrt(jnp.mean(center * center, axis=-1, keepdims=True) + EPSILON)
        n1 = center * inverse
        n1_scr[at, :] = n1
        i1_scr[at, :] = jnp.broadcast_to(inverse, (STRIP, 128))
        h1_ref[at, :] = (n1 * g1 + b1).astype(BF16)
        return 0

    lax.fori_loop(0, R // STRIP, first, 0, unroll=2)
    for c in range(0, FF, CHUNK):
        at = slice(c, c + CHUNK)
        f = dot_nn(h1_ref[...], wi[:, at]) + bf_ref[:, at]
        f_scr[:, at] = f
        act_ref[:, at] = (f * sig(f)).astype(BF16)
    a_scr[...] = dot_nn(act_ref[...], wo[...])

    def second(s, sums):
        at = pl.ds(pl.multiple_of(s * STRIP, STRIP), STRIP)
        y2 = n1_scr[at, :] * g1 + b1 + a_scr[at, :] + bo_ref[...]
        center = y2 - jnp.mean(y2, axis=-1, keepdims=True)
        inverse = lax.rsqrt(jnp.mean(center * center, axis=-1, keepdims=True) + EPSILON)
        n2 = center * inverse
        live = live_ref[at, :]
        o_ref[at, :] = ((n2 * g2 + b2) * live).astype(BF16)
        dn = cot_ref[at, :].astype(F32) * live
        w = dn * g2
        dy2 = inverse * (
            w - jnp.mean(w, axis=-1, keepdims=True) - n2 * jnp.mean(w * n2, axis=-1, keepdims=True)
        )
        a_scr[at, :] = dy2
        dg_ref[at, :] = dy2.astype(BF16)
        s_gain, s_shift, s_bias = sums
        return s_gain + fold(dn * n2), s_shift + fold(dn), s_bias + fold(dy2)

    zero = jnp.zeros((8, D), F32)
    s_gain, s_shift, s_bias = lax.fori_loop(0, R // STRIP, second, (zero, zero, zero), unroll=2)
    sd_ref[1:2, :] += jnp.sum(s_gain, axis=0, keepdims=True)
    sd_ref[3:4, :] += jnp.sum(s_shift, axis=0, keepdims=True)
    sd_ref[4:5, :] += jnp.sum(s_bias, axis=0, keepdims=True)
    for c in range(0, FF, CHUNK):
        at = slice(c, c + CHUNK)
        f = f_scr[:, at]
        s = sig(f)
        df = (dot_nt(dg_ref[...], wo[at, :]) * (s * (1.0 + f * (1.0 - s)))).astype(BF16)
        df_ref[:, at] = df
        add_sums(sf_ref, at, df.astype(F32))
    a_scr[...] += dot_nt(df_ref[...], wi[...])

    def third(k, sums):
        at = pl.ds(pl.multiple_of(k * STRIP, STRIP), STRIP)
        dh1 = a_scr[at, :]
        n1 = n1_scr[at, :]
        w = dh1 * g1
        dy = i1_scr[at, 0:1] * (
            w - jnp.mean(w, axis=-1, keepdims=True) - n1 * jnp.mean(w * n1, axis=-1, keepdims=True)
        )
        x = x_ref[at, :].astype(F32)
        h = h_ref[at, :]
        sh = sig(h)
        gate = sig(u_ref[at, :])
        rest = 1.0 - gate
        dyg = dy * gate
        dm_ref[at, :] = (dyg * (sh * (1.0 + h * (1.0 - sh)))).astype(BF16)
        du_ref[at, :] = (dyg * (h * sh - x) * rest).astype(BF16)
        dt_ref[at, :] = dy * rest
        s_gain, s_shift = sums
        return s_gain + fold(dh1 * n1), s_shift + fold(dh1)

    s_gain, s_shift = lax.fori_loop(0, R // STRIP, third, (zero, zero), unroll=2)
    sd_ref[0:1, :] += jnp.sum(s_gain, axis=0, keepdims=True)
    sd_ref[2:3, :] += jnp.sum(s_shift, axis=0, keepdims=True)


def mix_bwd_kernel(R, dims, dm_ref, du_ref, dt_ref, r_ref, v_ref, z_ref, p_ref, qk_ref, *refs):
    D, Z, V = dims
    pieces, refs = refs[:18], refs[18:]
    db_ref, dv_ref, dxp_ref, do_ref, sm_ref, sv_ref, sq_ref, ss_ref, wm, wv, wo, sem = refs
    bring(((pieces[:6], wm), (pieces[6:12], wv), (pieces[12:], wo)), sem)

    @pl.when(pl.program_id(0) == 0)
    def _():
        for ref in (sm_ref, sv_ref, sq_ref, ss_ref):
            ref[...] = jnp.zeros_like(ref)

    dm = dm_ref[...]
    du = du_ref[...]
    db_ref[:, :D] = du
    db_ref[:, D + Z + V :] = dm
    add_sums(sm_ref, slice(0, D), du.astype(F32))
    add_sums(sm_ref, slice(D + Z + V, 2 * D + Z + V), dm.astype(F32))
    blocks = [slice(b * BLOCK, (b + 1) * BLOCK) for b in range(R // BLOCK)]
    full = [p_ref[rows, :] for rows in blocks]
    probs = [prob.astype(BF16) for prob in full]
    dprob = [jnp.zeros((BLOCK, BLOCK), F32) for _ in blocks]
    for c in range(0, V, CHUNK):
        at = slice(c, c + CHUNK)
        rat = slice(D + Z + c, D + Z + c + CHUNK)
        dmix = dot_nt(dm, wo[at, :])
        r = r_ref[:, at]
        v = v_ref[:, at]
        sr = sig(r)
        sv = sig(v)
        value = (v * sv).astype(BF16)
        datt = (dmix * (r * sr)).astype(BF16)
        turned = dmix * (sr * (1.0 + r * (1.0 - sr)))
        slope = sv * (1.0 + v * (1.0 - sv))
        sum_r = jnp.zeros((1, CHUNK), F32)
        sum_v = jnp.zeros((1, CHUNK), F32)
        for b, rows in enumerate(blocks):
            dr = (turned[rows] * dot_nn(probs[b], value[rows])).astype(BF16)
            db_ref[rows, rat] = dr
            sum_r += jnp.sum(dr.astype(F32), axis=0, keepdims=True)
            dprob[b] += dot_nt(datt[rows], value[rows])
            dv = (dot_tn(probs[b], datt[rows]) * slope[rows]).astype(BF16)
            dv_ref[rows, at] = dv
            sum_v += jnp.sum(dv.astype(F32), axis=0, keepdims=True)
        sm_ref[:, rat] += sum_r
        sv_ref[:, at] += sum_v
    for b, rows in enumerate(blocks):
        z = z_ref[rows, :]
        sz = sig(z)
        shared = z * sz
        query = (shared * qk_ref[0:1, :] + qk_ref[2:3, :]).astype(BF16)
        key = (shared * qk_ref[1:2, :]).astype(BF16)
        inner = jnp.sum(full[b] * dprob[b], axis=-1, keepdims=True)
        ds = (full[b] * (dprob[b] - inner)).astype(BF16)
        ss_ref[...] += ds.astype(F32)
        dq = dot_nn(ds, key) * Z ** (-0.5)
        dk = dot_tn(ds, query) * Z ** (-0.5)
        sq_ref[0:1, :] += jnp.sum(dq * shared, axis=0, keepdims=True)
        sq_ref[1:2, :] += jnp.sum(dk * shared, axis=0, keepdims=True)
        sq_ref[2:3, :] += jnp.sum(dq, axis=0, keepdims=True)
        dz = (dq * qk_ref[0:1, :] + dk * qk_ref[1:2, :]) * (sz * (1.0 + z * (1.0 - sz)))
        dz = dz.astype(BF16)
        db_ref[rows, D : D + Z] = dz
        add_sums(sm_ref, slice(D, D + Z), dz.astype(F32))
    do_ref[...] = dt_ref[...] + dot_nt(dv_ref[...], wv[...])
    dxp_ref[...] = dot_nt(db_ref[...], wm[...]).astype(BF16)


def any_specs(n):
    return [pl.BlockSpec(memory_space=pl.ANY)] * n


def tile(R, n):
    return pl.BlockSpec((R, n), lambda t: (t, 0))


def fixed(r, n):
    return pl.BlockSpec((r, n), lambda t: (0, 0))


def shape(r, n, dtype=F32):
    return jax.ShapeDtypeStruct((r, n), dtype)


def mix_forward(R, x, xp, bm, bv, qk, rel, pieces):
    T, D = x.shape
    V = bv.shape[1]
    Z = qk.shape[1]
    E = bm.shape[1]
    return pl.pallas_call(
        functools.partial(mix_fwd_kernel, R, (D, Z, V)),
        grid=(T // R,),
        in_specs=[tile(R, D), tile(R, D), fixed(1, E), fixed(1, V), fixed(8, Z), fixed(BLOCK, BLOCK)]
        + any_specs(18),
        out_specs=[tile(R, D), tile(R, D), tile(R, V), tile(R, V), tile(R, Z), tile(R, BLOCK), tile(R, V)],
        out_shape=[
            shape(T, D), shape(T, D), shape(T, V), shape(T, V), shape(T, Z), shape(T, BLOCK), shape(T, V, BF16),
        ],
        scratch_shapes=[
            pltpu.VMEM((D, E), BF16), pltpu.VMEM((D, V), BF16), pltpu.VMEM((V, D), BF16),
            pltpu.SemaphoreType.DMA((18,)),
        ],
        compiler_params=pltpu.CompilerParams(vmem_limit_bytes=VMEM_LIMIT),
        cost_estimate=pl.CostEstimate(flops=2 * T * D * (E + 2 * V), bytes_accessed=40 * T * D, transcendentals=T * (E + V)),
        name="mix_forward",
    )(x, xp, bm, bv, qk, rel, *pieces)


def ffn_both(R, x, u, h, cot, live, norms, bf, bo, pieces):
    T, D = x.shape
    FF = bf.shape[1]
    return pl.pallas_call(
        functools.partial(ffn_kernel, R, (D, FF)),
        grid=(T // R,),
        in_specs=[tile(R, D), tile(R, D), tile(R, D), tile(R, D), tile(R, 1), fixed(8, D), fixed(1, FF), fixed(1, D)]
        + any_specs(12),
        out_specs=[
            tile(R, D), tile(R, D), tile(R, FF), tile(R, D), tile(R, FF), tile(R, D), tile(R, D), tile(R, D),
            fixed(8, D), fixed(1, FF),
        ],
        out_shape=[
            shape(T, D, BF16), shape(T, D, BF16), shape(T, FF, BF16), shape(T, D, BF16), shape(T, FF, BF16),
            shape(T, D, BF16), shape(T, D, BF16), shape(T, D), shape(8, D), shape(1, FF),
        ],
        scratch_shapes=[
            pltpu.VMEM((D, FF), BF16), pltpu.VMEM((FF, D), BF16), pltpu.VMEM((R, FF), F32), pltpu.VMEM((R, D), F32),
            pltpu.VMEM((R, D), F32), pltpu.VMEM((R, 128), F32), pltpu.SemaphoreType.DMA((12,)),
        ],
        compiler_params=pltpu.CompilerParams(vmem_limit_bytes=VMEM_LIMIT),
        cost_estimate=pl.CostEstimate(flops=8 * T * D * FF, bytes_accessed=40 * T * D, transcendentals=T * 2 * FF),
        name="ffn_both",
    )(x, u, h, cot, live, norms, bf, bo, *pieces)


def mix_backward(R, dm, du, dt, r, v, z, p, qk, pieces):
    T, D = dm.shape
    V = r.shape[1]
    Z = qk.shape[1]
    E = 2 * D + Z + V
    return pl.pallas_call(
        functools.partial(mix_bwd_kernel, R, (D, Z, V)),
        grid=(T // R,),
        in_specs=[
            tile(R, D), tile(R, D), tile(R, D), tile(R, V), tile(R, V), tile(R, Z), tile(R, BLOCK), fixed(8, Z),
        ]
        + any_specs(18),
        out_specs=[
            tile(R, E), tile(R, V), tile(R, D), tile(R, D), fixed(1, E), fixed(1, V), fixed(8, Z), fixed(BLOCK, BLOCK),
        ],
        out_shape=[
            shape(T, E, BF16), shape(T, V, BF16), shape(T, D, BF16), shape(T, D), shape(1, E), shape(1, V),
            shape(8, Z), shape(BLOCK, BLOCK),
        ],
        scratch_shapes=[
            pltpu.VMEM((D, E), BF16), pltpu.VMEM((D, V), BF16), pltpu.VMEM((V, D), BF16),
            pltpu.SemaphoreType.DMA((18,)),
        ],
        compiler_params=pltpu.CompilerParams(vmem_limit_bytes=VMEM_LIMIT),
        cost_estimate=pl.CostEstimate(flops=2 * T * D * (E + 2 * V), bytes_accessed=40 * T * D, transcendentals=T * 2 * V),
        name="mix_backward",
    )(dm, du, dt, r, v, z, p, qk, *pieces)


def exchange(value, axis, step):
    return lax.ppermute(value, axis, [(k, k ^ step) for k in range(lax.axis_size(axis))])


def shift(value, axis, step):
    n = lax.axis_size(axis)
    return lax.ppermute(value, axis, [(k, k + step) for k in range(n) if 0 <= k + step < n])


def weight_pieces(own):
    half = own.shape[0] // 2
    bit = lax.rem(lax.axis_index("seq"), 2)
    part = lax.dynamic_slice_in_dim(own, bit * half, half, 0)
    across = exchange(part, "wsh", 2)
    across_y = exchange(across, "seq", 1)
    core = exchange(own, "wsh", 1)
    return (own, core, across, across_y, exchange(across, "wsh", 1), exchange(across_y, "wsh", 1))


def gather_small(own):
    j = lax.axis_index("wsh")
    pair = jnp.stack([own, exchange(own, "wsh", 1)])
    four = jnp.concatenate([pair, exchange(pair, "wsh", 2)])
    return jnp.stack([lax.dynamic_index_in_dim(four, j ^ k, 0, False) for k in range(4)])


def carry_in(states, decay, sign):
    n = lax.axis_size("seq")
    total = shift(states, "seq", sign)
    factor = decay
    for k in range(2, 5):
        if k < n:
            total = total + factor * shift(states, "seq", sign * k)
        factor = factor * decay
    window, factor = 4, factor
    while window < n:
        grown, scale = total, factor
        for k in range(1, 4):
            if k * window < n:
                grown = grown + scale * shift(total, "seq", sign * k * window)
            scale = scale * factor
        total, factor, window = grown, scale, window * 4
    return total


def pick(value, dim, bit):
    return lax.dynamic_index_in_dim(value, bit, dim, False)


def halve(value, dim, axis, step):
    bit = lax.rem(lax.axis_index(axis) // step, 2)
    sent = exchange(pick(value, dim, 1 - bit).astype(BF16), axis, step)
    return pick(value, dim, bit) + sent.astype(F32)


def reduce_grad(grad, order):
    rows, cols = grad.shape
    n_seq, n_wsh = lax.axis_size("seq"), lax.axis_size("wsh")
    steps = [2**k for k in reversed(range(n_seq.bit_length() - 1))]
    labels = ["x", "c"] + [("seq", s) for s in steps]
    value = grad.reshape((2, 2) + (2,) * len(steps) + (rows // n_wsh // n_seq, cols))
    marks = [("wsh", 2), ("wsh", 1)] + [("seq", s) for s in steps]
    plan = [("wsh", 1)] + (
        [("wsh", 2), ("seq", 1), ("seq", 2)] * 2
    )[order : order + 3]
    plan += [("seq", s) for s in reversed(steps) if ("seq", s) not in plan]
    for mark in plan:
        value = halve(value, marks.index(mark), *mark)
        marks.remove(mark)
    return value.astype(BF16)


def spread_grad(mine):
    i = lax.axis_index("seq")
    n = lax.axis_size("seq")
    steps = []
    step = n // 2
    while step:
        steps.append(step)
        step //= 2
    block = mine[None]
    for step in reversed(steps):
        bit = lax.rem(i // step, 2)
        other = exchange(block, "seq", step)
        first = jnp.where(bit == 0, block, other)
        second = jnp.where(bit == 0, other, block)
        block = jnp.concatenate([first, second], axis=0)
    return block.reshape(-1, mine.shape[-1]).astype(F32)


def sum_small(value):
    j = lax.axis_index("wsh")
    total = lax.dynamic_index_in_dim(value, j, 0, False)
    for d in range(1, 4):
        total = total + exchange(lax.dynamic_index_in_dim(value, j ^ d, 0, False), "wsh", d)
    step = 1
    while step < lax.axis_size("seq"):
        total = total + exchange(total, "seq", step)
        step *= 2
    return total


def body(
    tokens, cotangent, lengths, ema_alpha, ema_delta, ema_beta, ema_eta, ema_omega, mix_weight, mix_bias,
    value_weight, value_bias, qk_gain, qk_bias, rel_bias, out_weight, norm_gain, norm_bias, ffn_in, ffn_in_bias,
    ffn_out, ffn_out_bias,
):
    micro, seqs, L, D = tokens.shape
    G = micro * seqs
    T = G * L
    H = ema_alpha.shape[1]
    R = min(512, T)
    n_wsh = lax.axis_size("wsh")
    i = lax.axis_index("seq")
    Z = qk_gain.shape[0] * n_wsh
    V = value_weight.shape[1]
    FF = ffn_in.shape[1]

    wm, wv, wo, wi, wf = (weight_pieces(w) for w in (mix_weight, value_weight, out_weight, ffn_in, ffn_out))
    chan = gather_small(
        jnp.concatenate(
            [ema_alpha, ema_delta, ema_beta, ema_eta, ema_omega[:, None], norm_gain, norm_bias, ffn_out_bias[:, None]],
            axis=1,
        )
    )
    chan = chan.reshape(D, -1).T.astype(F32)
    flat_parts = (mix_bias, value_bias, ffn_in_bias, rel_bias, qk_gain[:, 0], qk_gain[:, 1], qk_bias)
    flat = gather_small(jnp.concatenate(flat_parts)).astype(F32)
    vectors, start = [], 0
    for part in flat_parts:
        vectors.append(flat[:, start : start + part.shape[0]].reshape(1, -1))
        start += part.shape[0]
    bm, bv, bf, rel, gain_q, gain_k, shift_q = vectors
    rate = jax.nn.sigmoid(chan[0:H])
    damp = jax.nn.sigmoid(chan[H : 2 * H])
    beta = chan[2 * H : 3 * H]
    eta = chan[3 * H : 4 * H]
    omega = chan[4 * H : 4 * H + 1]
    norms = jnp.concatenate([chan[4 * H + 1 : 4 * H + 5], jnp.zeros((4, D), F32)])
    bo = chan[4 * H + 5 : 4 * H + 6]
    qk = jnp.concatenate([gain_q, gain_k, shift_q, jnp.zeros((5, Z), F32)])
    rel_matrix = skew_matrix(jnp.roll(rel[0, ::-1], BLOCK))
    keep = 1.0 - rate * damp
    weight = eta * beta * rate
    decay = power(keep, L)
    x3 = tokens.reshape(G, L, D)
    x = tokens.reshape(T, D)
    position = i * L + jnp.arange(L, dtype=jnp.int32)
    live = (position[None, :] < lengths.reshape(G)[:, None]).astype(F32).reshape(T, 1)

    ends, slice_end = ema_ends(x3, keep)
    xp, pre, finals = ema_forward(x3, keep, weight, omega, ends, carry_in(slice_end, decay, 1))
    xp = xp.reshape(T, D)
    u, h, r, v, z, p, mixed = mix_forward(R, x, xp, bm, bv, qk, rel_matrix, wm + wv + wo)
    output, h1, act, dg, df, dm, du, dt, sum_d, sum_f = ffn_both(
        R, x, u, h, cotangent.reshape(T, D), live, norms, bf, bo, wi + wf
    )
    g_ffn_out = reduce_grad(dot_rows(act, dg), 0)
    g_ffn_in = reduce_grad(dot_rows(h1, df), 1)
    g_out = reduce_grad(dot_rows(mixed, dm), 2)
    db, dv, dxp, dtok, sum_m, sum_v, sum_q, sum_s = mix_backward(R, dm, du, dt, r, v, z, p, qk, wm + wv + wo)
    g_mix = reduce_grad(dot_rows(xp, db), 0)
    g_value = reduce_grad(dot_rows(x, dv), 1)
    dpe, back_ends, slice_start = ema_back_ends(dxp.reshape(G, L, D), pre, keep)
    dx, s1, s3, g_omega = ema_backward(
        dpe, x3, keep, 1.0 / keep, weight, omega, finals, back_ends, carry_in(slice_start, decay, -1)
    )
    input_grad = (dtok + dx.reshape(T, D).astype(F32)).astype(BF16).reshape(tokens.shape)

    g_eta = rate * beta * s1
    g_beta = rate * eta * s1
    g_alpha = eta * beta * rate * (1.0 - rate) * (s1 - damp * rate * s3)
    g_delta = -eta * beta * rate * rate * damp * (1.0 - damp) * s3
    late = jnp.concatenate([g_alpha, g_delta, g_beta, g_eta, g_omega])
    late = sum_small(late.reshape(-1, n_wsh, D // n_wsh).transpose(1, 0, 2))
    widened = jnp.pad(sum_s, ((0, 0), (0, BLOCK - 1))).reshape(-1)
    diagonals = jnp.sum(jnp.pad(widened, (0, BLOCK)).reshape(BLOCK, 2 * BLOCK), axis=0)
    g_rel = jnp.roll(diagonals[::-1], BLOCK)
    early_parts = (
        sum_m[0], sum_v[0], sum_f[0], g_rel, sum_q[0], sum_q[1], sum_q[2],
        sum_d[0], sum_d[1], sum_d[2], sum_d[3], sum_d[4],
    )
    early = sum_small(jnp.concatenate([part.reshape(n_wsh, -1) for part in early_parts], axis=1))
    smalls, start = [], 0
    for part in early_parts:
        size = part.shape[0] // n_wsh
        smalls.append(early[start : start + size])
        start += size
    (
        g_mix_bias, g_value_bias, g_ffn_in_bias, g_rel, g_gain_q, g_gain_k, g_shift, gain_1, gain_2, shift_1, shift_2,
        g_ffn_out_bias,
    ) = smalls
    late = late.T
    return (
        output.reshape(tokens.shape), input_grad,
        late[:, 0:H], late[:, H : 2 * H], late[:, 2 * H : 3 * H], late[:, 3 * H : 4 * H], late[:, 4 * H],
        spread_grad(g_mix), g_mix_bias, spread_grad(g_value), g_value_bias,
        jnp.stack([g_gain_q, g_gain_k], axis=1), g_shift, g_rel, spread_grad(g_out),
        jnp.stack([gain_1, gain_2], axis=1), jnp.stack([shift_1, shift_2], axis=1),
        spread_grad(g_ffn_in), g_ffn_in_bias, spread_grad(g_ffn_out), g_ffn_out_bias,
    )


def solution(mesh):
    in_specs = (
        P(None, "wsh", "seq", None),
        P(None, "wsh", "seq", None),
        P(None, "wsh"),
        P("wsh", None),
        P("wsh", None),
        P("wsh", None),
        P("wsh", None),
        P("wsh"),
        P("wsh", None),
        P("wsh"),
        P("wsh", None),
        P("wsh"),
        P("wsh", None),
        P("wsh"),
        P("wsh"),
        P("wsh", None),
        P("wsh", None),
        P("wsh", None),
        P("wsh", None),
        P("wsh"),
        P("wsh", None),
        P("wsh"),
    )
    out_specs = (
        P(None, "wsh", "seq", None),
        P(None, "wsh", "seq", None),
        P("wsh", None),
        P("wsh", None),
        P("wsh", None),
        P("wsh", None),
        P("wsh"),
        P("wsh", None),
        P("wsh"),
        P("wsh", None),
        P("wsh"),
        P("wsh", None),
        P("wsh"),
        P("wsh"),
        P("wsh", None),
        P("wsh", None),
        P("wsh", None),
        P("wsh", None),
        P("wsh"),
        P("wsh", None),
        P("wsh"),
    )
    return jax.shard_map(body, mesh=mesh, in_specs=in_specs, out_specs=out_specs, check_vma=False)
```

```python
import functools

import jax
import jax.numpy as jnp
from jax import lax
from jax.experimental import pallas as pl
from jax.experimental.pallas import tpu as pltpu
from jax.sharding import PartitionSpec as P

BLOCK = 128
LANES = 128
CH = 8
PAD = 8
CHUNK = 768
STRIP = 32
EPSILON = 1e-05
VMEM_LIMIT = 62 * 1024 * 1024
F32 = jnp.float32
BF16 = jnp.bfloat16


def dot_rows(left_op, right_op):
    return jnp.einsum("ri,rj->ij", left_op, right_op, preferred_element_type=jnp.float32)


def skew_matrix(wrapped):
    lead = wrapped.shape[:-1]
    flat = jnp.tile(wrapped, (1,) * len(lead) + (BLOCK,))[..., : BLOCK * (2 * BLOCK - 1)]
    return flat.reshape(lead + (BLOCK, 2 * BLOCK - 1))[..., :BLOCK]


def power(v, n):
    k = 1
    while k < n:
        v = v * v
        k *= 2
    return v

def rows_of(scr, s, T):
    return scr[pl.ds(s, CH, stride=T+PAD), :]

def spread(scr, v, T):
    for k in range(CH):
        scr[k*(T+PAD):k*(T+PAD)+T, :] = v[k*T:(k+1)*T, :]

def collect(scr, T):
    return jnp.concatenate([scr[k*(T+PAD):k*(T+PAD)+T, :] for k in range(CH)], axis=0)

def ends_kernel(H, T, x_ref, q_ref, e_ref, s_ref, scr):
    spread(scr, x_ref[0].astype(F32), T)
    q = [jnp.broadcast_to(q_ref[h:h+1, :], (CH, LANES)) for h in range(H)]
    def step(s, st):
        xs = rows_of(scr, s, T)
        return tuple(q[h]*st[h] + xs for h in range(H))
    st = lax.fori_loop(0, T, step, tuple(jnp.zeros((CH,LANES),F32) for _ in range(H)), unroll=8)
    for h in range(H):
        e_ref[0, h*CH:(h+1)*CH, :] = st[h]
    qT = power(q_ref[...], T)
    c = jnp.zeros((H,LANES),F32)
    for k in range(CH):
        c = qT*c + e_ref[0, pl.ds(k,H,stride=CH), :]
    s_ref[0] = c

def fwd_kernel(H, T, x_ref, q_ref, w_ref, om_ref, e_ref, c_ref, *refs):
    xp_ref, p_ref, f_ref, scr, cs, ps = refs[-6:]
    spread(scr, x_ref[0].astype(F32), T)
    qT = power(q_ref[...], T)
    c = c_ref[0]
    for k in range(CH):
        cs[pl.ds(k,H,stride=CH), :] = c
        c = qT*c + e_ref[0, pl.ds(k,H,stride=CH), :]
    q = [jnp.broadcast_to(q_ref[h:h+1, :], (CH, LANES)) for h in range(H)]
    w = [jnp.broadcast_to(w_ref[h:h+1, :], (CH, LANES)) for h in range(H)]
    om = jnp.broadcast_to(om_ref[...], (CH,LANES))
    def step(s, st):
        xs = rows_of(scr, s, T)
        st = tuple(q[h]*st[h] + xs for h in range(H))
        terms = [w[h]*st[h] for h in range(H)]
        while len(terms) > 1:
            terms = [terms[i]+terms[i+1] for i in range(0,len(terms)-1,2)] + ([terms[-1]] if len(terms)%2 else [])
        ps[pl.ds(s, CH, stride=T+PAD), :] = terms[0] + om*xs
        return st
    st = lax.fori_loop(0, T, step, tuple(cs[h*CH:(h+1)*CH, :] for h in range(H)), unroll=8)
    for h in range(H):
        f_ref[0, h*CH:(h+1)*CH, :] = st[h]
    p = collect(ps, T)
    p_ref[0] = p
    xp_ref[0] = (p*jax.nn.sigmoid(p)).astype(xp_ref.dtype)

def bends_kernel(H, T, dxp_ref, p_ref, q_ref, d_ref, e_ref, s_ref, ds):
    p = p_ref[0]
    sg = jax.nn.sigmoid(p)
    d = dxp_ref[0].astype(F32) * (sg*(1.0+p*(1.0-sg)))
    d_ref[0] = d
    spread(ds, d, T)
    q = [jnp.broadcast_to(q_ref[h:h+1, :], (CH, LANES)) for h in range(H)]
    def step(s, st):
        xs = rows_of(ds, T-1-s, T)
        return tuple(q[h]*st[h] + xs for h in range(H))
    st = lax.fori_loop(0, T, step, tuple(jnp.zeros((CH,LANES),F32) for _ in range(H)), unroll=8)
    for h in range(H):
        e_ref[0, h*CH:(h+1)*CH, :] = st[h]
    qT = power(q_ref[...], T)
    c = jnp.zeros((H,LANES),F32)
    for k in reversed(range(CH)):
        c = qT*c + e_ref[0, pl.ds(k,H,stride=CH), :]
    s_ref[0] = c

def bwd_kernel(H, T, d_ref, x_ref, q_ref, qi_ref, w_ref, om_ref, f_ref, e_ref, c_ref, *refs):
    dx_ref, s1_ref, s3_ref, go_ref, scr, cs, dx, ds = refs[-8:]
    g = pl.program_id(1)
    x = x_ref[0].astype(F32)
    spread(scr, x, T)
    dv = d_ref[0]
    spread(ds, dv, T)
    qT = power(q_ref[...], T)
    c = c_ref[0]
    for k in reversed(range(CH)):
        cs[pl.ds(k,H,stride=CH), :] = c
        c = qT*c + e_ref[0, pl.ds(k,H,stride=CH), :]
    om = jnp.broadcast_to(om_ref[...], (CH,LANES))
    HH = H//2
    zero = jnp.zeros((CH,LANES),F32)
    @pl.when(g==0)
    def _():
        go_ref[...] = jnp.zeros_like(go_ref)
        s1_ref[...] = jnp.zeros_like(s1_ref)
        s3_ref[...] = jnp.zeros_like(s3_ref)
    go_ref[...] += jnp.sum(dv*x, axis=0, keepdims=True)
    for half in range(2):
        hs = range(half*HH, half*HH+HH)
        q = [jnp.broadcast_to(q_ref[h:h+1, :], (CH, LANES)) for h in hs]
        qi = [jnp.broadcast_to(qi_ref[h:h+1, :], (CH, LANES)) for h in hs]
        w = [jnp.broadcast_to(w_ref[h:h+1, :], (CH, LANES)) for h in hs]
        def step(s, carry):
            l, st, a1, a3 = carry
            at = pl.ds(T-1-s, CH, stride=T+PAD)
            d = ds[at, :]
            xs = scr[at, :]
            a1 = tuple(a1[i] + d*st[i] for i in range(HH))
            l = tuple(q[i]*l[i] + d for i in range(HH))
            st = tuple((st[i]-xs)*qi[i] for i in range(HH))
            a3 = tuple(a3[i] + l[i]*st[i] for i in range(HH))
            terms = [w[i]*l[i] for i in range(HH)]
            while len(terms) > 1:
                terms = [terms[i]+terms[i+1] for i in range(0,len(terms)-1,2)]
            if half == 0:
                dx[at, :] = terms[0] + om*d
            else:
                dx[at, :] = dx[at, :] + terms[0]
            return l, st, a1, a3
        init = (tuple(cs[h*CH:(h+1)*CH,:] for h in hs), tuple(f_ref[0,h*CH:(h+1)*CH,:] for h in hs), (zero,)*HH, (zero,)*HH)
        l, st, a1, a3 = lax.fori_loop(0, T, step, init, unroll=4)
        for i,h in enumerate(hs):
            s1_ref[h:h+1,:] += jnp.sum(a1[i],axis=0,keepdims=True)
            s3_ref[h:h+1,:] += jnp.sum(a3[i],axis=0,keepdims=True)
    dx_ref[0] = collect(dx, T).astype(dx_ref.dtype)

def specs(L, H, first=0):
    blk = pl.BlockSpec((1, L, LANES), lambda c, g: (g, 0, c + first))
    par = pl.BlockSpec((H, LANES), lambda c, g: (0, c + first))
    one = pl.BlockSpec((1, LANES), lambda c, g: (0, c + first))
    st = pl.BlockSpec((1, H * CH, LANES), lambda c, g: (g, 0, c + first))
    car = pl.BlockSpec((1, H, LANES), lambda c, g: (g, 0, c + first))
    return blk, par, one, st, car


def ema_ends(x, q):
    G, L, C = x.shape
    H = q.shape[0]
    blk, par, one, st, car = specs(L, H)
    return pl.pallas_call(
        functools.partial(ends_kernel, H, L // CH),
        grid=(C // LANES, G),
        in_specs=[blk, par],
        out_specs=[st, car],
        out_shape=[jax.ShapeDtypeStruct((G, H * CH, C), F32), jax.ShapeDtypeStruct((G, H, C), F32)],
        scratch_shapes=[pltpu.VMEM((L + CH * PAD, LANES), F32)],
        cost_estimate=cost_of(0, 11),
        name="ema_ends",
    )(x, q)


def ema_forward(span, so_far, x, q, w, om, e, c):
    G, L, C = x.shape
    H = q.shape[0]
    first, count = span
    blk, par, one, st, car = specs(L, H, first)
    return pl.pallas_call(
        functools.partial(fwd_kernel, H, L // CH),
        grid=(count, G),
        in_specs=[blk, par, par, one, st, car] + [pl.BlockSpec(memory_space=pl.ANY)] * len(so_far),
        out_specs=[blk, blk, st],
        out_shape=[
            jax.ShapeDtypeStruct((G, L, C), BF16), jax.ShapeDtypeStruct((G, L, C), F32),
            jax.ShapeDtypeStruct((G, H * CH, C), F32),
        ],
        scratch_shapes=[
            pltpu.VMEM((L + CH * PAD, LANES), F32), pltpu.VMEM((H * CH, LANES), F32),
            pltpu.VMEM((L + CH * PAD, LANES), F32),
        ],
        input_output_aliases={6 + k: k for k in range(len(so_far))},
        cost_estimate=cost_of(0, 3 * count),
        name="ema_forward",
    )(x, q, w, om, e, c, *so_far)


def ema_back_ends(dxp, p, q):
    G, L, C = p.shape
    H = q.shape[0]
    blk, par, one, st, car = specs(L, H)
    return pl.pallas_call(
        functools.partial(bends_kernel, H, L // CH),
        grid=(C // LANES, G),
        in_specs=[blk, blk, par],
        out_specs=[blk, st, car],
        out_shape=[
            jax.ShapeDtypeStruct((G, L, C), F32), jax.ShapeDtypeStruct((G, H * CH, C), F32),
            jax.ShapeDtypeStruct((G, H, C), F32),
        ],
        scratch_shapes=[pltpu.VMEM((L + CH * PAD, LANES), F32)],
        cost_estimate=cost_of(0, 15),
        name="ema_back_ends",
    )(dxp, p, q)


def ema_backward(span, so_far, d, x, q, qi, w, om, f, e, c):
    G, L, C = x.shape
    H = q.shape[0]
    first, count = span
    blk, par, one, st, car = specs(L, H, first)
    return pl.pallas_call(
        functools.partial(bwd_kernel, H, L // CH),
        grid=(count, G),
        in_specs=[blk, blk, par, par, par, one, st, st, car]
        + [pl.BlockSpec(memory_space=pl.ANY)] * len(so_far),
        out_specs=[blk, par, par, one],
        out_shape=[
            jax.ShapeDtypeStruct((G, L, C), BF16), jax.ShapeDtypeStruct((H, C), F32),
            jax.ShapeDtypeStruct((H, C), F32), jax.ShapeDtypeStruct((1, C), F32),
        ],
        scratch_shapes=[
            pltpu.VMEM((L + CH * PAD, LANES), F32), pltpu.VMEM((H * CH, LANES), F32),
            pltpu.VMEM((L + CH * PAD, LANES), F32), pltpu.VMEM((L + CH * PAD, LANES), F32),
        ],
        input_output_aliases={9 + k: k for k in range(len(so_far))},
        cost_estimate=cost_of(0, 8 * count),
        name="ema_backward",
    )(d, x, q, qi, w, om, f, e, c, *so_far)


def sig(v):
    return 0.5 * jnp.tanh(0.5 * v) + 0.5


def dot_nn(left_op, right_op):
    return jnp.dot(left_op, right_op, preferred_element_type=F32)


def dot_nt(left_op, right_op):
    return lax.dot_general(left_op, right_op, (((1,), (1,)), ((), ())), preferred_element_type=F32)


def dot_tn(left_op, right_op):
    return lax.dot_general(left_op, right_op, (((0,), (0,)), ((), ())), preferred_element_type=F32)


def piece_copies(pieces, target, sem, first):
    own, core, across, across_y, across_core, across_y_core = pieces
    rows = own.shape[0]
    half = across.shape[0]
    j = lax.axis_index("wsh")
    i = lax.axis_index("seq")
    bit = lax.rem(i, 2)
    spots = (
        (own, j * rows),
        (core, (j ^ 1) * rows),
        (across, (j ^ 2) * rows + bit * half),
        (across_y, (j ^ 2) * rows + (1 - bit) * half),
        (across_core, (j ^ 3) * rows + bit * half),
        (across_y_core, (j ^ 3) * rows + (1 - bit) * half),
    )
    copies = []
    for n, (piece, start) in enumerate(spots):
        rows_at = pl.ds(pl.multiple_of(start, 32), piece.shape[0])
        copies.append(pltpu.make_async_copy(piece, target.at[rows_at, :], sem.at[first + n]))
    return copies


def bring(pieces, targets, sem):
    @pl.when(pl.program_id(0) == 0)
    def _():
        copies = []
        for n, target in enumerate(targets):
            copies.extend(piece_copies(pieces[6 * n : 6 * n + 6], target, sem, 6 * n))
        for copy in copies:
            copy.start()
        for copy in copies:
            copy.wait()


def fold(rows):
    total = rows[:8]
    for k in range(8, STRIP, 8):
        total = total + rows[k : k + 8]
    return total


def add_sums(ref, at, rows):
    ref[:, at] += jnp.sum(rows, axis=0, keepdims=True)


def mix_fwd_kernel(R, dims, x_ref, xp_ref, bm_ref, bv_ref, qk_ref, rel_ref, *refs):
    D, Z, V = dims
    pieces, refs = refs[:18], refs[18:]
    u_ref, h_ref, r_ref, v_ref, z_ref, p_ref, m_ref, wm, wv, wo, sem = refs
    bring(pieces, (wm, wv, wo), sem)
    xp = xp_ref[...]
    x = x_ref[...]
    z = dot_nn(xp, wm[:, D : D + Z]) + bm_ref[:, D : D + Z]
    z_ref[...] = z
    shared = z * sig(z)
    query = (shared * qk_ref[0:1, :] + qk_ref[2:3, :]).astype(BF16)
    key = (shared * qk_ref[1:2, :]).astype(BF16)
    probs = []
    row = lax.broadcasted_iota(jnp.int32, (BLOCK, BLOCK), 0)
    col = lax.broadcasted_iota(jnp.int32, (BLOCK, BLOCK), 1)
    for b in range(R // BLOCK):
        at = slice(b * BLOCK, (b + 1) * BLOCK)
        score = dot_nt(query[at], key[at]) * Z ** (-0.5) + rel_ref[...]
        score = jnp.where(row >= col, score, -1e30)
        grown = jnp.exp(score - jnp.max(score, axis=-1, keepdims=True))
        prob = grown / jnp.sum(grown, axis=-1, keepdims=True)
        p_ref[at, :] = prob
        probs.append(prob.astype(BF16))
    for c in range(0, V, CHUNK):
        at = slice(c, c + CHUNK)
        rat = slice(D + Z + c, D + Z + c + CHUNK)
        v = dot_nn(x, wv[:, at]) + bv_ref[:, at]
        v_ref[:, at] = v
        value = (v * sig(v)).astype(BF16)
        r = dot_nn(xp, wm[:, rat]) + bm_ref[:, rat]
        r_ref[:, at] = r
        reset = r * sig(r)
        for b in range(R // BLOCK):
            rows = slice(b * BLOCK, (b + 1) * BLOCK)
            m_ref[rows, at] = (reset[rows] * dot_nn(probs[b], value[rows])).astype(BF16)
    u_ref[...] = dot_nn(xp, wm[:, :D]) + bm_ref[:, :D]
    h_ref[...] = dot_nn(xp, wm[:, D + Z + V :]) + bm_ref[:, D + Z + V :] + dot_nn(m_ref[...], wo[...])


def slope_of(pre, logistic):
    return logistic * (1.0 + pre * (1.0 - logistic))


def mean_of(rows):
    return jnp.mean(rows, axis=-1, keepdims=True)


def ffn_kernel(R, dims, x_ref, u_ref, h_ref, cot_ref, live_ref, gn_ref, bf_ref, bo_ref, *refs):
    D, FF = dims
    pieces, refs = refs[:12], refs[12:]
    (
        o_ref, h1_ref, act_ref, dg_ref, df_ref, dum_ref, dt_ref, sd_ref, sf_ref,
        wi, wo, f_scr, n1_scr, a_scr, i1_scr, sem,
    ) = refs
    bring(pieces, (wi, wo), sem)

    @pl.when(pl.program_id(0) == 0)
    def _():
        sd_ref[...] = jnp.zeros_like(sd_ref)
        sf_ref[...] = jnp.zeros_like(sf_ref)

    g1, g2, b1, b2 = (gn_ref[k : k + 1, :] for k in range(4))
    part = min(256, R)

    def strips(s):
        return [slice(k, k + STRIP) for k in range(s * part, (s + 1) * part, STRIP)]

    def first(s):
        for at in strips(s):
            x = x_ref[at, :].astype(F32)
            h = h_ref[at, :]
            y = x + sig(u_ref[at, :]) * (h * sig(h) - x)
            center = y - mean_of(y)
            inverse = lax.rsqrt(mean_of(center * center) + EPSILON)
            n1 = center * inverse
            n1_scr[at, :] = n1
            i1_scr[at, :] = jnp.broadcast_to(inverse, (STRIP, LANES))
            h1_ref[at, :] = (n1 * g1 + b1).astype(BF16)

    def spread(s):
        rows = slice(s * part, (s + 1) * part)
        for c in range(0, FF, CHUNK):
            at = slice(c, c + CHUNK)
            f = dot_nn(h1_ref[rows, :], wi[:, at]) + bf_ref[:, at]
            f_scr[rows, at] = f
            act_ref[rows, at] = (f * sig(f)).astype(BF16)

    def narrow(s):
        rows = slice(s * part, (s + 1) * part)
        a_scr[rows, :] = dot_nn(act_ref[rows, :], wo[...])

    def second(s):
        zero = jnp.zeros((8, D), F32)
        s_gain, s_shift, s_bias = zero, zero, zero
        for at in strips(s):
            y2 = n1_scr[at, :] * g1 + b1 + a_scr[at, :] + bo_ref[...]
            center = y2 - mean_of(y2)
            inverse = lax.rsqrt(mean_of(center * center) + EPSILON)
            n2 = center * inverse
            live = live_ref[at, :]
            o_ref[at, :] = ((n2 * g2 + b2) * live).astype(BF16)
            dn = cot_ref[at, :].astype(F32) * live
            w = dn * g2
            dy2 = inverse * (w - mean_of(w) - n2 * mean_of(w * n2))
            a_scr[at, :] = dy2
            dg_ref[at, :] = dy2.astype(BF16)
            s_gain, s_shift, s_bias = s_gain + fold(dn * n2), s_shift + fold(dn), s_bias + fold(dy2)
        sd_ref[1:2, :] += jnp.sum(s_gain, axis=0, keepdims=True)
        sd_ref[3:4, :] += jnp.sum(s_shift, axis=0, keepdims=True)
        sd_ref[4:5, :] += jnp.sum(s_bias, axis=0, keepdims=True)

    def spread_back(s):
        rows = slice(s * part, (s + 1) * part)
        for c in range(0, FF, CHUNK):
            at = slice(c, c + CHUNK)
            f = f_scr[rows, at]
            df = (dot_nt(dg_ref[rows, :], wo[at, :]) * slope_of(f, sig(f))).astype(BF16)
            df_ref[rows, at] = df
            add_sums(sf_ref, at, df.astype(F32))

    def narrow_back(s):
        rows = slice(s * part, (s + 1) * part)
        a_scr[rows, :] += dot_nt(df_ref[rows, :], wi[...])

    def third(s):
        zero = jnp.zeros((8, D), F32)
        s_gain, s_shift = zero, zero
        for at in strips(s):
            dh1 = a_scr[at, :]
            n1 = n1_scr[at, :]
            w = dh1 * g1
            dy = i1_scr[at, 0:1] * (w - mean_of(w) - n1 * mean_of(w * n1))
            x = x_ref[at, :].astype(F32)
            h = h_ref[at, :]
            sh = sig(h)
            gate = sig(u_ref[at, :])
            rest = 1.0 - gate
            dyg = dy * gate
            dum_ref[at, :D] = (dyg * (h * sh - x) * rest).astype(BF16)
            dum_ref[at, D:] = (dyg * slope_of(h, sh)).astype(BF16)
            dt_ref[at, :] = dy * rest
            s_gain, s_shift = s_gain + fold(dh1 * n1), s_shift + fold(dh1)
        sd_ref[0:1, :] += jnp.sum(s_gain, axis=0, keepdims=True)
        sd_ref[2:3, :] += jnp.sum(s_shift, axis=0, keepdims=True)

    stages = (first, spread, narrow, second, spread_back, narrow_back, third)
    count = R // part
    for tick in range(len(stages) + count - 1):
        for s in range(count):
            if 0 <= tick - s < len(stages):
                stages[tick - s](s)


def mix_bwd_kernel(R, dims, dum_ref, dt_ref, r_ref, v_ref, z_ref, p_ref, qk_ref, *refs):
    D, Z, V = dims
    pieces, refs = refs[:18], refs[18:]
    db_ref, dv_ref, dxp_ref, do_ref, sm_ref, sv_ref, sq_ref, ss_ref, wm, wv, wo, acc, sem = refs
    bring(pieces, (wm, wv, wo), sem)

    @pl.when(pl.program_id(0) == 0)
    def _():
        for ref in (sm_ref, sv_ref, sq_ref, ss_ref):
            ref[...] = jnp.zeros_like(ref)

    last = D + Z + V
    blocks = [slice(b * BLOCK, (b + 1) * BLOCK) for b in range(R // BLOCK)]
    full = [p_ref[rows, :] for rows in blocks]
    probs = [prob.astype(BF16) for prob in full]
    dprob = [jnp.zeros((BLOCK, BLOCK), F32) for _ in blocks]
    size = 512

    def chunk(c):
        at = slice(c, c + size)
        rat = slice(D + Z + c, D + Z + c + size)
        zat = slice(Z + c, Z + c + size)
        dmix = dot_nt(dum_ref[:, D:], wo[at, :])
        sum_r = jnp.zeros((1, size), F32)
        sum_v = jnp.zeros((1, size), F32)
        for b, rows in enumerate(blocks):
            r = r_ref[rows, at]
            v = v_ref[rows, at]
            sr = sig(r)
            sv = sig(v)
            value = (v * sv).astype(BF16)
            datt = (dmix[rows] * (r * sr)).astype(BF16)
            dr = (dmix[rows] * slope_of(r, sr) * dot_nn(probs[b], value)).astype(BF16)
            db_ref[rows, zat] = dr
            sum_r += jnp.sum(dr.astype(F32), axis=0, keepdims=True)
            dprob[b] += dot_nt(datt, value)
            dv = (dot_tn(probs[b], datt) * slope_of(v, sv)).astype(BF16)
            dv_ref[rows, at] = dv
            sum_v += jnp.sum(dv.astype(F32), axis=0, keepdims=True)
        sm_ref[:, rat] += sum_r
        sv_ref[:, at] += sum_v

    def give(c):
        at = slice(c, c + size)
        rat = slice(D + Z + c, D + Z + c + size)
        zat = slice(Z + c, Z + c + size)
        acc[...] += dot_nt(db_ref[:, zat], wm[:, rat])
        do_ref[...] += dot_nt(dv_ref[:, at], wv[:, at])

    starts = list(range(0, V, size))
    chunk(starts[0])
    acc[...] = dot_nt(dum_ref[:, :D], wm[:, :D]) + dot_nt(dum_ref[:, D:], wm[:, last:])
    do_ref[...] = dt_ref[...]
    for n, c in enumerate(starts[1:]):
        chunk(c)
        give(starts[n])
    add_sums(sm_ref, slice(0, D), dum_ref[:, :D].astype(F32))
    add_sums(sm_ref, slice(last, D + last), dum_ref[:, D:].astype(F32))
    for b, rows in enumerate(blocks):
        z = z_ref[rows, :]
        sz = sig(z)
        shared = z * sz
        query = (shared * qk_ref[0:1, :] + qk_ref[2:3, :]).astype(BF16)
        key = (shared * qk_ref[1:2, :]).astype(BF16)
        inner = jnp.sum(full[b] * dprob[b], axis=-1, keepdims=True)
        ds = (full[b] * (dprob[b] - inner)).astype(BF16)
        ss_ref[...] += ds.astype(F32)
        dq = dot_nn(ds, key) * Z ** (-0.5)
        dk = dot_tn(ds, query) * Z ** (-0.5)
        sq_ref[0:1, :] += jnp.sum(dq * shared, axis=0, keepdims=True)
        sq_ref[1:2, :] += jnp.sum(dk * shared, axis=0, keepdims=True)
        sq_ref[2:3, :] += jnp.sum(dq, axis=0, keepdims=True)
        dz = (dq * qk_ref[0:1, :] + dk * qk_ref[1:2, :]) * slope_of(z, sz)
        dz = dz.astype(BF16)
        db_ref[rows, :Z] = dz
        add_sums(sm_ref, slice(D, D + Z), dz.astype(F32))
    give(starts[-1])
    dxp_ref[...] = (acc[...] + dot_nt(db_ref[:, :Z], wm[:, D : D + Z])).astype(BF16)


def cost_of(flops, microseconds):
    return pl.CostEstimate(flops=flops, bytes_accessed=microseconds * 3_600_000, transcendentals=0)


def any_specs(n):
    return [pl.BlockSpec(memory_space=pl.ANY)] * n


def tile(R, n):
    return pl.BlockSpec((R, n), lambda t: (t, 0))


def fixed(r, n):
    return pl.BlockSpec((r, n), lambda t: (0, 0))


def shape(r, n, dtype=F32):
    return jax.ShapeDtypeStruct((r, n), dtype)


def mix_forward(R, x, xp, bm, bv, qk, rel, pieces):
    T, D = x.shape
    V = bv.shape[1]
    Z = qk.shape[1]
    E = bm.shape[1]
    return pl.pallas_call(
        functools.partial(mix_fwd_kernel, R, (D, Z, V)),
        grid=(T // R,),
        in_specs=[tile(R, D), tile(R, D), fixed(1, E), fixed(1, V), fixed(8, Z), fixed(BLOCK, BLOCK)]
        + any_specs(18),
        out_specs=[tile(R, D), tile(R, D), tile(R, V), tile(R, V), tile(R, Z), tile(R, BLOCK), tile(R, V)],
        out_shape=[
            shape(T, D), shape(T, D), shape(T, V), shape(T, V), shape(T, Z), shape(T, BLOCK), shape(T, V, BF16),
        ],
        scratch_shapes=[
            pltpu.VMEM((D, E), BF16), pltpu.VMEM((D, V), BF16), pltpu.VMEM((V, D), BF16),
            pltpu.SemaphoreType.DMA((18,)),
        ],
        compiler_params=pltpu.CompilerParams(vmem_limit_bytes=VMEM_LIMIT),
        cost_estimate=cost_of(2 * T * D * (E + 2 * V), 33),
        name="mix_forward",
    )(x, xp, bm, bv, qk, rel, *pieces)


def ffn_both(R, x, u, h, cot, live, norms, bf, bo, pieces):
    T, D = x.shape
    FF = bf.shape[1]
    return pl.pallas_call(
        functools.partial(ffn_kernel, R, (D, FF)),
        grid=(T // R,),
        in_specs=[tile(R, D), tile(R, D), tile(R, D), tile(R, D), tile(R, 1), fixed(8, D), fixed(1, FF), fixed(1, D)]
        + any_specs(12),
        out_specs=[
            tile(R, D), tile(R, D), tile(R, FF), tile(R, D), tile(R, FF), tile(R, 2 * D), tile(R, D),
            fixed(8, D), fixed(1, FF),
        ],
        out_shape=[
            shape(T, D, BF16), shape(T, D, BF16), shape(T, FF, BF16), shape(T, D, BF16), shape(T, FF, BF16),
            shape(T, 2 * D, BF16), shape(T, D), shape(8, D), shape(1, FF),
        ],
        scratch_shapes=[
            pltpu.VMEM((D, FF), BF16), pltpu.VMEM((FF, D), BF16), pltpu.VMEM((R, FF), F32), pltpu.VMEM((R, D), F32),
            pltpu.VMEM((R, D), F32), pltpu.VMEM((R, 128), F32), pltpu.SemaphoreType.DMA((12,)),
        ],
        compiler_params=pltpu.CompilerParams(vmem_limit_bytes=VMEM_LIMIT),
        cost_estimate=cost_of(2 * T * D * 4 * FF, 50),
        name="ffn_both",
    )(x, u, h, cot, live, norms, bf, bo, *pieces)


def mix_backward(R, dum, dt, r, v, z, p, qk, pieces):
    T, D = dt.shape
    V = r.shape[1]
    Z = qk.shape[1]
    E = 2 * D + Z + V
    return pl.pallas_call(
        functools.partial(mix_bwd_kernel, R, (D, Z, V)),
        grid=(T // R,),
        in_specs=[
            tile(R, 2 * D), tile(R, D), tile(R, V), tile(R, V), tile(R, Z), tile(R, BLOCK), fixed(8, Z),
        ]
        + any_specs(18),
        out_specs=[
            tile(R, Z + V), tile(R, V), tile(R, D), tile(R, D), fixed(1, E), fixed(1, V), fixed(8, Z), fixed(BLOCK, BLOCK),
        ],
        out_shape=[
            shape(T, Z + V, BF16), shape(T, V, BF16), shape(T, D, BF16), shape(T, D), shape(1, E), shape(1, V),
            shape(8, Z), shape(BLOCK, BLOCK),
        ],
        scratch_shapes=[
            pltpu.VMEM((D, E), BF16), pltpu.VMEM((D, V), BF16), pltpu.VMEM((V, D), BF16), pltpu.VMEM((R, D), F32),
            pltpu.SemaphoreType.DMA((18,)),
        ],
        compiler_params=pltpu.CompilerParams(vmem_limit_bytes=VMEM_LIMIT),
        cost_estimate=cost_of(2 * T * D * (E + 2 * V), 40),
        name="mix_backward",
    )(dum, dt, r, v, z, p, qk, *pieces)


def exchange(value, axis, step):
    return lax.ppermute(value, axis, [(k, k ^ step) for k in range(lax.axis_size(axis))])


def shift(value, axis, step):
    n = lax.axis_size(axis)
    return lax.ppermute(value, axis, [(k, k + step) for k in range(n) if 0 <= k + step < n])


def join(*values):
    return lax.optimization_barrier(values)


def own_half(own):
    half = own.shape[0] // 2
    return lax.dynamic_slice_in_dim(own, lax.rem(lax.axis_index("seq"), 2) * half, half, 0)


def over_x(value):
    return exchange(value, "wsh", 2)


def over_y(value):
    return exchange(value, "seq", 1)


def over_core(value):
    return exchange(value, "wsh", 1)


def gather_small(own):
    j = lax.axis_index("wsh")
    four = jnp.stack([own] + [exchange(own, "wsh", d) for d in range(1, 4)])
    return jnp.stack([lax.dynamic_index_in_dim(four, j ^ k, 0, False) for k in range(4)])


def carry_in(states, decay, sign):
    n = lax.axis_size("seq")
    total = shift(states, "seq", sign)
    factor = decay
    for k in range(2, 5):
        if k < n:
            total = total + factor * shift(states, "seq", sign * k)
        factor = factor * decay
    window, factor = 4, factor
    while window < n:
        grown, scale = total, factor
        for k in range(1, 4):
            if k * window < n:
                grown = grown + scale * shift(total, "seq", sign * k * window)
            scale = scale * factor
        total, factor, window = grown, scale, window * 4
    return total


def pick(value, dim, bit):
    return lax.dynamic_index_in_dim(value, bit, dim, False)


def send_half(value, dim, mark):
    axis, step = mark
    bit = lax.rem(lax.axis_index(axis) // step, 2)
    return exchange(pick(value, dim, 1 - bit).astype(BF16), axis, step), pick(value, dim, bit)


def add_half(sent, kept):
    return kept + sent.astype(F32)


def seq_steps():
    return [2**k for k in range(lax.axis_size("seq").bit_length() - 1)]


def send_core(grad):
    rows, cols = grad.shape
    bits = (2,) * len(seq_steps())
    rest = rows // lax.axis_size("wsh") // lax.axis_size("seq")
    return send_half(grad.reshape((2, 2) + bits + (rest, cols)), 1, ("wsh", 1))


def merge(parts, cols):
    pieces = []
    for part in parts:
        for c in range(0, part.shape[-1], cols):
            pieces.append(part[..., c : c + cols])
    return jnp.concatenate(pieces, axis=-2)


class Sum:
    def __init__(self, value):
        self.value = value
        self.marks = [("wsh", 2)] + [("seq", s) for s in reversed(seq_steps())]

    def send(self, mark):
        dim = self.marks.index(mark)
        self.marks.pop(dim)
        sent, self.kept = send_half(self.value, dim, mark)
        return sent

    def add(self, sent):
        self.value = add_half(sent, self.kept)


def widen(block, other, step):
    bit = lax.rem(lax.axis_index("seq") // step, 2)
    first = jnp.where(bit == 0, block, other)
    second = jnp.where(bit == 0, other, block)
    return jnp.concatenate([first, second], axis=0)


def in_order(block):
    bits = block.shape[0].bit_length() - 1
    split = block.reshape((2,) * bits + block.shape[1:])
    turned = split.transpose(tuple(reversed(range(bits))) + (bits, bits + 1))
    return turned.reshape(block.shape)


def sum_small(value):
    j = lax.axis_index("wsh")
    total = lax.dynamic_index_in_dim(value, j, 0, False)
    for d in range(1, 4):
        total = total + exchange(lax.dynamic_index_in_dim(value, j ^ d, 0, False), "wsh", d)
    step = 1
    while step < lax.axis_size("seq"):
        total = total + exchange(total, "seq", step)
        step *= 2
    return total


def body(
    tokens, cotangent, lengths, ema_alpha, ema_delta, ema_beta, ema_eta, ema_omega, mix_weight, mix_bias,
    value_weight, value_bias, qk_gain, qk_bias, rel_bias, out_weight, norm_gain, norm_bias, ffn_in, ffn_in_bias,
    ffn_out, ffn_out_bias,
):
    micro, seqs, L, D = tokens.shape
    G = micro * seqs
    T = G * L
    H = ema_alpha.shape[1]
    R = min(512, T)
    n_wsh = lax.axis_size("wsh")
    i = lax.axis_index("seq")
    Z = qk_gain.shape[0] * n_wsh
    V = value_weight.shape[1]
    FF = ffn_in.shape[1]

    chan = gather_small(
        jnp.concatenate(
            [ema_alpha, ema_delta, ema_beta, ema_eta, ema_omega[:, None], norm_gain, norm_bias, ffn_out_bias[:, None]],
            axis=1,
        )
    )
    chan = chan.reshape(D, -1).T.astype(F32)
    flat_parts = (mix_bias, value_bias, ffn_in_bias, rel_bias, qk_gain[:, 0], qk_gain[:, 1], qk_bias)
    flat = gather_small(jnp.concatenate(flat_parts)).astype(F32)
    vectors, start = [], 0
    for part in flat_parts:
        vectors.append(flat[:, start : start + part.shape[0]].reshape(1, -1))
        start += part.shape[0]
    bm, bv, bf, rel, gain_q, gain_k, shift_q = vectors
    rate = jax.nn.sigmoid(chan[0:H])
    damp = jax.nn.sigmoid(chan[H : 2 * H])
    beta = chan[2 * H : 3 * H]
    eta = chan[3 * H : 4 * H]
    omega = chan[4 * H : 4 * H + 1]
    norms = jnp.concatenate([chan[4 * H + 1 : 4 * H + 5], jnp.zeros((4, D), F32)])
    bo = chan[4 * H + 5 : 4 * H + 6]
    qk = jnp.concatenate([gain_q, gain_k, shift_q, jnp.zeros((5, Z), F32)])
    rel_matrix = skew_matrix(jnp.roll(rel[0, ::-1], BLOCK))
    keep = 1.0 - rate * damp
    weight = eta * beta * rate
    decay = power(keep, L)
    x3 = tokens.reshape(G, L, D)
    x = tokens.reshape(T, D)
    position = i * L + jnp.arange(L, dtype=jnp.int32)
    live = (position[None, :] < lengths.reshape(G)[:, None]).astype(F32).reshape(T, 1)

    y_step, z_steps = ("seq", 1), [("seq", s) for s in seq_steps()[1:]]
    x_step = ("wsh", 2)
    third = D // LANES // 3
    half = D // LANES // 2

    keep, *owns = join(keep, mix_weight, value_weight, out_weight, ffn_in, ffn_out)
    o_mix, o_value, o_out, o_in, o_fout = owns
    x_mix, x_value, x_out = over_x(own_half(o_mix)), over_x(own_half(o_value)), over_x(own_half(o_out))
    c_mix, c_value, c_out = over_core(o_mix), over_core(o_value), over_core(o_out)
    ends, slice_end = ema_ends(x3, keep)
    ends, slice_end, x_mix, c_mix = join(ends, slice_end, x_mix, c_mix)
    y_mix = over_y(x_mix)
    state_in = carry_in(slice_end, decay, 1)
    state_in, x_value, x_out, c_value, c_out = join(state_in, x_value, x_out, c_value, c_out)
    y_value, y_out = over_y(x_value), over_y(x_out)
    xc_mix = over_core(x_mix)
    x_in, x_fout = over_x(own_half(o_in)), over_x(own_half(o_fout))
    so_far = ema_forward((0, half), (), x3, keep, weight, omega, ends, state_in)
    *so_far, y_mix, xc_mix = join(*so_far, y_mix, xc_mix)
    yc_mix, xc_value, xc_out = over_core(y_mix), over_core(x_value), over_core(x_out)
    c_in, c_fout = over_core(o_in), over_core(o_fout)
    xp, pre, finals = ema_forward((half, half), tuple(so_far), x3, keep, weight, omega, ends, state_in)
    xp, x_in, x_fout, c_in, c_fout, y_value, y_out, yc_mix, xc_value, xc_out = join(
        xp, x_in, x_fout, c_in, c_fout, y_value, y_out, yc_mix, xc_value, xc_out
    )
    yc_value, yc_out = over_core(y_value), over_core(y_out)
    y_in, y_fout, xc_in, xc_fout = over_y(x_in), over_y(x_fout), over_core(x_in), over_core(x_fout)
    mix_pieces = (
        (o_mix, c_mix, x_mix, y_mix, xc_mix, yc_mix) + (o_value, c_value, x_value, y_value, xc_value, yc_value)
        + (o_out, c_out, x_out, y_out, xc_out, yc_out)
    )
    xp = xp.reshape(T, D)
    forward = mix_forward(R, x, xp, bm, bv, qk, rel_matrix, mix_pieces)
    (u, h, r, v, z, p, mixed), y_in, y_fout, xc_in, xc_fout = join(forward, y_in, y_fout, xc_in, xc_fout)
    ffn_pieces = (o_in, c_in, x_in, y_in, xc_in, over_core(y_in)) + (
        o_fout, c_fout, x_fout, y_fout, xc_fout, over_core(y_fout)
    )
    output, h1, act, dg, df, dum, dt, sum_d, sum_f = ffn_both(
        R, x, u, h, cotangent.reshape(T, D), live, norms, bf, bo, ffn_pieces
    )

    (sent_1, kept_1), (sent_2, kept_2) = send_core(dot_rows(act, dg)), send_core(dot_rows(h1, df))
    d_out, d_edge = dot_rows(mixed, dum[:, D:]), dot_rows(xp, dum)
    d_out, d_edge, sent_1, sent_2 = join(d_out, d_edge, sent_1, sent_2)
    sum_a = Sum(merge([add_half(sent_1, kept_1), add_half(sent_2, kept_2)], D))
    over_a = sum_a.send(x_step)
    (sent_1, kept_1), (sent_2, kept_2) = send_core(d_out), send_core(d_edge)
    sum_b = Sum(merge([add_half(sent_1, kept_1), add_half(sent_2, kept_2)], D))
    over_b = sum_b.send(y_step)
    back = mix_backward(R, dum, dt, r, v, z, p, qk, mix_pieces)
    (db, dv, dxp, dtok, sum_m, sum_v, sum_q, sum_s), over_a, over_b = join(back, over_a, over_b)
    sum_a.add(over_a)
    sum_b.add(over_b)
    over_a, over_b = sum_a.send(y_step), sum_b.send(x_step)
    d_side, over_a, over_b = join(dot_rows(xp, db), over_a, over_b)
    sum_a.add(over_a)
    sum_b.add(over_b)
    rows_a = sum_a.value.shape[-2]
    sum_a.value = jnp.concatenate([sum_a.value, sum_b.value], axis=-2)
    over_a = sum_a.send(z_steps[0])
    sent_1, kept_1 = send_core(d_side)
    d_value, over_a, sent_1 = join(dot_rows(x, dv), over_a, sent_1)
    sum_c = Sum(add_half(sent_1, kept_1))
    sum_a.add(over_a)
    over_a = sum_a.send(z_steps[1])
    sent_2, kept_2 = send_core(d_value)
    dpe, back_ends, slice_start = ema_back_ends(dxp.reshape(G, L, D), pre, keep)
    dpe, back_ends, slice_start, over_a, sent_2 = join(dpe, back_ends, slice_start, over_a, sent_2)
    sum_a.add(over_a)
    sum_d_ = Sum(add_half(sent_2, kept_2))
    back_in = carry_in(slice_start, decay, -1)
    over_c, over_d = sum_c.send(x_step), sum_d_.send(y_step)
    for mark in z_steps[2:]:
        sum_a.add(sum_a.send(mark))
    block = sum_a.value.astype(BF16)[None]
    consts = (dpe, x3, keep, 1.0 / keep, weight, omega, finals, back_ends, back_in)
    order = list(reversed(seq_steps()))
    more = exchange(block, "seq", order[0])
    so_far = ema_backward((0, third), (), *consts)
    *so_far, over_c, over_d, more = join(*so_far, over_c, over_d, more)
    sum_c.add(over_c)
    sum_d_.add(over_d)
    over_c, over_d = sum_c.send(y_step), sum_d_.send(x_step)
    block = widen(block, more, order[0])
    more = exchange(block, "seq", order[1])
    so_far = ema_backward((third, third), tuple(so_far), *consts)
    *so_far, over_c, over_d, more = join(*so_far, over_c, over_d, more)
    sum_c.add(over_c)
    sum_d_.add(over_d)
    cols_c = sum_c.value.shape[-1]
    sum_c.value = jnp.concatenate([sum_c.value, sum_d_.value], axis=-1)
    over_c = sum_c.send(z_steps[0])
    block = widen(block, more, order[1])
    more = exchange(block, "seq", order[2])
    so_far = ema_backward((2 * third, third), tuple(so_far), *consts)
    *so_far, over_c = join(*so_far, over_c)
    sum_c.add(over_c)
    for mark in z_steps[1:]:
        sum_c.add(sum_c.send(mark))
    block = widen(block, more, order[2])
    for step in order[3:]:
        block = widen(block, exchange(block, "seq", step), step)
    small = sum_c.value.astype(BF16)[None]
    for step in order:
        small = widen(small, exchange(small, "seq", step), step)
    block, small = in_order(block), in_order(small)
    g_a, g_b = block[:, :rows_a].reshape(-1, D).astype(F32), block[:, rows_a:].reshape(-1, D).astype(F32)
    small = small.reshape(-1, small.shape[-1]).astype(F32)
    g_c, g_d = small[:, :cols_c], small[:, cols_c:]
    dx, s1, s3, g_omega = so_far
    input_grad = (dtok + dx.reshape(T, D).astype(F32)).astype(BF16).reshape(tokens.shape)

    g_eta = rate * beta * s1
    g_beta = rate * eta * s1
    g_alpha = eta * beta * rate * (1.0 - rate) * (s1 - damp * rate * s3)
    g_delta = -eta * beta * rate * rate * damp * (1.0 - damp) * s3
    late = jnp.concatenate([g_alpha, g_delta, g_beta, g_eta, g_omega])
    late = sum_small(late.reshape(-1, n_wsh, D // n_wsh).transpose(1, 0, 2))
    widened = jnp.pad(sum_s, ((0, 0), (0, BLOCK - 1))).reshape(-1)
    diagonals = jnp.sum(jnp.pad(widened, (0, BLOCK)).reshape(BLOCK, 2 * BLOCK), axis=0)
    g_rel = jnp.roll(diagonals[::-1], BLOCK)
    early_parts = (
        sum_m[0], sum_v[0], sum_f[0], g_rel, sum_q[0], sum_q[1], sum_q[2],
        sum_d[0], sum_d[1], sum_d[2], sum_d[3], sum_d[4],
    )
    early = sum_small(jnp.concatenate([part.reshape(n_wsh, -1) for part in early_parts], axis=1))
    smalls, start = [], 0
    for part in early_parts:
        size = part.shape[0] // n_wsh
        smalls.append(early[start : start + size])
        start += size
    (
        g_mix_bias, g_value_bias, g_ffn_in_bias, g_rel, g_gain_q, g_gain_k, g_shift, gain_1, gain_2, shift_1, shift_2,
        g_ffn_out_bias,
    ) = smalls
    late = late.T
    tall_rows, wide_rows = ffn_out.shape[0], ffn_in.shape[0]
    n_seq = lax.axis_size("seq")
    first_rows = tall_rows // n_seq

    def unmerge(merged):
        parts = merged.reshape(n_seq, -1, D)
        top = parts[:, :first_rows].reshape(tall_rows, D)
        sides = parts[:, first_rows:].reshape(n_seq, 2, wide_rows // n_seq, D)
        return top, jnp.concatenate([sides[:, k].reshape(wide_rows, D) for k in range(2)], axis=1)

    g_ffn_out, g_ffn_in = unmerge(g_a)
    g_out, g_edges = unmerge(g_b)
    g_mix = jnp.concatenate([g_edges[:, :D], g_c, g_edges[:, D:]], axis=1)
    return (
        output.reshape(tokens.shape), input_grad,
        late[:, 0:H], late[:, H : 2 * H], late[:, 2 * H : 3 * H], late[:, 3 * H : 4 * H], late[:, 4 * H],
        g_mix, g_mix_bias, g_d, g_value_bias,
        jnp.stack([g_gain_q, g_gain_k], axis=1), g_shift, g_rel, g_out,
        jnp.stack([gain_1, gain_2], axis=1), jnp.stack([shift_1, shift_2], axis=1),
        g_ffn_in, g_ffn_in_bias, g_ffn_out, g_ffn_out_bias,
    )


def solution(mesh):
    in_specs = (
        P(None, "wsh", "seq", None),
        P(None, "wsh", "seq", None),
        P(None, "wsh"),
        P("wsh", None),
        P("wsh", None),
        P("wsh", None),
        P("wsh", None),
        P("wsh"),
        P("wsh", None),
        P("wsh"),
        P("wsh", None),
        P("wsh"),
        P("wsh", None),
        P("wsh"),
        P("wsh"),
        P("wsh", None),
        P("wsh", None),
        P("wsh", None),
        P("wsh", None),
        P("wsh"),
        P("wsh", None),
        P("wsh"),
    )
    out_specs = (
        P(None, "wsh", "seq", None),
        P(None, "wsh", "seq", None),
        P("wsh", None),
        P("wsh", None),
        P("wsh", None),
        P("wsh", None),
        P("wsh"),
        P("wsh", None),
        P("wsh"),
        P("wsh", None),
        P("wsh"),
        P("wsh", None),
        P("wsh"),
        P("wsh"),
        P("wsh", None),
        P("wsh", None),
        P("wsh", None),
        P("wsh", None),
        P("wsh"),
        P("wsh", None),
        P("wsh"),
    )
    return jax.shard_map(body, mesh=mesh, in_specs=in_specs, out_specs=out_specs, check_vma=False)
```

```python
import functools

import jax
import jax.numpy as jnp
from jax import lax
from jax.experimental import pallas as pl
from jax.experimental.pallas import tpu as pltpu
from jax.sharding import PartitionSpec as P

BLOCK = 128
LANES = 128
CH = 8
PAD = 8
CHUNK = 768
STRIP = 32
EPSILON = 1e-05
VMEM_LIMIT = 62 * 1024 * 1024
F32 = jnp.float32
BF16 = jnp.bfloat16


def dot_rows(left_op, right_op):
    return jnp.einsum("ri,rj->ij", left_op, right_op, preferred_element_type=jnp.float32)


def skew_matrix(wrapped):
    lead = wrapped.shape[:-1]
    flat = jnp.tile(wrapped, (1,) * len(lead) + (BLOCK,))[..., : BLOCK * (2 * BLOCK - 1)]
    return flat.reshape(lead + (BLOCK, 2 * BLOCK - 1))[..., :BLOCK]


def power(v, n):
    k = 1
    while k < n:
        v = v * v
        k *= 2
    return v

def rows_of(scr, s, T):
    return scr[pl.ds(s, CH, stride=T+PAD), :]

def spread(scr, v, T):
    for k in range(CH):
        scr[k*(T+PAD):k*(T+PAD)+T, :] = v[k*T:(k+1)*T, :]

def collect(scr, T):
    return jnp.concatenate([scr[k*(T+PAD):k*(T+PAD)+T, :] for k in range(CH)], axis=0)

def ends_kernel(H, T, x_ref, q_ref, e_ref, s_ref, scr):
    spread(scr, x_ref[0].astype(F32), T)
    q = [jnp.broadcast_to(q_ref[h:h+1, :], (CH, LANES)) for h in range(H)]
    def step(s, st):
        xs = rows_of(scr, s, T)
        return tuple(q[h]*st[h] + xs for h in range(H))
    st = lax.fori_loop(0, T, step, tuple(jnp.zeros((CH,LANES),F32) for _ in range(H)), unroll=8)
    for h in range(H):
        e_ref[0, h*CH:(h+1)*CH, :] = st[h]
    qT = power(q_ref[...], T)
    c = jnp.zeros((H,LANES),F32)
    for k in range(CH):
        c = qT*c + e_ref[0, pl.ds(k,H,stride=CH), :]
    s_ref[0] = c

def fwd_kernel(H, T, x_ref, q_ref, w_ref, om_ref, e_ref, c_ref, *refs):
    xp_ref, p_ref, f_ref, scr, cs, ps = refs[-6:]
    spread(scr, x_ref[0].astype(F32), T)
    qT = power(q_ref[...], T)
    c = c_ref[0]
    for k in range(CH):
        cs[pl.ds(k,H,stride=CH), :] = c
        c = qT*c + e_ref[0, pl.ds(k,H,stride=CH), :]
    q = [jnp.broadcast_to(q_ref[h:h+1, :], (CH, LANES)) for h in range(H)]
    w = [jnp.broadcast_to(w_ref[h:h+1, :], (CH, LANES)) for h in range(H)]
    om = jnp.broadcast_to(om_ref[...], (CH,LANES))
    def step(s, st):
        xs = rows_of(scr, s, T)
        st = tuple(q[h]*st[h] + xs for h in range(H))
        terms = [w[h]*st[h] for h in range(H)]
        while len(terms) > 1:
            terms = [terms[i]+terms[i+1] for i in range(0,len(terms)-1,2)] + ([terms[-1]] if len(terms)%2 else [])
        ps[pl.ds(s, CH, stride=T+PAD), :] = terms[0] + om*xs
        return st
    st = lax.fori_loop(0, T, step, tuple(cs[h*CH:(h+1)*CH, :] for h in range(H)), unroll=8)
    for h in range(H):
        f_ref[0, h*CH:(h+1)*CH, :] = st[h]
    p = collect(ps, T)
    p_ref[0] = p
    xp_ref[0] = (p*jax.nn.sigmoid(p)).astype(xp_ref.dtype)

def bends_kernel(H, T, dxp_ref, p_ref, q_ref, d_ref, e_ref, s_ref, ds):
    p = p_ref[0]
    sg = jax.nn.sigmoid(p)
    d = dxp_ref[0].astype(F32) * (sg*(1.0+p*(1.0-sg)))
    d_ref[0] = d
    spread(ds, d, T)
    q = [jnp.broadcast_to(q_ref[h:h+1, :], (CH, LANES)) for h in range(H)]
    def step(s, st):
        xs = rows_of(ds, T-1-s, T)
        return tuple(q[h]*st[h] + xs for h in range(H))
    st = lax.fori_loop(0, T, step, tuple(jnp.zeros((CH,LANES),F32) for _ in range(H)), unroll=8)
    for h in range(H):
        e_ref[0, h*CH:(h+1)*CH, :] = st[h]
    qT = power(q_ref[...], T)
    c = jnp.zeros((H,LANES),F32)
    for k in reversed(range(CH)):
        c = qT*c + e_ref[0, pl.ds(k,H,stride=CH), :]
    s_ref[0] = c

def bwd_kernel(H, T, d_ref, x_ref, q_ref, qi_ref, w_ref, om_ref, f_ref, e_ref, c_ref, t_ref, *refs):
    dx_ref, s1_ref, s3_ref, go_ref, scr, cs, dx, ds = refs[-8:]
    g = pl.program_id(1)
    x = x_ref[0].astype(F32)
    spread(scr, x, T)
    dv = d_ref[0]
    spread(ds, dv, T)
    qT = power(q_ref[...], T)
    c = c_ref[0]
    for k in reversed(range(CH)):
        cs[pl.ds(k,H,stride=CH), :] = c
        c = qT*c + e_ref[0, pl.ds(k,H,stride=CH), :]
    om = jnp.broadcast_to(om_ref[...], (CH,LANES))
    HH = H//2
    zero = jnp.zeros((CH,LANES),F32)
    @pl.when(g==0)
    def _():
        go_ref[...] = jnp.zeros_like(go_ref)
        s1_ref[...] = jnp.zeros_like(s1_ref)
        s3_ref[...] = jnp.zeros_like(s3_ref)
    go_ref[...] += jnp.sum(dv*x, axis=0, keepdims=True)
    for half in range(2):
        hs = range(half*HH, half*HH+HH)
        q = [jnp.broadcast_to(q_ref[h:h+1, :], (CH, LANES)) for h in hs]
        qi = [jnp.broadcast_to(qi_ref[h:h+1, :], (CH, LANES)) for h in hs]
        w = [jnp.broadcast_to(w_ref[h:h+1, :], (CH, LANES)) for h in hs]
        def step(s, carry):
            l, st, a1, a3 = carry
            at = pl.ds(T-1-s, CH, stride=T+PAD)
            d = ds[at, :]
            xs = scr[at, :]
            a1 = tuple(a1[i] + d*st[i] for i in range(HH))
            l = tuple(q[i]*l[i] + d for i in range(HH))
            st = tuple((st[i]-xs)*qi[i] for i in range(HH))
            a3 = tuple(a3[i] + l[i]*st[i] for i in range(HH))
            terms = [w[i]*l[i] for i in range(HH)]
            while len(terms) > 1:
                terms = [terms[i]+terms[i+1] for i in range(0,len(terms)-1,2)]
            if half == 0:
                dx[at, :] = terms[0] + om*d
            else:
                dx[at, :] = dx[at, :] + terms[0]
            return l, st, a1, a3
        init = (tuple(cs[h*CH:(h+1)*CH,:] for h in hs), tuple(f_ref[0,h*CH:(h+1)*CH,:] for h in hs), (zero,)*HH, (zero,)*HH)
        l, st, a1, a3 = lax.fori_loop(0, T, step, init, unroll=4)
        for i,h in enumerate(hs):
            s1_ref[h:h+1,:] += jnp.sum(a1[i],axis=0,keepdims=True)
            s3_ref[h:h+1,:] += jnp.sum(a3[i],axis=0,keepdims=True)
    dx_ref[0] = (t_ref[0] + collect(dx, T).astype(dx_ref.dtype).astype(F32)).astype(dx_ref.dtype)

def specs(L, H, first=0):
    blk = pl.BlockSpec((1, L, LANES), lambda c, g: (g, 0, c + first))
    par = pl.BlockSpec((H, LANES), lambda c, g: (0, c + first))
    one = pl.BlockSpec((1, LANES), lambda c, g: (0, c + first))
    st = pl.BlockSpec((1, H * CH, LANES), lambda c, g: (g, 0, c + first))
    car = pl.BlockSpec((1, H, LANES), lambda c, g: (g, 0, c + first))
    return blk, par, one, st, car


def ema_ends(x, q):
    G, L, C = x.shape
    H = q.shape[0]
    blk, par, one, st, car = specs(L, H)
    return pl.pallas_call(
        functools.partial(ends_kernel, H, L // CH),
        grid=(C // LANES, G),
        in_specs=[blk, par],
        out_specs=[st, car],
        out_shape=[jax.ShapeDtypeStruct((G, H * CH, C), F32), jax.ShapeDtypeStruct((G, H, C), F32)],
        scratch_shapes=[pltpu.VMEM((L + CH * PAD, LANES), F32)],
        cost_estimate=cost_of(0, 11),
        name="ema_ends",
    )(x, q)


def ema_forward(span, so_far, x, q, w, om, e, c):
    G, L, C = x.shape
    H = q.shape[0]
    first, count = span
    blk, par, one, st, car = specs(L, H, first)
    return pl.pallas_call(
        functools.partial(fwd_kernel, H, L // CH),
        grid=(count, G),
        in_specs=[blk, par, par, one, st, car] + [pl.BlockSpec(memory_space=pl.ANY)] * len(so_far),
        out_specs=[blk, blk, st],
        out_shape=[
            jax.ShapeDtypeStruct((G, L, C), BF16), jax.ShapeDtypeStruct((G, L, C), F32),
            jax.ShapeDtypeStruct((G, H * CH, C), F32),
        ],
        scratch_shapes=[
            pltpu.VMEM((L + CH * PAD, LANES), F32), pltpu.VMEM((H * CH, LANES), F32),
            pltpu.VMEM((L + CH * PAD, LANES), F32),
        ],
        input_output_aliases={6 + k: k for k in range(len(so_far))},
        cost_estimate=cost_of(0, 3 * count),
        name="ema_forward",
    )(x, q, w, om, e, c, *so_far)


def ema_back_ends(dxp, p, q):
    G, L, C = p.shape
    H = q.shape[0]
    blk, par, one, st, car = specs(L, H)
    return pl.pallas_call(
        functools.partial(bends_kernel, H, L // CH),
        grid=(C // LANES, G),
        in_specs=[blk, blk, par],
        out_specs=[blk, st, car],
        out_shape=[
            jax.ShapeDtypeStruct((G, L, C), F32), jax.ShapeDtypeStruct((G, H * CH, C), F32),
            jax.ShapeDtypeStruct((G, H, C), F32),
        ],
        scratch_shapes=[pltpu.VMEM((L + CH * PAD, LANES), F32)],
        cost_estimate=cost_of(0, 15),
        name="ema_back_ends",
    )(dxp, p, q)


def ema_backward(span, so_far, d, x, q, qi, w, om, f, e, c, t):
    G, L, C = x.shape
    H = q.shape[0]
    first, count = span
    blk, par, one, st, car = specs(L, H, first)
    return pl.pallas_call(
        functools.partial(bwd_kernel, H, L // CH),
        grid=(count, G),
        in_specs=[blk, blk, par, par, par, one, st, st, car, blk]
        + [pl.BlockSpec(memory_space=pl.ANY)] * len(so_far),
        out_specs=[blk, par, par, one],
        out_shape=[
            jax.ShapeDtypeStruct((G, L, C), BF16), jax.ShapeDtypeStruct((H, C), F32),
            jax.ShapeDtypeStruct((H, C), F32), jax.ShapeDtypeStruct((1, C), F32),
        ],
        scratch_shapes=[
            pltpu.VMEM((L + CH * PAD, LANES), F32), pltpu.VMEM((H * CH, LANES), F32),
            pltpu.VMEM((L + CH * PAD, LANES), F32), pltpu.VMEM((L + CH * PAD, LANES), F32),
        ],
        input_output_aliases={10 + k: k for k in range(len(so_far))},
        cost_estimate=cost_of(0, 8 * count),
        name="ema_backward",
    )(d, x, q, qi, w, om, f, e, c, t, *so_far)


def sig(v):
    return 0.5 * jnp.tanh(0.5 * v) + 0.5


def dot_nn(left_op, right_op):
    return jnp.dot(left_op, right_op, preferred_element_type=F32)


def dot_nt(left_op, right_op):
    return lax.dot_general(left_op, right_op, (((1,), (1,)), ((), ())), preferred_element_type=F32)


def dot_tn(left_op, right_op):
    return lax.dot_general(left_op, right_op, (((0,), (0,)), ((), ())), preferred_element_type=F32)


def piece_copies(pieces, targets):
    own, core, across, across_y, across_core, across_y_core = pieces
    j = lax.axis_index("wsh")
    bit = lax.rem(lax.axis_index("seq"), 2)
    copies = []
    start = 0
    for target in targets:
        rows, cols = target.shape[0] // 4, pl.ds(start, target.shape[1])
        half = rows // 2
        spots = (
            (own, j * rows),
            (core, (j ^ 1) * rows),
            (across, (j ^ 2) * rows + bit * half),
            (across_y, (j ^ 2) * rows + (1 - bit) * half),
            (across_core, (j ^ 3) * rows + bit * half),
            (across_y_core, (j ^ 3) * rows + (1 - bit) * half),
        )
        for piece, at in spots:
            rows_at = pl.ds(pl.multiple_of(at, 32), piece.shape[0])
            copies.append((piece.at[:, cols], target.at[rows_at, :]))
        start += target.shape[1]
    return copies


def bring(groups, sem):
    @pl.when(pl.program_id(0) == 0)
    def _():
        copies = []
        for pieces, targets in groups:
            for source, spot in piece_copies(pieces, targets):
                copies.append(pltpu.make_async_copy(source, spot, sem.at[len(copies)]))
        for copy in copies:
            copy.start()
        for copy in copies:
            copy.wait()


def fold(rows):
    total = rows[:8]
    for k in range(8, STRIP, 8):
        total = total + rows[k : k + 8]
    return total


def add_sums(ref, at, rows):
    ref[:, at] += jnp.sum(rows, axis=0, keepdims=True)


def mix_fwd_kernel(R, dims, x_ref, xp_ref, bm_ref, bv_ref, qk_ref, rel_ref, *refs):
    D, Z, V = dims
    pieces, refs = refs[:18], refs[18:]
    u_ref, h_ref, r_ref, v_ref, z_ref, p_ref, m_ref, wm, wv, wo, sem = refs
    bring(((pieces[:6], (wm,)), (pieces[6:12], (wv,)), (pieces[12:], (wo,))), sem)
    xp = xp_ref[...]
    x = x_ref[...]
    z = dot_nn(xp, wm[:, D : D + Z]) + bm_ref[:, D : D + Z]
    z_ref[...] = z
    shared = z * sig(z)
    query = (shared * qk_ref[0:1, :] + qk_ref[2:3, :]).astype(BF16)
    key = (shared * qk_ref[1:2, :]).astype(BF16)
    probs = []
    row = lax.broadcasted_iota(jnp.int32, (BLOCK, BLOCK), 0)
    col = lax.broadcasted_iota(jnp.int32, (BLOCK, BLOCK), 1)
    for b in range(R // BLOCK):
        at = slice(b * BLOCK, (b + 1) * BLOCK)
        score = dot_nt(query[at], key[at]) * Z ** (-0.5) + rel_ref[...]
        score = jnp.where(row >= col, score, -1e30)
        grown = jnp.exp(score - jnp.max(score, axis=-1, keepdims=True))
        prob = grown / jnp.sum(grown, axis=-1, keepdims=True)
        p_ref[at, :] = prob
        probs.append(prob.astype(BF16))
    for c in range(0, V, CHUNK):
        at = slice(c, c + CHUNK)
        rat = slice(D + Z + c, D + Z + c + CHUNK)
        v = dot_nn(x, wv[:, at]) + bv_ref[:, at]
        v_ref[:, at] = v
        value = (v * sig(v)).astype(BF16)
        r = dot_nn(xp, wm[:, rat]) + bm_ref[:, rat]
        r_ref[:, at] = r
        reset = r * sig(r)
        for b in range(R // BLOCK):
            rows = slice(b * BLOCK, (b + 1) * BLOCK)
            m_ref[rows, at] = (reset[rows] * dot_nn(probs[b], value[rows])).astype(BF16)
    u_ref[...] = dot_nn(xp, wm[:, :D]) + bm_ref[:, :D]
    h_ref[...] = dot_nn(xp, wm[:, D + Z + V :]) + bm_ref[:, D + Z + V :] + dot_nn(m_ref[...], wo[...])


def slope_of(pre, logistic):
    return logistic * (1.0 + pre * (1.0 - logistic))


def mean_of(rows):
    return jnp.mean(rows, axis=-1, keepdims=True)


def ffn_kernel(R, dims, x_ref, u_ref, h_ref, cot_ref, live_ref, gn_ref, bf_ref, bo_ref, *refs):
    D, FF = dims
    pieces, refs = refs[:12], refs[12:]
    (
        o_ref, h1_ref, act_ref, dg_ref, df_ref, dum_ref, dt_ref, sd_ref, sf_ref,
        wi, wo, f_scr, n1_scr, a_scr, i1_scr, sem,
    ) = refs
    bring(((pieces[:6], (wi,)), (pieces[6:], (wo,))), sem)

    @pl.when(pl.program_id(0) == 0)
    def _():
        sd_ref[...] = jnp.zeros_like(sd_ref)
        sf_ref[...] = jnp.zeros_like(sf_ref)

    g1, g2, b1, b2 = (gn_ref[k : k + 1, :] for k in range(4))
    part = min(256, R)

    def strips(s):
        return [slice(k, k + STRIP) for k in range(s * part, (s + 1) * part, STRIP)]

    def first(s):
        for at in strips(s):
            x = x_ref[at, :].astype(F32)
            h = h_ref[at, :]
            y = x + sig(u_ref[at, :]) * (h * sig(h) - x)
            center = y - mean_of(y)
            inverse = lax.rsqrt(mean_of(center * center) + EPSILON)
            n1 = center * inverse
            n1_scr[at, :] = n1
            i1_scr[at, :] = jnp.broadcast_to(inverse, (STRIP, LANES))
            h1_ref[at, :] = (n1 * g1 + b1).astype(BF16)

    def spread(s):
        rows = slice(s * part, (s + 1) * part)
        for c in range(0, FF, CHUNK):
            at = slice(c, c + CHUNK)
            f = dot_nn(h1_ref[rows, :], wi[:, at]) + bf_ref[:, at]
            f_scr[rows, at] = f
            act_ref[rows, at] = (f * sig(f)).astype(BF16)

    def narrow(s):
        rows = slice(s * part, (s + 1) * part)
        a_scr[rows, :] = dot_nn(act_ref[rows, :], wo[...])

    def second(s):
        zero = jnp.zeros((8, D), F32)
        s_gain, s_shift, s_bias = zero, zero, zero
        for at in strips(s):
            y2 = n1_scr[at, :] * g1 + b1 + a_scr[at, :] + bo_ref[...]
            center = y2 - mean_of(y2)
            inverse = lax.rsqrt(mean_of(center * center) + EPSILON)
            n2 = center * inverse
            live = live_ref[at, :]
            o_ref[at, :] = ((n2 * g2 + b2) * live).astype(BF16)
            dn = cot_ref[at, :].astype(F32) * live
            w = dn * g2
            dy2 = inverse * (w - mean_of(w) - n2 * mean_of(w * n2))
            a_scr[at, :] = dy2
            dg_ref[at, :] = dy2.astype(BF16)
            s_gain, s_shift, s_bias = s_gain + fold(dn * n2), s_shift + fold(dn), s_bias + fold(dy2)
        sd_ref[1:2, :] += jnp.sum(s_gain, axis=0, keepdims=True)
        sd_ref[3:4, :] += jnp.sum(s_shift, axis=0, keepdims=True)
        sd_ref[4:5, :] += jnp.sum(s_bias, axis=0, keepdims=True)

    def spread_back(s):
        rows = slice(s * part, (s + 1) * part)
        for c in range(0, FF, CHUNK):
            at = slice(c, c + CHUNK)
            f = f_scr[rows, at]
            df = (dot_nt(dg_ref[rows, :], wo[at, :]) * slope_of(f, sig(f))).astype(BF16)
            df_ref[rows, at] = df
            add_sums(sf_ref, at, df.astype(F32))

    def narrow_back(s):
        rows = slice(s * part, (s + 1) * part)
        a_scr[rows, :] += dot_nt(df_ref[rows, :], wi[...])

    def third(s):
        zero = jnp.zeros((8, D), F32)
        s_gain, s_shift = zero, zero
        for at in strips(s):
            dh1 = a_scr[at, :]
            n1 = n1_scr[at, :]
            w = dh1 * g1
            dy = i1_scr[at, 0:1] * (w - mean_of(w) - n1 * mean_of(w * n1))
            x = x_ref[at, :].astype(F32)
            h = h_ref[at, :]
            sh = sig(h)
            gate = sig(u_ref[at, :])
            rest = 1.0 - gate
            dyg = dy * gate
            dum_ref[at, :D] = (dyg * (h * sh - x) * rest).astype(BF16)
            dum_ref[at, D:] = (dyg * slope_of(h, sh)).astype(BF16)
            dt_ref[at, :] = dy * rest
            s_gain, s_shift = s_gain + fold(dh1 * n1), s_shift + fold(dh1)
        sd_ref[0:1, :] += jnp.sum(s_gain, axis=0, keepdims=True)
        sd_ref[2:3, :] += jnp.sum(s_shift, axis=0, keepdims=True)

    stages = (first, spread, narrow, second, spread_back, narrow_back, third)
    count = R // part
    for tick in range(len(stages) + count - 1):
        for s in range(count):
            if 0 <= tick - s < len(stages):
                stages[tick - s](s)


def sum_spots(D, Z, V, FF):
    spans = [("mix", D, Z), ("rel", 0, 2 * BLOCK), ("qk", 0, 3 * Z), ("mix", 0, D), ("mix", D + Z + V, D)]
    spans += [("mix", D + Z + k, D) for k in range(0, V, D)] + [("value", k, D) for k in range(0, V, D)]
    spans += [("ffn", k, D) for k in range(0, FF, D)] + [("rows", k * D, D) for k in range(5)]
    spots, place = [], 0
    for name, start, size in spans:
        spots.append((name, start, place // D, place % D, size))
        place += size
    return spots


def mix_bwd_kernel(R, dims, dum_ref, dt_ref, r_ref, v_ref, z_ref, p_ref, qk_ref, sd_ref, sf_ref, *refs):
    D, Z, V = dims
    pieces, refs = refs[:18], refs[18:]
    db_ref, dv_ref, dxp_ref, do_ref, all_ref, sm_ref, sv_ref, sq_ref, ss_ref, wm, wv, wo, acc, sem = refs
    bring(((pieces[:6], (wm,)), (pieces[6:12], (wv,)), (pieces[12:], (wo,))), sem)

    @pl.when(pl.program_id(0) == 0)
    def _():
        for ref in (sm_ref, sv_ref, sq_ref, ss_ref):
            ref[...] = jnp.zeros_like(ref)

    last = D + Z + V
    blocks = [slice(b * BLOCK, (b + 1) * BLOCK) for b in range(R // BLOCK)]
    full = [p_ref[rows, :] for rows in blocks]
    probs = [prob.astype(BF16) for prob in full]
    dprob = [jnp.zeros((BLOCK, BLOCK), F32) for _ in blocks]
    size = 512

    def chunk(c):
        at = slice(c, c + size)
        rat = slice(D + Z + c, D + Z + c + size)
        zat = slice(Z + c, Z + c + size)
        dmix = dot_nt(dum_ref[:, D:], wo[at, :])
        sum_r = jnp.zeros((1, size), F32)
        sum_v = jnp.zeros((1, size), F32)
        for b, rows in enumerate(blocks):
            r = r_ref[rows, at]
            v = v_ref[rows, at]
            sr = sig(r)
            sv = sig(v)
            value = (v * sv).astype(BF16)
            datt = (dmix[rows] * (r * sr)).astype(BF16)
            dr = (dmix[rows] * slope_of(r, sr) * dot_nn(probs[b], value)).astype(BF16)
            db_ref[rows, zat] = dr
            sum_r += jnp.sum(dr.astype(F32), axis=0, keepdims=True)
            dprob[b] += dot_nt(datt, value)
            dv = (dot_tn(probs[b], datt) * slope_of(v, sv)).astype(BF16)
            dv_ref[rows, at] = dv
            sum_v += jnp.sum(dv.astype(F32), axis=0, keepdims=True)
        sm_ref[:, rat] += sum_r
        sv_ref[:, at] += sum_v

    def give(c):
        at = slice(c, c + size)
        rat = slice(D + Z + c, D + Z + c + size)
        zat = slice(Z + c, Z + c + size)
        acc[...] += dot_nt(db_ref[:, zat], wm[:, rat])
        do_ref[...] += dot_nt(dv_ref[:, at], wv[:, at])

    starts = list(range(0, V, size))
    chunk(starts[0])
    acc[...] = dot_nt(dum_ref[:, :D], wm[:, :D]) + dot_nt(dum_ref[:, D:], wm[:, last:])
    do_ref[...] = dt_ref[...]
    for n, c in enumerate(starts[1:]):
        chunk(c)
        give(starts[n])
    add_sums(sm_ref, slice(0, D), dum_ref[:, :D].astype(F32))
    add_sums(sm_ref, slice(last, D + last), dum_ref[:, D:].astype(F32))
    for b, rows in enumerate(blocks):
        z = z_ref[rows, :]
        sz = sig(z)
        shared = z * sz
        query = (shared * qk_ref[0:1, :] + qk_ref[2:3, :]).astype(BF16)
        key = (shared * qk_ref[1:2, :]).astype(BF16)
        inner = jnp.sum(full[b] * dprob[b], axis=-1, keepdims=True)
        ds = (full[b] * (dprob[b] - inner)).astype(BF16)
        ss_ref[...] += ds.astype(F32)
        dq = dot_nn(ds, key) * Z ** (-0.5)
        dk = dot_tn(ds, query) * Z ** (-0.5)
        sq_ref[0:1, :] += jnp.sum(dq * shared, axis=0, keepdims=True)
        sq_ref[1:2, :] += jnp.sum(dk * shared, axis=0, keepdims=True)
        sq_ref[2:3, :] += jnp.sum(dq, axis=0, keepdims=True)
        dz = (dq * qk_ref[0:1, :] + dk * qk_ref[1:2, :]) * slope_of(z, sz)
        dz = dz.astype(BF16)
        db_ref[rows, :Z] = dz
        add_sums(sm_ref, slice(D, D + Z), dz.astype(F32))
    give(starts[-1])
    dxp_ref[...] = (acc[...] + dot_nt(db_ref[:, :Z], wm[:, D : D + Z])).astype(BF16)

    @pl.when(pl.program_id(0) == pl.num_programs(0) - 1)
    def _():
        moved = jnp.concatenate([ss_ref[...].T, jnp.zeros((BLOCK, BLOCK), F32)], axis=1)
        row = lax.broadcasted_iota(jnp.int32, moved.shape, 0)
        step = 1
        while step < BLOCK:
            moved = jnp.where(jnp.bitwise_and(row, step) == 0, pltpu.roll(moved, step, 1), moved)
            step *= 2
        spots = sum_spots(D, Z, V, sf_ref.shape[1])
        sums = {
            "mix": sm_ref[...], "value": sv_ref[...], "ffn": sf_ref[...], "rel": jnp.sum(moved, axis=0, keepdims=True),
            "qk": jnp.concatenate([sq_ref[k : k + 1, :] for k in range(3)], axis=1),
            "rows": jnp.concatenate([sd_ref[k : k + 1, :] for k in range(5)], axis=1),
        }
        all_ref[...] = jnp.zeros_like(all_ref)
        for name, start, row, col, size in spots:
            all_ref[row : row + 1, col : col + size] = sums[name][:, start : start + size]


def cost_of(flops, microseconds):
    return pl.CostEstimate(flops=flops, bytes_accessed=microseconds * 3_600_000, transcendentals=0)


def any_specs(n):
    return [pl.BlockSpec(memory_space=pl.ANY)] * n


def tile(R, n):
    return pl.BlockSpec((R, n), lambda t: (t, 0))


def fixed(r, n):
    return pl.BlockSpec((r, n), lambda t: (0, 0))


def shape(r, n, dtype=F32):
    return jax.ShapeDtypeStruct((r, n), dtype)


def mix_forward(R, x, xp, bm, bv, qk, rel, pieces):
    T, D = x.shape
    V = bv.shape[1]
    Z = qk.shape[1]
    E = bm.shape[1]
    return pl.pallas_call(
        functools.partial(mix_fwd_kernel, R, (D, Z, V)),
        grid=(T // R,),
        in_specs=[tile(R, D), tile(R, D), fixed(1, E), fixed(1, V), fixed(8, Z), fixed(BLOCK, BLOCK)]
        + any_specs(18),
        out_specs=[tile(R, D), tile(R, D), tile(R, V), tile(R, V), tile(R, Z), tile(R, BLOCK), tile(R, V)],
        out_shape=[
            shape(T, D), shape(T, D), shape(T, V), shape(T, V), shape(T, Z), shape(T, BLOCK), shape(T, V, BF16),
        ],
        scratch_shapes=[
            pltpu.VMEM((D, E), BF16), pltpu.VMEM((D, V), BF16), pltpu.VMEM((V, D), BF16),
            pltpu.SemaphoreType.DMA((18,)),
        ],
        compiler_params=pltpu.CompilerParams(vmem_limit_bytes=VMEM_LIMIT),
        cost_estimate=cost_of(2 * T * D * (E + 2 * V), 33),
        name="mix_forward",
    )(x, xp, bm, bv, qk, rel, *pieces)


def ffn_both(R, x, u, h, cot, live, norms, bf, bo, pieces):
    T, D = x.shape
    FF = bf.shape[1]
    return pl.pallas_call(
        functools.partial(ffn_kernel, R, (D, FF)),
        grid=(T // R,),
        in_specs=[tile(R, D), tile(R, D), tile(R, D), tile(R, D), tile(R, 1), fixed(8, D), fixed(1, FF), fixed(1, D)]
        + any_specs(12),
        out_specs=[
            tile(R, D), tile(R, D), tile(R, FF), tile(R, D), tile(R, FF), tile(R, 2 * D), tile(R, D),
            fixed(8, D), fixed(1, FF),
        ],
        out_shape=[
            shape(T, D, BF16), shape(T, D, BF16), shape(T, FF, BF16), shape(T, D, BF16), shape(T, FF, BF16),
            shape(T, 2 * D, BF16), shape(T, D), shape(8, D), shape(1, FF),
        ],
        scratch_shapes=[
            pltpu.VMEM((D, FF), BF16), pltpu.VMEM((FF, D), BF16), pltpu.VMEM((R, FF), F32), pltpu.VMEM((R, D), F32),
            pltpu.VMEM((R, D), F32), pltpu.VMEM((R, 128), F32), pltpu.SemaphoreType.DMA((12,)),
        ],
        compiler_params=pltpu.CompilerParams(vmem_limit_bytes=VMEM_LIMIT),
        cost_estimate=cost_of(2 * T * D * 4 * FF, 50),
        name="ffn_both",
    )(x, u, h, cot, live, norms, bf, bo, *pieces)


def mix_backward(R, dum, dt, r, v, z, p, qk, sum_d, sum_f, pieces):
    T, D = dt.shape
    V = r.shape[1]
    Z = qk.shape[1]
    E = 2 * D + Z + V
    return pl.pallas_call(
        functools.partial(mix_bwd_kernel, R, (D, Z, V)),
        grid=(T // R,),
        in_specs=[
            tile(R, 2 * D), tile(R, D), tile(R, V), tile(R, V), tile(R, Z), tile(R, BLOCK), fixed(8, Z),
            fixed(8, D), fixed(1, sum_f.shape[1]),
        ]
        + any_specs(18),
        out_specs=[
            tile(R, Z + V), tile(R, V), tile(R, D), tile(R, D), fixed(16, D),
        ],
        out_shape=[
            shape(T, Z + V, BF16), shape(T, V, BF16), shape(T, D, BF16), shape(T, D), shape(16, D),
        ],
        scratch_shapes=[
            pltpu.VMEM((1, E), F32), pltpu.VMEM((1, V), F32), pltpu.VMEM((8, Z), F32), pltpu.VMEM((BLOCK, BLOCK), F32),
            pltpu.VMEM((D, E), BF16), pltpu.VMEM((D, V), BF16), pltpu.VMEM((V, D), BF16), pltpu.VMEM((R, D), F32),
            pltpu.SemaphoreType.DMA((18,)),
        ],
        compiler_params=pltpu.CompilerParams(vmem_limit_bytes=VMEM_LIMIT),
        cost_estimate=cost_of(2 * T * D * (E + 2 * V), 40),
        name="mix_backward",
    )(dum, dt, r, v, z, p, qk, sum_d, sum_f, *pieces)


def exchange(value, axis, step):
    return lax.ppermute(value, axis, [(k, k ^ step) for k in range(lax.axis_size(axis))])


def join(*values):
    return lax.optimization_barrier(values)


def own_half(own):
    half = own.shape[0] // 2
    return lax.dynamic_slice_in_dim(own, lax.rem(lax.axis_index("seq"), 2) * half, half, 0)


def over_x(value):
    return exchange(value, "wsh", 2)


def over_y(value):
    return exchange(value, "seq", 1)


def over_core(value):
    return exchange(value, "wsh", 1)


def gather_small(own):
    j = lax.axis_index("wsh")
    four = jnp.stack([own] + [exchange(own, "wsh", d) for d in range(1, 4)])
    return jnp.stack([lax.dynamic_index_in_dim(four, j ^ k, 0, False) for k in range(4)])


class Carry:
    def __init__(self, states, decay, reverse):
        self.entry, self.total = jnp.zeros_like(states), states
        self.own, self.window, self.reverse = jnp.ones_like(decay), decay, reverse

    def send(self, step):
        return exchange(self.total, "seq", step)

    def add(self, step, sent):
        bit = lax.rem(lax.axis_index("seq") // step, 2)
        later = (bit == 0) if self.reverse else (bit == 1)
        self.entry = jnp.where(later, self.entry + self.own * sent, self.entry)
        self.total = jnp.where(later, self.total + self.window * sent, sent + self.window * self.total)
        self.own = jnp.where(later, self.own * self.window, self.own)
        self.window = self.window * self.window


def pick(value, dim, bit):
    return lax.dynamic_index_in_dim(value, bit, dim, False)


def send_half(value, dim, mark):
    axis, step = mark
    bit = lax.rem(lax.axis_index(axis) // step, 2)
    return exchange(pick(value, dim, 1 - bit).astype(BF16), axis, step), pick(value, dim, bit)


def add_half(sent, kept):
    return kept + sent.astype(F32)


def seq_steps():
    return [2**k for k in range(lax.axis_size("seq").bit_length() - 1)]


def send_core(grad):
    rows, cols = grad.shape
    bits = (2,) * len(seq_steps())
    rest = rows // lax.axis_size("wsh") // lax.axis_size("seq")
    return send_half(grad.reshape((2, 2) + bits + (rest, cols)), 1, ("wsh", 1))


def merge(parts, cols):
    pieces = []
    for part in parts:
        for c in range(0, part.shape[-1], cols):
            pieces.append(part[..., c : c + cols])
    return jnp.concatenate(pieces, axis=-2)


class Sum:
    def __init__(self, value):
        self.value = value
        self.marks = [("wsh", 2)] + [("seq", s) for s in reversed(seq_steps())]

    def send(self, mark):
        dim = self.marks.index(mark)
        self.marks.pop(dim)
        sent, self.kept = send_half(self.value, dim, mark)
        return sent

    def add(self, sent):
        self.value = add_half(sent, self.kept)


def widen(block, other, step):
    bit = lax.rem(lax.axis_index("seq") // step, 2)
    first = jnp.where(bit == 0, block, other)
    second = jnp.where(bit == 0, other, block)
    return jnp.concatenate([first, second], axis=0)


def in_order(block):
    bits = block.shape[0].bit_length() - 1
    split = block.reshape((2,) * bits + block.shape[1:])
    turned = split.transpose(tuple(reversed(range(bits))) + (bits, bits + 1))
    return turned.reshape(block.shape)


def sum_over_wsh(value):
    j = lax.axis_index("wsh")
    total = lax.dynamic_index_in_dim(value, j, 0, False)
    for d in range(1, 4):
        total = total + exchange(lax.dynamic_index_in_dim(value, j ^ d, 0, False), "wsh", d)
    return total


def sum_over_seq(total):
    for step in reversed(seq_steps()):
        total = total + exchange(total, "seq", step)
    return total


def body(
    tokens, cotangent, lengths, ema_alpha, ema_delta, ema_beta, ema_eta, ema_omega, mix_weight, mix_bias,
    value_weight, value_bias, qk_gain, qk_bias, rel_bias, out_weight, norm_gain, norm_bias, ffn_in, ffn_in_bias,
    ffn_out, ffn_out_bias,
):
    micro, seqs, L, D = tokens.shape
    G = micro * seqs
    T = G * L
    H = ema_alpha.shape[1]
    R = min(512, T)
    n_wsh = lax.axis_size("wsh")
    i = lax.axis_index("seq")
    Z = qk_gain.shape[0] * n_wsh
    V = value_weight.shape[1]
    FF = ffn_in.shape[1]

    flat_parts = (mix_bias, value_bias, ffn_in_bias, rel_bias, qk_gain[:, 0], qk_gain[:, 1], qk_bias)
    flat = jnp.concatenate(flat_parts).reshape(ema_alpha.shape[0], -1)
    chan = jnp.concatenate(
        [ema_alpha, ema_delta, ema_beta, ema_eta, ema_omega[:, None], norm_gain, norm_bias, ffn_out_bias[:, None], flat],
        axis=1,
    )
    chan, o_mix, o_value, o_out, o_in, o_fout = join(chan, mix_weight, value_weight, out_weight, ffn_in, ffn_out)
    chan = gather_small(chan)
    flat = chan[:, :, 4 * H + 6 :].reshape(n_wsh, -1).astype(F32)
    chan = chan[:, :, : 4 * H + 6].reshape(D, -1).T.astype(F32)
    vectors, start = [], 0
    for part in flat_parts:
        vectors.append(flat[:, start : start + part.shape[0]].reshape(1, -1))
        start += part.shape[0]
    bm, bv, bf, rel, gain_q, gain_k, shift_q = vectors
    rate = jax.nn.sigmoid(chan[0:H])
    damp = jax.nn.sigmoid(chan[H : 2 * H])
    beta = chan[2 * H : 3 * H]
    eta = chan[3 * H : 4 * H]
    omega = chan[4 * H : 4 * H + 1]
    norms = jnp.concatenate([chan[4 * H + 1 : 4 * H + 5], jnp.zeros((4, D), F32)])
    bo = chan[4 * H + 5 : 4 * H + 6]
    qk = jnp.concatenate([gain_q, gain_k, shift_q, jnp.zeros((5, Z), F32)])
    rel_matrix = skew_matrix(jnp.roll(rel[0, ::-1], BLOCK))
    keep = 1.0 - rate * damp
    weight = eta * beta * rate
    decay = power(keep, L)
    x3 = tokens.reshape(G, L, D)
    x = tokens.reshape(T, D)
    position = i * L + jnp.arange(L, dtype=jnp.int32)
    live = (position[None, :] < lengths.reshape(G)[:, None]).astype(F32).reshape(T, 1)

    y_step, z_steps = ("seq", 1), [("seq", s) for s in seq_steps()[1:]]
    x_step = ("wsh", 2)
    sixth = D // LANES // 6
    steps = seq_steps()
    half = D // LANES // 2

    x_mix, x_value, x_out = over_x(own_half(o_mix)), over_x(own_half(o_value)), over_x(own_half(o_out))
    c_mix = over_core(o_mix)
    ends, slice_end = ema_ends(x3, keep)
    ends, slice_end, c_mix = join(ends, slice_end, c_mix)
    entry = Carry(slice_end, decay, False)
    sent, x_mix = join(entry.send(steps[0]), x_mix)
    entry.add(steps[0], sent)
    y_mix, xc_mix = over_y(x_mix), over_core(x_mix)
    for step in steps[1:]:
        entry.add(step, entry.send(step))
    state_in, x_value, xc_mix = join(entry.entry, x_value, xc_mix)
    y_value, xc_value = over_y(x_value), over_core(x_value)
    so_far = ema_forward((0, half), (), x3, keep, weight, omega, ends, state_in)
    *so_far, y_mix, x_out, xc_value, o_value, o_out, o_in, o_fout = join(
        *so_far, y_mix, x_out, xc_value, o_value, o_out, o_in, o_fout
    )
    y_out, xc_out, yc_mix = over_y(x_out), over_core(x_out), over_core(y_mix)
    x_in, x_fout = over_x(own_half(o_in)), over_x(own_half(o_fout))
    c_value, c_out = over_core(o_value), over_core(o_out)
    xp, pre, finals = ema_forward((half, half), tuple(so_far), x3, keep, weight, omega, ends, state_in)
    xp, x_in, x_fout, y_value, y_out, xc_out, yc_mix, c_value, c_out, o_in, o_fout = join(
        xp, x_in, x_fout, y_value, y_out, xc_out, yc_mix, c_value, c_out, o_in, o_fout
    )
    yc_value, yc_out = over_core(y_value), over_core(y_out)
    y_in, y_fout, xc_in, xc_fout = over_y(x_in), over_y(x_fout), over_core(x_in), over_core(x_fout)
    c_in, c_fout = over_core(o_in), over_core(o_fout)
    mix_pieces = (
        (o_mix, c_mix, x_mix, y_mix, xc_mix, yc_mix) + (o_value, c_value, x_value, y_value, xc_value, yc_value)
        + (o_out, c_out, x_out, y_out, xc_out, yc_out)
    )
    xp = xp.reshape(T, D)
    forward = mix_forward(R, x, xp, bm, bv, qk, rel_matrix, mix_pieces)
    (u, h, r, v, z, p, mixed), y_in, y_fout, xc_in, xc_fout, c_in, c_fout = join(
        forward, y_in, y_fout, xc_in, xc_fout, c_in, c_fout
    )
    ffn_pieces = (o_in, c_in, x_in, y_in, xc_in, over_core(y_in)) + (
        o_fout, c_fout, x_fout, y_fout, xc_fout, over_core(y_fout)
    )
    output, h1, act, dg, df, dum, dt, sum_d, sum_f = ffn_both(
        R, x, u, h, cotangent.reshape(T, D), live, norms, bf, bo, ffn_pieces
    )

    (sent_1, kept_1), (sent_2, kept_2) = send_core(dot_rows(act, dg)), send_core(dot_rows(h1, df))
    (sent_3, kept_3), (sent_4, kept_4) = send_core(dot_rows(mixed, dum[:, D:])), send_core(dot_rows(xp, dum))
    kept_3, kept_4, sent_1, sent_2 = join(kept_3, kept_4, sent_1, sent_2)
    sum_a = Sum(merge([add_half(sent_1, kept_1), add_half(sent_2, kept_2)], D))
    over_a = sum_a.send(x_step)
    sum_b = Sum(merge([add_half(sent_3, kept_3), add_half(sent_4, kept_4)], D))
    over_b = sum_b.send(y_step)
    back = mix_backward(R, dum, dt, r, v, z, p, qk, sum_d, sum_f, mix_pieces)
    (db, dv, dxp, dtok, early), over_a, over_b = join(back, over_a, over_b)
    sum_a.add(over_a)
    sum_b.add(over_b)
    over_a, over_b = sum_a.send(y_step), sum_b.send(x_step)
    sent_1, kept_1 = send_core(dot_rows(xp, db))
    dxp, kept_1, over_a, over_b = join(dxp, kept_1, over_a, over_b)
    sum_a.add(over_a)
    sum_b.add(over_b)
    rows_a = sum_a.value.shape[-2]
    sum_a.value = jnp.concatenate([sum_a.value, sum_b.value], axis=-2)
    over_a = sum_a.send(z_steps[0])
    dpe, back_ends, slice_start = ema_back_ends(dxp.reshape(G, L, D), pre, keep)
    dpe, back_ends, slice_start, over_a, sent_1, dv = join(dpe, back_ends, slice_start, over_a, sent_1, dv)
    sum_a.add(over_a)
    sum_c = Sum(add_half(sent_1, kept_1))
    over_a = sum_a.send(z_steps[1])
    entry = Carry(slice_start, decay, True)
    sent = entry.send(steps[0])
    sent_2, kept_2 = send_core(dot_rows(x, dv))
    kept_2, sent, over_a = join(kept_2, sent, over_a)
    over_c = sum_c.send(x_step)
    entry.add(steps[0], sent)
    sent, sent_2 = join(entry.send(steps[1]), sent_2)
    entry.add(steps[1], sent)
    sum_d_ = Sum(add_half(sent_2, kept_2))
    over_d = sum_d_.send(y_step)
    for step in steps[2:]:
        entry.add(step, entry.send(step))
    state_in = entry.entry
    consts = (dpe, x3, keep, 1.0 / keep, weight, omega, finals, back_ends, state_in, dtok.reshape(G, L, D))
    order = list(reversed(steps))

    def back_part(k, so_far):
        return ema_backward((k * sixth, sixth), tuple(so_far), *consts)

    so_far = back_part(0, ())
    *so_far, over_a, over_c = join(*so_far, over_a, over_c)
    sum_a.add(over_a)
    for mark in z_steps[2:]:
        sum_a.add(sum_a.send(mark))
    sum_c.add(over_c)
    over_c = sum_c.send(y_step)
    block = sum_a.value.astype(BF16)[None]
    more = exchange(block, "seq", order[0])
    so_far = back_part(1, so_far)
    *so_far, over_c, over_d, more = join(*so_far, over_c, over_d, more)
    sum_c.add(over_c)
    sum_d_.add(over_d)
    over_d = sum_d_.send(x_step)
    block = widen(block, more, order[0])
    more = exchange(block, "seq", order[1])
    so_far = back_part(2, so_far)
    *so_far, over_d, more = join(*so_far, over_d, more)
    sum_d_.add(over_d)
    block = widen(block, more, order[1])
    more = exchange(block, "seq", order[2])
    cols_c = sum_c.value.shape[-1]
    sum_c.value = jnp.concatenate([sum_c.value, sum_d_.value], axis=-1)
    over_c = sum_c.send(z_steps[0])
    so_far = back_part(3, so_far)
    *so_far, over_c = join(*so_far, over_c)
    sum_c.add(over_c)
    over_c = sum_c.send(z_steps[1])
    so_far = back_part(4, so_far)
    *so_far, over_c = join(*so_far, over_c)
    sum_c.add(over_c)
    for mark in z_steps[2:]:
        sum_c.add(sum_c.send(mark))
    small = sum_c.value.astype(BF16)[None]
    over_c = exchange(small, "seq", order[0])
    so_far = back_part(5, so_far)
    *so_far, over_c, more = join(*so_far, over_c, more)
    small = widen(small, over_c, order[0])
    block = widen(block, more, order[2])
    for step in order[3:]:
        block = widen(block, exchange(block, "seq", step), step)
    input_grad, s1, s3, g_omega = so_far
    over_c = exchange(small, "seq", order[1])
    g_eta = rate * beta * s1
    g_beta = rate * eta * s1
    g_alpha = eta * beta * rate * (1.0 - rate) * (s1 - damp * rate * s3)
    g_delta = -eta * beta * rate * rate * damp * (1.0 - damp) * s3
    late = jnp.concatenate([g_alpha, g_delta, g_beta, g_eta, g_omega])
    late = late.reshape(-1, n_wsh, D // n_wsh).transpose(1, 0, 2)
    sides = jnp.concatenate([early[:, k : k + D // n_wsh] for k in range(0, D, D // n_wsh)])
    late = jnp.concatenate([late, jnp.broadcast_to(sides, (n_wsh,) + sides.shape)], axis=1)
    late, over_c = join(sum_over_wsh(late), over_c)
    small = widen(small, over_c, order[1])
    over_c = exchange(small, "seq", order[2])
    late, over_c = join(sum_over_seq(late), over_c)
    small = widen(small, over_c, order[2])
    for step in order[3:]:
        small = widen(small, exchange(small, "seq", step), step)
    block, small = in_order(block), in_order(small)
    g_a, g_b = block[:, :rows_a].reshape(-1, D).astype(F32), block[:, rows_a:].reshape(-1, D).astype(F32)
    small = small.reshape(-1, small.shape[-1]).astype(F32)
    g_c, g_d = small[:, :cols_c], small[:, cols_c:]
    input_grad = input_grad.reshape(tokens.shape)

    FF = ffn_in.shape[1]
    sides = late[4 * H + 1 :].reshape(n_wsh, 16, -1)
    early = jnp.concatenate([sides[k] for k in range(n_wsh)], axis=1)
    spans = {}
    for name, start, row, col, size in sum_spots(D, Z, V, FF):
        spans[name, start] = early[row, col : col + size]

    def span_of(name):
        return jnp.concatenate([spans[key] for key in sorted(spans) if key[0] == name])

    j = lax.axis_index("wsh")
    qk_sums, row_sums = span_of("qk"), span_of("rows")
    smalls = []
    for part in (
        span_of("mix"), span_of("value"), span_of("ffn"), span_of("rel"),
        *(qk_sums[k * Z : k * Z + Z] for k in range(3)), *(row_sums[k * D : k * D + D] for k in range(5)),
    ):
        size = part.shape[0] // n_wsh
        smalls.append(lax.dynamic_slice(part, (j * size,), (size,)))
    (
        g_mix_bias, g_value_bias, g_ffn_in_bias, g_rel, g_gain_q, g_gain_k, g_shift, gain_1, gain_2, shift_1, shift_2,
        g_ffn_out_bias,
    ) = smalls
    late = late[: 4 * H + 1].T
    tall_rows, wide_rows = ffn_out.shape[0], ffn_in.shape[0]
    n_seq = lax.axis_size("seq")
    first_rows = tall_rows // n_seq

    def unmerge(merged):
        parts = merged.reshape(n_seq, -1, D)
        top = parts[:, :first_rows].reshape(tall_rows, D)
        sides = parts[:, first_rows:].reshape(n_seq, 2, wide_rows // n_seq, D)
        return top, jnp.concatenate([sides[:, k].reshape(wide_rows, D) for k in range(2)], axis=1)

    g_ffn_out, g_ffn_in = unmerge(g_a)
    g_out, g_edges = unmerge(g_b)
    g_mix = jnp.concatenate([g_edges[:, :D], g_c, g_edges[:, D:]], axis=1)
    return (
        output.reshape(tokens.shape), input_grad,
        late[:, 0:H], late[:, H : 2 * H], late[:, 2 * H : 3 * H], late[:, 3 * H : 4 * H], late[:, 4 * H],
        g_mix, g_mix_bias, g_d, g_value_bias,
        jnp.stack([g_gain_q, g_gain_k], axis=1), g_shift, g_rel, g_out,
        jnp.stack([gain_1, gain_2], axis=1), jnp.stack([shift_1, shift_2], axis=1),
        g_ffn_in, g_ffn_in_bias, g_ffn_out, g_ffn_out_bias,
    )


def solution(mesh):
    in_specs = (
        P(None, "wsh", "seq", None),
        P(None, "wsh", "seq", None),
        P(None, "wsh"),
        P("wsh", None),
        P("wsh", None),
        P("wsh", None),
        P("wsh", None),
        P("wsh"),
        P("wsh", None),
        P("wsh"),
        P("wsh", None),
        P("wsh"),
        P("wsh", None),
        P("wsh"),
        P("wsh"),
        P("wsh", None),
        P("wsh", None),
        P("wsh", None),
        P("wsh", None),
        P("wsh"),
        P("wsh", None),
        P("wsh"),
    )
    out_specs = (
        P(None, "wsh", "seq", None),
        P(None, "wsh", "seq", None),
        P("wsh", None),
        P("wsh", None),
        P("wsh", None),
        P("wsh", None),
        P("wsh"),
        P("wsh", None),
        P("wsh"),
        P("wsh", None),
        P("wsh"),
        P("wsh", None),
        P("wsh"),
        P("wsh"),
        P("wsh", None),
        P("wsh", None),
        P("wsh", None),
        P("wsh", None),
        P("wsh"),
        P("wsh", None),
        P("wsh"),
    )
    return jax.shard_map(body, mesh=mesh, in_specs=in_specs, out_specs=out_specs, check_vma=False)
```

```python
import functools

import jax
import jax.numpy as jnp
from jax import lax
from jax.experimental import pallas as pl
from jax.experimental.pallas import tpu as pltpu
from jax.sharding import PartitionSpec as P

BLOCK = 128
LANES = 128
CH = 8
PAD = 8
CHUNK = 768
STRIP = 32
EPSILON = 1e-05
VMEM_LIMIT = 62 * 1024 * 1024
F32 = jnp.float32
BF16 = jnp.bfloat16


def dot_rows(left_op, right_op):
    return jnp.einsum("ri,rj->ij", left_op, right_op, preferred_element_type=jnp.float32)


def skew_matrix(wrapped):
    lead = wrapped.shape[:-1]
    flat = jnp.tile(wrapped, (1,) * len(lead) + (BLOCK,))[..., : BLOCK * (2 * BLOCK - 1)]
    return flat.reshape(lead + (BLOCK, 2 * BLOCK - 1))[..., :BLOCK]


def power(v, n):
    k = 1
    while k < n:
        v = v * v
        k *= 2
    return v

def rows_of(scr, s, T):
    return scr[pl.ds(s, CH, stride=T+PAD), :]

def spread(scr, v, T):
    for k in range(CH):
        scr[k*(T+PAD):k*(T+PAD)+T, :] = v[k*T:(k+1)*T, :]

def collect(scr, T):
    return jnp.concatenate([scr[k*(T+PAD):k*(T+PAD)+T, :] for k in range(CH)], axis=0)

def ends_kernel(H, T, x_ref, q_ref, e_ref, s_ref, scr):
    spread(scr, x_ref[0].astype(F32), T)
    q = [jnp.broadcast_to(q_ref[h:h+1, :], (CH, LANES)) for h in range(H)]
    def step(s, st):
        xs = rows_of(scr, s, T)
        return tuple(q[h]*st[h] + xs for h in range(H))
    st = lax.fori_loop(0, T, step, tuple(jnp.zeros((CH,LANES),F32) for _ in range(H)), unroll=8)
    for h in range(H):
        e_ref[0, h*CH:(h+1)*CH, :] = st[h]
    qT = power(q_ref[...], T)
    c = jnp.zeros((H,LANES),F32)
    for k in range(CH):
        c = qT*c + e_ref[0, pl.ds(k,H,stride=CH), :]
    s_ref[0] = c

def fwd_kernel(H, T, x_ref, q_ref, w_ref, om_ref, e_ref, c_ref, *refs):
    xp_ref, p_ref, f_ref, scr, cs, ps = refs[-6:]
    spread(scr, x_ref[0].astype(F32), T)
    qT = power(q_ref[...], T)
    c = c_ref[0]
    for k in range(CH):
        cs[pl.ds(k,H,stride=CH), :] = c
        c = qT*c + e_ref[0, pl.ds(k,H,stride=CH), :]
    q = [jnp.broadcast_to(q_ref[h:h+1, :], (CH, LANES)) for h in range(H)]
    w = [jnp.broadcast_to(w_ref[h:h+1, :], (CH, LANES)) for h in range(H)]
    om = jnp.broadcast_to(om_ref[...], (CH,LANES))
    def step(s, st):
        xs = rows_of(scr, s, T)
        st = tuple(q[h]*st[h] + xs for h in range(H))
        terms = [w[h]*st[h] for h in range(H)]
        while len(terms) > 1:
            terms = [terms[i]+terms[i+1] for i in range(0,len(terms)-1,2)] + ([terms[-1]] if len(terms)%2 else [])
        ps[pl.ds(s, CH, stride=T+PAD), :] = terms[0] + om*xs
        return st
    st = lax.fori_loop(0, T, step, tuple(cs[h*CH:(h+1)*CH, :] for h in range(H)), unroll=8)
    for h in range(H):
        f_ref[0, h*CH:(h+1)*CH, :] = st[h]
    p = collect(ps, T)
    p_ref[0] = p
    xp_ref[0] = (p*jax.nn.sigmoid(p)).astype(xp_ref.dtype)

def bends_kernel(H, T, dxp_ref, p_ref, q_ref, d_ref, e_ref, s_ref, ds):
    p = p_ref[0]
    sg = jax.nn.sigmoid(p)
    d = dxp_ref[0].astype(F32) * (sg*(1.0+p*(1.0-sg)))
    d_ref[0] = d
    spread(ds, d, T)
    q = [jnp.broadcast_to(q_ref[h:h+1, :], (CH, LANES)) for h in range(H)]
    def step(s, st):
        xs = rows_of(ds, T-1-s, T)
        return tuple(q[h]*st[h] + xs for h in range(H))
    st = lax.fori_loop(0, T, step, tuple(jnp.zeros((CH,LANES),F32) for _ in range(H)), unroll=8)
    for h in range(H):
        e_ref[0, h*CH:(h+1)*CH, :] = st[h]
    qT = power(q_ref[...], T)
    c = jnp.zeros((H,LANES),F32)
    for k in reversed(range(CH)):
        c = qT*c + e_ref[0, pl.ds(k,H,stride=CH), :]
    s_ref[0] = c

def bwd_kernel(H, T, d_ref, x_ref, q_ref, qi_ref, w_ref, om_ref, f_ref, e_ref, c_ref, t_ref, k_ref, *refs):
    dx_ref, out_ref, s1_ref, s3_ref, go_ref, scr, cs, dx, ds = refs[-9:]
    g = pl.program_id(1)
    x = x_ref[0].astype(F32)
    spread(scr, x, T)
    dv = d_ref[0]
    spread(ds, dv, T)
    qT = power(q_ref[...], T)
    c = c_ref[0]
    for k in reversed(range(CH)):
        cs[pl.ds(k,H,stride=CH), :] = c
        c = qT*c + e_ref[0, pl.ds(k,H,stride=CH), :]
    om = jnp.broadcast_to(om_ref[...], (CH,LANES))
    HH = H//2
    zero = jnp.zeros((CH,LANES),F32)
    @pl.when(g==0)
    def _():
        go_ref[...] = jnp.zeros_like(go_ref)
        s1_ref[...] = jnp.zeros_like(s1_ref)
        s3_ref[...] = jnp.zeros_like(s3_ref)
    go_ref[...] += jnp.sum(dv*x, axis=0, keepdims=True)
    for half in range(2):
        hs = range(half*HH, half*HH+HH)
        q = [jnp.broadcast_to(q_ref[h:h+1, :], (CH, LANES)) for h in hs]
        qi = [jnp.broadcast_to(qi_ref[h:h+1, :], (CH, LANES)) for h in hs]
        w = [jnp.broadcast_to(w_ref[h:h+1, :], (CH, LANES)) for h in hs]
        def step(s, carry):
            l, st, a1, a3 = carry
            at = pl.ds(T-1-s, CH, stride=T+PAD)
            d = ds[at, :]
            xs = scr[at, :]
            a1 = tuple(a1[i] + d*st[i] for i in range(HH))
            l = tuple(q[i]*l[i] + d for i in range(HH))
            st = tuple((st[i]-xs)*qi[i] for i in range(HH))
            a3 = tuple(a3[i] + l[i]*st[i] for i in range(HH))
            terms = [w[i]*l[i] for i in range(HH)]
            while len(terms) > 1:
                terms = [terms[i]+terms[i+1] for i in range(0,len(terms)-1,2)]
            if half == 0:
                dx[at, :] = terms[0] + om*d
            else:
                dx[at, :] = dx[at, :] + terms[0]
            return l, st, a1, a3
        init = (tuple(cs[h*CH:(h+1)*CH,:] for h in hs), tuple(f_ref[0,h*CH:(h+1)*CH,:] for h in hs), (zero,)*HH, (zero,)*HH)
        l, st, a1, a3 = lax.fori_loop(0, T, step, init, unroll=4)
        for i,h in enumerate(hs):
            s1_ref[h:h+1,:] += jnp.sum(a1[i],axis=0,keepdims=True)
            s3_ref[h:h+1,:] += jnp.sum(a3[i],axis=0,keepdims=True)
    dx_ref[0] = (t_ref[0] + collect(dx, T).astype(dx_ref.dtype).astype(F32)).astype(dx_ref.dtype)

    @pl.when(g == pl.num_programs(1) - 1)
    def _():
        s1, s3 = s1_ref[...], s3_ref[...]
        out_ref[0:H, :] = k_ref[0:H, :] * s1 + k_ref[H : 2 * H, :] * s3
        out_ref[H : 2 * H, :] = k_ref[2 * H : 3 * H, :] * s3
        out_ref[2 * H : 3 * H, :] = k_ref[3 * H : 4 * H, :] * s1
        out_ref[3 * H : 4 * H, :] = k_ref[4 * H : 5 * H, :] * s1
        out_ref[4 * H : 4 * H + 8, :] = jnp.broadcast_to(go_ref[...], (8, LANES))


def specs(L, H, first=0):
    blk = pl.BlockSpec((1, L, LANES), lambda c, g: (g, 0, c + first))
    par = pl.BlockSpec((H, LANES), lambda c, g: (0, c + first))
    one = pl.BlockSpec((1, LANES), lambda c, g: (0, c + first))
    st = pl.BlockSpec((1, H * CH, LANES), lambda c, g: (g, 0, c + first))
    car = pl.BlockSpec((1, H, LANES), lambda c, g: (g, 0, c + first))
    return blk, par, one, st, car


def ema_ends(x, q):
    G, L, C = x.shape
    H = q.shape[0]
    blk, par, one, st, car = specs(L, H)
    return pl.pallas_call(
        functools.partial(ends_kernel, H, L // CH),
        grid=(C // LANES, G),
        in_specs=[blk, par],
        out_specs=[st, car],
        out_shape=[jax.ShapeDtypeStruct((G, H * CH, C), F32), jax.ShapeDtypeStruct((G, H, C), F32)],
        scratch_shapes=[pltpu.VMEM((L + CH * PAD, LANES), F32)],
        cost_estimate=cost_of(0, 11),
        name="ema_ends",
    )(x, q)


def ema_forward(span, so_far, x, q, w, om, e, c):
    G, L, C = x.shape
    H = q.shape[0]
    first, count = span
    blk, par, one, st, car = specs(L, H, first)
    return pl.pallas_call(
        functools.partial(fwd_kernel, H, L // CH),
        grid=(count, G),
        in_specs=[blk, par, par, one, st, car] + [pl.BlockSpec(memory_space=pl.ANY)] * len(so_far),
        out_specs=[blk, blk, st],
        out_shape=[
            jax.ShapeDtypeStruct((G, L, C), BF16), jax.ShapeDtypeStruct((G, L, C), F32),
            jax.ShapeDtypeStruct((G, H * CH, C), F32),
        ],
        scratch_shapes=[
            pltpu.VMEM((L + CH * PAD, LANES), F32), pltpu.VMEM((H * CH, LANES), F32),
            pltpu.VMEM((L + CH * PAD, LANES), F32),
        ],
        input_output_aliases={6 + k: k for k in range(len(so_far))},
        cost_estimate=cost_of(0, 3 * count),
        name="ema_forward",
    )(x, q, w, om, e, c, *so_far)


def ema_back_ends(dxp, p, q):
    G, L, C = p.shape
    H = q.shape[0]
    blk, par, one, st, car = specs(L, H)
    return pl.pallas_call(
        functools.partial(bends_kernel, H, L // CH),
        grid=(C // LANES, G),
        in_specs=[blk, blk, par],
        out_specs=[blk, st, car],
        out_shape=[
            jax.ShapeDtypeStruct((G, L, C), F32), jax.ShapeDtypeStruct((G, H * CH, C), F32),
            jax.ShapeDtypeStruct((G, H, C), F32),
        ],
        scratch_shapes=[pltpu.VMEM((L + CH * PAD, LANES), F32)],
        cost_estimate=cost_of(0, 15),
        name="ema_back_ends",
    )(dxp, p, q)


def ema_backward(span, so_far, d, x, q, qi, w, om, f, e, c, t, k):
    G, L, C = x.shape
    H = q.shape[0]
    first, count = span
    blk, par, one, st, car = specs(L, H, first)
    factors = pl.BlockSpec((5 * H, LANES), lambda c, g: (0, c + first))
    sums = pl.BlockSpec((4 * H + 8, LANES), lambda c, g: (0, c + first))
    return pl.pallas_call(
        functools.partial(bwd_kernel, H, L // CH),
        grid=(count, G),
        in_specs=[blk, blk, par, par, par, one, st, st, car, blk, factors]
        + [pl.BlockSpec(memory_space=pl.ANY)] * len(so_far),
        out_specs=[blk, sums],
        out_shape=[
            jax.ShapeDtypeStruct((G, L, C), BF16), jax.ShapeDtypeStruct((4 * H + 8, C), F32),
        ],
        scratch_shapes=[
            pltpu.VMEM((H, LANES), F32), pltpu.VMEM((H, LANES), F32), pltpu.VMEM((1, LANES), F32),
            pltpu.VMEM((L + CH * PAD, LANES), F32), pltpu.VMEM((H * CH, LANES), F32),
            pltpu.VMEM((L + CH * PAD, LANES), F32), pltpu.VMEM((L + CH * PAD, LANES), F32),
        ],
        input_output_aliases={11 + n: n for n in range(len(so_far))},
        cost_estimate=cost_of(0, 8 * count),
        name="ema_backward",
    )(d, x, q, qi, w, om, f, e, c, t, k, *so_far)


def sig(v):
    return 0.5 * jnp.tanh(0.5 * v) + 0.5


def dot_nn(left_op, right_op):
    return jnp.dot(left_op, right_op, preferred_element_type=F32)


def dot_nt(left_op, right_op):
    return lax.dot_general(left_op, right_op, (((1,), (1,)), ((), ())), preferred_element_type=F32)


def dot_tn(left_op, right_op):
    return lax.dot_general(left_op, right_op, (((0,), (0,)), ((), ())), preferred_element_type=F32)


def piece_copies(pieces, target):
    j = lax.axis_index("wsh")
    bit = lax.rem(lax.axis_index("seq"), 2)
    rows = target.shape[0] // 4
    half = rows // 2
    if len(pieces) == 4:
        starts = [(j ^ k) * rows for k in range(4)]
    else:
        low, high = bit * half, (1 - bit) * half
        starts = [j * rows, (j ^ 1) * rows]
        starts += [(j ^ 2) * rows + low, (j ^ 2) * rows + high, (j ^ 3) * rows + low, (j ^ 3) * rows + high]
    return [
        (piece, target.at[pl.ds(pl.multiple_of(start, 32), piece.shape[0]), :])
        for piece, start in zip(pieces, starts)
    ]


def bring(groups, sem):
    @pl.when(pl.program_id(0) == 0)
    def _():
        copies = []
        for pieces, target in groups:
            for source, spot in piece_copies(pieces, target):
                copies.append(pltpu.make_async_copy(source, spot, sem.at[len(copies)]))
        for copy in copies:
            copy.start()
        for copy in copies:
            copy.wait()


def fold(rows):
    total = rows[:8]
    for k in range(8, STRIP, 8):
        total = total + rows[k : k + 8]
    return total


def add_sums(ref, at, rows):
    ref[:, at] += jnp.sum(rows, axis=0, keepdims=True)


def mix_fwd_kernel(R, dims, x_ref, xp_ref, bm_ref, bv_ref, qk_ref, rel_ref, *refs):
    D, Z, V = dims
    pieces, refs = refs[:18], refs[18:]
    u_ref, h_ref, r_ref, v_ref, z_ref, p_ref, m_ref, wm, wv, wo, sem = refs
    bring(((pieces[:6], wm), (pieces[6:12], wv), (pieces[12:], wo)), sem)
    xp = xp_ref[...]
    x = x_ref[...]
    z = dot_nn(xp, wm[:, D : D + Z]) + bm_ref[:, D : D + Z]
    z_ref[...] = z
    shared = z * sig(z)
    query = (shared * qk_ref[0:1, :] + qk_ref[2:3, :]).astype(BF16)
    key = (shared * qk_ref[1:2, :]).astype(BF16)
    probs = []
    row = lax.broadcasted_iota(jnp.int32, (BLOCK, BLOCK), 0)
    col = lax.broadcasted_iota(jnp.int32, (BLOCK, BLOCK), 1)
    for b in range(R // BLOCK):
        at = slice(b * BLOCK, (b + 1) * BLOCK)
        score = dot_nt(query[at], key[at]) * Z ** (-0.5) + rel_ref[...]
        score = jnp.where(row >= col, score, -1e30)
        grown = jnp.exp(score - jnp.max(score, axis=-1, keepdims=True))
        prob = grown / jnp.sum(grown, axis=-1, keepdims=True)
        p_ref[at, :] = prob
        probs.append(prob.astype(BF16))
    for c in range(0, V, CHUNK):
        at = slice(c, c + CHUNK)
        rat = slice(D + Z + c, D + Z + c + CHUNK)
        v = dot_nn(x, wv[:, at]) + bv_ref[:, at]
        v_ref[:, at] = v
        value = (v * sig(v)).astype(BF16)
        r = dot_nn(xp, wm[:, rat]) + bm_ref[:, rat]
        r_ref[:, at] = r
        reset = r * sig(r)
        for b in range(0, R // BLOCK, 2):
            rows = slice(b * BLOCK, (b + 2) * BLOCK)
            m_ref[rows, at] = (reset[rows] * dot_nn(pair_of(probs[b], probs[b + 1]), value[rows])).astype(BF16)
    u_ref[...] = dot_nn(xp, wm[:, :D]) + bm_ref[:, :D]
    h_ref[...] = dot_nn(xp, wm[:, D + Z + V :]) + bm_ref[:, D + Z + V :] + dot_nn(m_ref[...], wo[...])


def slope_of(pre, logistic):
    return logistic * (1.0 + pre * (1.0 - logistic))


def mean_of(rows):
    return jnp.mean(rows, axis=-1, keepdims=True)


def ffn_kernel(R, dims, x_ref, u_ref, h_ref, cot_ref, live_ref, gn_ref, bf_ref, bo_ref, *refs):
    D, FF = dims
    pieces, refs = refs[:8], refs[8:]
    (
        o_ref, h1_ref, act_ref, dg_ref, df_ref, dum_ref, dt_ref, sd_ref, sf_ref,
        wi, wo, f_scr, n1_scr, a_scr, i1_scr, sem,
    ) = refs
    bring(((pieces[:4], wi), (pieces[4:], wo)), sem)

    @pl.when(pl.program_id(0) == 0)
    def _():
        sd_ref[...] = jnp.zeros_like(sd_ref)
        sf_ref[...] = jnp.zeros_like(sf_ref)

    g1, g2, b1, b2 = (gn_ref[k : k + 1, :] for k in range(4))
    part = min(256, R)

    def strips(s):
        return [slice(k, k + STRIP) for k in range(s * part, (s + 1) * part, STRIP)]

    def first(s):
        for at in strips(s):
            x = x_ref[at, :].astype(F32)
            h = h_ref[at, :]
            y = x + sig(u_ref[at, :]) * (h * sig(h) - x)
            center = y - mean_of(y)
            inverse = lax.rsqrt(mean_of(center * center) + EPSILON)
            n1 = center * inverse
            n1_scr[at, :] = n1
            i1_scr[at, :] = jnp.broadcast_to(inverse, (STRIP, LANES))
            h1_ref[at, :] = (n1 * g1 + b1).astype(BF16)

    def spread(s):
        rows = slice(s * part, (s + 1) * part)
        for c in range(0, FF, CHUNK):
            at = slice(c, c + CHUNK)
            f = dot_nn(h1_ref[rows, :], wi[:, at]) + bf_ref[:, at]
            f_scr[rows, at] = f
            act_ref[rows, at] = (f * sig(f)).astype(BF16)

    def narrow(s):
        rows = slice(s * part, (s + 1) * part)
        a_scr[rows, :] = dot_nn(act_ref[rows, :], wo[...])

    def second(s):
        zero = jnp.zeros((8, D), F32)
        s_gain, s_shift, s_bias = zero, zero, zero
        for at in strips(s):
            y2 = n1_scr[at, :] * g1 + b1 + a_scr[at, :] + bo_ref[...]
            center = y2 - mean_of(y2)
            inverse = lax.rsqrt(mean_of(center * center) + EPSILON)
            n2 = center * inverse
            live = live_ref[at, :]
            o_ref[at, :] = ((n2 * g2 + b2) * live).astype(BF16)
            dn = cot_ref[at, :].astype(F32) * live
            w = dn * g2
            dy2 = inverse * (w - mean_of(w) - n2 * mean_of(w * n2))
            a_scr[at, :] = dy2
            dg_ref[at, :] = dy2.astype(BF16)
            s_gain, s_shift, s_bias = s_gain + fold(dn * n2), s_shift + fold(dn), s_bias + fold(dy2)
        sd_ref[1:2, :] += jnp.sum(s_gain, axis=0, keepdims=True)
        sd_ref[3:4, :] += jnp.sum(s_shift, axis=0, keepdims=True)
        sd_ref[4:5, :] += jnp.sum(s_bias, axis=0, keepdims=True)

    def spread_back(s):
        rows = slice(s * part, (s + 1) * part)
        for c in range(0, FF, CHUNK):
            at = slice(c, c + CHUNK)
            f = f_scr[rows, at]
            df = (dot_nt(dg_ref[rows, :], wo[at, :]) * slope_of(f, sig(f))).astype(BF16)
            df_ref[rows, at] = df
            add_sums(sf_ref, at, df.astype(F32))

    def narrow_back(s):
        rows = slice(s * part, (s + 1) * part)
        a_scr[rows, :] += dot_nt(df_ref[rows, :], wi[...])

    def third(s):
        zero = jnp.zeros((8, D), F32)
        s_gain, s_shift = zero, zero
        for at in strips(s):
            dh1 = a_scr[at, :]
            n1 = n1_scr[at, :]
            w = dh1 * g1
            dy = i1_scr[at, 0:1] * (w - mean_of(w) - n1 * mean_of(w * n1))
            x = x_ref[at, :].astype(F32)
            h = h_ref[at, :]
            sh = sig(h)
            gate = sig(u_ref[at, :])
            rest = 1.0 - gate
            dyg = dy * gate
            dum_ref[at, :D] = (dyg * (h * sh - x) * rest).astype(BF16)
            dum_ref[at, D:] = (dyg * slope_of(h, sh)).astype(BF16)
            dt_ref[at, :] = dy * rest
            s_gain, s_shift = s_gain + fold(dh1 * n1), s_shift + fold(dh1)
        sd_ref[0:1, :] += jnp.sum(s_gain, axis=0, keepdims=True)
        sd_ref[2:3, :] += jnp.sum(s_shift, axis=0, keepdims=True)

    stages = (first, spread, narrow, second, spread_back, narrow_back, third)
    count = R // part
    for tick in range(len(stages) + count - 1):
        for s in range(count):
            if 0 <= tick - s < len(stages):
                stages[tick - s](s)


def pair_of(top, bottom):
    none = jnp.zeros_like(top)
    return jnp.concatenate([jnp.concatenate([top, none], axis=1), jnp.concatenate([none, bottom], axis=1)], axis=0)


def sum_spots(D, Z, V, FF):
    spans = [("mix", D, Z), ("rel", 0, 2 * BLOCK), ("qk", 0, 3 * Z), ("mix", 0, D), ("mix", D + Z + V, D)]
    spans += [("mix", D + Z + k, D) for k in range(0, V, D)] + [("value", k, D) for k in range(0, V, D)]
    spans += [("ffn", k, D) for k in range(0, FF, D)] + [("rows", k * D, D) for k in range(5)]
    spots, place = [], 0
    for name, start, size in spans:
        spots.append((name, start, place // D, place % D, size))
        place += size
    return spots


def mix_bwd_kernel(R, dims, dum_ref, dt_ref, r_ref, v_ref, z_ref, p_ref, qk_ref, sd_ref, sf_ref, *refs):
    D, Z, V = dims
    pieces, refs = refs[:18], refs[18:]
    db_ref, dv_ref, dxp_ref, do_ref, all_ref, sm_ref, sv_ref, sq_ref, ss_ref, wm, wv, wo, acc, sem = refs
    bring(((pieces[:6], wm), (pieces[6:12], wv), (pieces[12:], wo)), sem)

    @pl.when(pl.program_id(0) == 0)
    def _():
        for ref in (sm_ref, sv_ref, sq_ref, ss_ref):
            ref[...] = jnp.zeros_like(ref)

    last = D + Z + V
    blocks = [slice(b * BLOCK, (b + 1) * BLOCK) for b in range(R // BLOCK)]
    full = [p_ref[rows, :] for rows in blocks]
    probs = [prob.astype(BF16) for prob in full]
    pairs = [slice(k, k + 2 * BLOCK) for k in range(0, R, 2 * BLOCK)]
    double = [pair_of(probs[2 * k], probs[2 * k + 1]) for k in range(len(pairs))]
    wide = [jnp.zeros((2 * BLOCK, 2 * BLOCK), F32) for _ in pairs]
    size = 512

    def head(c):
        return dot_nt(dum_ref[:, D:], wo[c : c + size, :])

    def chunk(c, dmix):
        at = slice(c, c + size)
        rat = slice(D + Z + c, D + Z + c + size)
        zat = slice(Z + c, Z + c + size)
        sum_r = jnp.zeros((1, size), F32)
        sum_v = jnp.zeros((1, size), F32)
        for b, rows in enumerate(pairs):
            r = r_ref[rows, at]
            v = v_ref[rows, at]
            sr = sig(r)
            sv = sig(v)
            value = (v * sv).astype(BF16)
            datt = (dmix[rows] * (r * sr)).astype(BF16)
            dr = (dmix[rows] * slope_of(r, sr) * dot_nn(double[b], value)).astype(BF16)
            db_ref[rows, zat] = dr
            sum_r += jnp.sum(dr.astype(F32), axis=0, keepdims=True)
            wide[b] += dot_nt(datt, value)
            dv = (dot_tn(double[b], datt) * slope_of(v, sv)).astype(BF16)
            dv_ref[rows, at] = dv
            sum_v += jnp.sum(dv.astype(F32), axis=0, keepdims=True)
        sm_ref[:, rat] += sum_r
        sv_ref[:, at] += sum_v

    def give(c):
        at = slice(c, c + size)
        rat = slice(D + Z + c, D + Z + c + size)
        zat = slice(Z + c, Z + c + size)
        acc[...] += dot_nt(db_ref[:, zat], wm[:, rat])
        do_ref[...] += dot_nt(dv_ref[:, at], wv[:, at])

    starts = list(range(0, V, size))
    dmix = head(starts[0])
    acc[...] = dot_nt(dum_ref[:, :D], wm[:, :D]) + dot_nt(dum_ref[:, D:], wm[:, last:])
    do_ref[...] = dt_ref[...]
    chunk(starts[0], dmix)
    for n, c in enumerate(starts[1:]):
        dmix = head(c)
        give(starts[n])
        chunk(c, dmix)
    add_sums(sm_ref, slice(0, D), dum_ref[:, :D].astype(F32))
    add_sums(sm_ref, slice(last, D + last), dum_ref[:, D:].astype(F32))
    for b, rows in enumerate(blocks):
        z = z_ref[rows, :]
        sz = sig(z)
        shared = z * sz
        query = (shared * qk_ref[0:1, :] + qk_ref[2:3, :]).astype(BF16)
        key = (shared * qk_ref[1:2, :]).astype(BF16)
        side = slice(b % 2 * BLOCK, b % 2 * BLOCK + BLOCK)
        dprob = wide[b // 2][side, side]
        inner = jnp.sum(full[b] * dprob, axis=-1, keepdims=True)
        ds = (full[b] * (dprob - inner)).astype(BF16)
        ss_ref[...] += ds.astype(F32)
        dq = dot_nn(ds, key) * Z ** (-0.5)
        dk = dot_tn(ds, query) * Z ** (-0.5)
        sq_ref[0:1, :] += jnp.sum(dq * shared, axis=0, keepdims=True)
        sq_ref[1:2, :] += jnp.sum(dk * shared, axis=0, keepdims=True)
        sq_ref[2:3, :] += jnp.sum(dq, axis=0, keepdims=True)
        dz = (dq * qk_ref[0:1, :] + dk * qk_ref[1:2, :]) * slope_of(z, sz)
        dz = dz.astype(BF16)
        db_ref[rows, :Z] = dz
        add_sums(sm_ref, slice(D, D + Z), dz.astype(F32))
    give(starts[-1])
    dxp_ref[...] = (acc[...] + dot_nt(db_ref[:, :Z], wm[:, D : D + Z])).astype(BF16)

    @pl.when(pl.program_id(0) == pl.num_programs(0) - 1)
    def _():
        moved = jnp.concatenate([ss_ref[...].T, jnp.zeros((BLOCK, BLOCK), F32)], axis=1)
        row = lax.broadcasted_iota(jnp.int32, moved.shape, 0)
        step = 1
        while step < BLOCK:
            moved = jnp.where(jnp.bitwise_and(row, step) == 0, pltpu.roll(moved, step, 1), moved)
            step *= 2
        spots = sum_spots(D, Z, V, sf_ref.shape[1])
        sums = {
            "mix": sm_ref[...], "value": sv_ref[...], "ffn": sf_ref[...], "rel": jnp.sum(moved, axis=0, keepdims=True),
            "qk": jnp.concatenate([sq_ref[k : k + 1, :] for k in range(3)], axis=1),
            "rows": jnp.concatenate([sd_ref[k : k + 1, :] for k in range(5)], axis=1),
        }
        all_ref[...] = jnp.zeros_like(all_ref)
        for name, start, row, col, size in spots:
            all_ref[row : row + 1, col : col + size] = sums[name][:, start : start + size]


def cost_of(flops, microseconds):
    return pl.CostEstimate(flops=flops, bytes_accessed=microseconds * 3_600_000, transcendentals=0)


def any_specs(n):
    return [pl.BlockSpec(memory_space=pl.ANY)] * n


def tile(R, n):
    return pl.BlockSpec((R, n), lambda t: (t, 0))


def fixed(r, n):
    return pl.BlockSpec((r, n), lambda t: (0, 0))


def shape(r, n, dtype=F32):
    return jax.ShapeDtypeStruct((r, n), dtype)


def mix_forward(R, x, xp, bm, bv, qk, rel, pieces):
    T, D = x.shape
    V = bv.shape[1]
    Z = qk.shape[1]
    E = bm.shape[1]
    return pl.pallas_call(
        functools.partial(mix_fwd_kernel, R, (D, Z, V)),
        grid=(T // R,),
        in_specs=[tile(R, D), tile(R, D), fixed(1, E), fixed(1, V), fixed(8, Z), fixed(BLOCK, BLOCK)]
        + any_specs(18),
        out_specs=[tile(R, D), tile(R, D), tile(R, V), tile(R, V), tile(R, Z), tile(R, BLOCK), tile(R, V)],
        out_shape=[
            shape(T, D), shape(T, D), shape(T, V), shape(T, V), shape(T, Z), shape(T, BLOCK), shape(T, V, BF16),
        ],
        scratch_shapes=[
            pltpu.VMEM((D, E), BF16), pltpu.VMEM((D, V), BF16), pltpu.VMEM((V, D), BF16),
            pltpu.SemaphoreType.DMA((18,)),
        ],
        compiler_params=pltpu.CompilerParams(vmem_limit_bytes=VMEM_LIMIT),
        cost_estimate=cost_of(2 * T * D * (E + 2 * V), 33),
        name="mix_forward",
    )(x, xp, bm, bv, qk, rel, *pieces)


def ffn_both(R, x, u, h, cot, live, norms, bf, bo, pieces):
    T, D = x.shape
    FF = bf.shape[1]
    return pl.pallas_call(
        functools.partial(ffn_kernel, R, (D, FF)),
        grid=(T // R,),
        in_specs=[tile(R, D), tile(R, D), tile(R, D), tile(R, D), tile(R, 1), fixed(8, D), fixed(1, FF), fixed(1, D)]
        + any_specs(8),
        out_specs=[
            tile(R, D), tile(R, D), tile(R, FF), tile(R, D), tile(R, FF), tile(R, 2 * D), tile(R, D),
            fixed(8, D), fixed(1, FF),
        ],
        out_shape=[
            shape(T, D, BF16), shape(T, D, BF16), shape(T, FF, BF16), shape(T, D, BF16), shape(T, FF, BF16),
            shape(T, 2 * D, BF16), shape(T, D), shape(8, D), shape(1, FF),
        ],
        scratch_shapes=[
            pltpu.VMEM((D, FF), BF16), pltpu.VMEM((FF, D), BF16), pltpu.VMEM((R, FF), F32), pltpu.VMEM((R, D), F32),
            pltpu.VMEM((R, D), F32), pltpu.VMEM((R, 128), F32), pltpu.SemaphoreType.DMA((12,)),
        ],
        compiler_params=pltpu.CompilerParams(vmem_limit_bytes=VMEM_LIMIT),
        cost_estimate=cost_of(2 * T * D * 4 * FF, 50),
        name="ffn_both",
    )(x, u, h, cot, live, norms, bf, bo, *pieces)


def mix_backward(R, dum, dt, r, v, z, p, qk, sum_d, sum_f, pieces):
    T, D = dt.shape
    V = r.shape[1]
    Z = qk.shape[1]
    E = 2 * D + Z + V
    return pl.pallas_call(
        functools.partial(mix_bwd_kernel, R, (D, Z, V)),
        grid=(T // R,),
        in_specs=[
            tile(R, 2 * D), tile(R, D), tile(R, V), tile(R, V), tile(R, Z), tile(R, BLOCK), fixed(8, Z),
            fixed(8, D), fixed(1, sum_f.shape[1]),
        ]
        + any_specs(18),
        out_specs=[
            tile(R, Z + V), tile(R, V), tile(R, D), tile(R, D), fixed(16, D),
        ],
        out_shape=[
            shape(T, Z + V, BF16), shape(T, V, BF16), shape(T, D, BF16), shape(T, D), shape(16, D),
        ],
        scratch_shapes=[
            pltpu.VMEM((1, E), F32), pltpu.VMEM((1, V), F32), pltpu.VMEM((8, Z), F32), pltpu.VMEM((BLOCK, BLOCK), F32),
            pltpu.VMEM((D, E), BF16), pltpu.VMEM((D, V), BF16), pltpu.VMEM((V, D), BF16), pltpu.VMEM((R, D), F32),
            pltpu.SemaphoreType.DMA((18,)),
        ],
        compiler_params=pltpu.CompilerParams(vmem_limit_bytes=VMEM_LIMIT),
        cost_estimate=cost_of(2 * T * D * (E + 2 * V), 40),
        name="mix_backward",
    )(dum, dt, r, v, z, p, qk, sum_d, sum_f, *pieces)


def exchange(value, axis, step):
    return lax.ppermute(value, axis, [(k, k ^ step) for k in range(lax.axis_size(axis))])


def join(*values):
    return lax.optimization_barrier(values)


def own_half(own):
    half = own.shape[0] // 2
    return lax.dynamic_slice_in_dim(own, lax.rem(lax.axis_index("seq"), 2) * half, half, 0)


def over_x(value):
    return exchange(value, "wsh", 2)


def over_y(value):
    return exchange(value, "seq", 1)


def over_core(value):
    return exchange(value, "wsh", 1)


def gather_small(own):
    j = lax.axis_index("wsh")
    four = jnp.stack([own] + [exchange(own, "wsh", d) for d in range(1, 4)])
    return jnp.stack([lax.dynamic_index_in_dim(four, j ^ k, 0, False) for k in range(4)])


class Carry:
    def __init__(self, states, decay, reverse):
        self.entry, self.total = jnp.zeros_like(states), states
        self.own, self.window, self.reverse = jnp.ones_like(decay), decay, reverse

    def send(self, step):
        return exchange(self.total, "seq", step)

    def add(self, step, sent):
        bit = lax.rem(lax.axis_index("seq") // step, 2)
        later = (bit == 0) if self.reverse else (bit == 1)
        self.entry = jnp.where(later, self.entry + self.own * sent, self.entry)
        self.total = jnp.where(later, self.total + self.window * sent, sent + self.window * self.total)
        self.own = jnp.where(later, self.own * self.window, self.own)
        self.window = self.window * self.window


def pick(value, dim, bit):
    return lax.dynamic_index_in_dim(value, bit, dim, False)


def send_half(value, dim, mark):
    axis, step = mark
    bit = lax.rem(lax.axis_index(axis) // step, 2)
    return exchange(pick(value, dim, 1 - bit).astype(BF16), axis, step), pick(value, dim, bit)


def add_half(sent, kept):
    return kept + sent.astype(F32)


def seq_steps():
    return [2**k for k in range(lax.axis_size("seq").bit_length() - 1)]


def send_core(grad):
    rows, cols = grad.shape
    bits = (2,) * len(seq_steps())
    rest = rows // lax.axis_size("wsh") // lax.axis_size("seq")
    return send_half(grad.reshape((2, 2) + bits + (rest, cols)), 1, ("wsh", 1))


def merge(parts, cols):
    pieces = []
    for part in parts:
        for c in range(0, part.shape[-1], cols):
            pieces.append(part[..., c : c + cols])
    return jnp.concatenate(pieces, axis=-2)


class Sum:
    def __init__(self, value):
        self.value = value
        self.marks = [("wsh", 2)] + [("seq", s) for s in reversed(seq_steps())]

    def send(self, mark):
        dim = self.marks.index(mark)
        self.marks.pop(dim)
        sent, self.kept = send_half(self.value, dim, mark)
        return sent

    def add(self, sent):
        self.value = add_half(sent, self.kept)


def widen(block, other, step):
    bit = lax.rem(lax.axis_index("seq") // step, 2)
    first = jnp.where(bit == 0, block, other)
    second = jnp.where(bit == 0, other, block)
    return jnp.concatenate([first, second], axis=0)


def in_order(block):
    bits = block.shape[0].bit_length() - 1
    split = block.reshape((2,) * bits + block.shape[1:])
    turned = split.transpose(tuple(reversed(range(bits))) + (bits, bits + 1))
    return turned.reshape(block.shape)


def sum_over_wsh(value):
    j = lax.axis_index("wsh")
    total = lax.dynamic_index_in_dim(value, j, 0, False)
    for d in range(1, 4):
        total = total + exchange(lax.dynamic_index_in_dim(value, j ^ d, 0, False), "wsh", d)
    return total


def sum_over_seq(total):
    for step in reversed(seq_steps()):
        total = total + exchange(total, "seq", step)
    return total


def body(
    tokens, cotangent, lengths, ema_alpha, ema_delta, ema_beta, ema_eta, ema_omega, mix_weight, mix_bias,
    value_weight, value_bias, qk_gain, qk_bias, rel_bias, out_weight, norm_gain, norm_bias, ffn_in, ffn_in_bias,
    ffn_out, ffn_out_bias,
):
    micro, seqs, L, D = tokens.shape
    G = micro * seqs
    T = G * L
    H = ema_alpha.shape[1]
    R = min(512, T)
    n_wsh = lax.axis_size("wsh")
    i = lax.axis_index("seq")
    Z = qk_gain.shape[0] * n_wsh
    V = value_weight.shape[1]
    FF = ffn_in.shape[1]

    flat_parts = (mix_bias, value_bias, ffn_in_bias, rel_bias, qk_gain[:, 0], qk_gain[:, 1], qk_bias)
    flat = jnp.concatenate(flat_parts).reshape(ema_alpha.shape[0], -1)
    chan = jnp.concatenate(
        [ema_alpha, ema_delta, ema_beta, ema_eta, ema_omega[:, None], norm_gain, norm_bias, ffn_out_bias[:, None], flat],
        axis=1,
    )
    chan, o_mix, o_value, o_out, o_in, o_fout = join(chan, mix_weight, value_weight, out_weight, ffn_in, ffn_out)
    chan = gather_small(chan)
    flat = chan[:, :, 4 * H + 6 :].reshape(n_wsh, -1).astype(F32)
    chan = chan[:, :, : 4 * H + 6].reshape(D, -1).T.astype(F32)
    rate = jax.nn.sigmoid(chan[0:H])
    damp = jax.nn.sigmoid(chan[H : 2 * H])
    beta = chan[2 * H : 3 * H]
    eta = chan[3 * H : 4 * H]
    omega = chan[4 * H : 4 * H + 1]
    keep = 1.0 - rate * damp
    weight = eta * beta * rate
    decay = power(keep, L)
    inward = eta * beta * rate
    x3 = tokens.reshape(G, L, D)
    x = tokens.reshape(T, D)
    y_step, z_steps = ("seq", 1), [("seq", s) for s in seq_steps()[1:]]
    x_step = ("wsh", 2)
    sixth = D // LANES // 6
    steps = seq_steps()
    half = D // LANES // 2

    x_mix = over_x(own_half(o_mix))
    c_mix, c_value = over_core(o_mix), over_core(o_value)
    ends, slice_end = ema_ends(x3, keep)
    ends, slice_end, c_mix, c_value, o_value, o_out = join(ends, slice_end, c_mix, c_value, o_value, o_out)
    x_value, x_out = over_x(own_half(o_value)), over_x(own_half(o_out))
    entry = Carry(slice_end, decay, False)
    sent, x_mix, chan, flat, rate, damp, inward, keep_later, lengths = join(
        entry.send(steps[0]), x_mix, chan, flat, rate, damp, inward, keep, lengths
    )
    vectors, start = [], 0
    for part in flat_parts:
        vectors.append(flat[:, start : start + part.shape[0]].reshape(1, -1))
        start += part.shape[0]
    bm, bv, bf, rel, gain_q, gain_k, shift_q = vectors
    norms = jnp.concatenate([chan[4 * H + 1 : 4 * H + 5], jnp.zeros((4, D), F32)])
    bo = chan[4 * H + 5 : 4 * H + 6]
    qk = jnp.concatenate([gain_q, gain_k, shift_q, jnp.zeros((5, Z), F32)])
    rel_matrix = skew_matrix(jnp.roll(rel[0, ::-1], BLOCK))
    inverse = 1.0 / keep_later
    factors = jnp.concatenate(
        [
            inward * (1.0 - rate), -inward * (1.0 - rate) * damp * rate, -inward * rate * damp * (1.0 - damp),
            rate * eta, rate * beta,
        ]
    )
    position = i * L + jnp.arange(L, dtype=jnp.int32)
    live = (position[None, :] < lengths.reshape(G)[:, None]).astype(F32).reshape(T, 1)
    entry.add(steps[0], sent)
    y_mix, xc_mix = over_y(x_mix), over_core(x_mix)
    for step in steps[1:]:
        entry.add(step, entry.send(step))
    state_in, x_value, xc_mix, rel_matrix, norms, bo, qk, inverse, factors, live, bm = join(
        entry.entry, x_value, xc_mix, rel_matrix, norms, bo, qk, inverse, factors, live, bm
    )
    y_value, xc_value = over_y(x_value), over_core(x_value)
    so_far = ema_forward((0, half), (), x3, keep, weight, omega, ends, state_in)
    *so_far, y_mix, x_out, xc_value, o_out, o_in, o_fout = join(*so_far, y_mix, x_out, xc_value, o_out, o_in, o_fout)
    y_out, xc_out, yc_mix = over_y(x_out), over_core(x_out), over_core(y_mix)
    c_out = over_core(o_out)
    x_in = over_x(o_in)
    xp, pre, finals = ema_forward((half, half), tuple(so_far), x3, keep, weight, omega, ends, state_in)
    xp, y_value, y_out, xc_out, yc_mix, c_out, o_fout = join(xp, y_value, y_out, xc_out, yc_mix, c_out, o_fout)
    yc_value, yc_out = over_core(y_value), over_core(y_out)
    x_fout = over_x(o_fout)
    mix_pieces = (
        (o_mix, c_mix, x_mix, y_mix, xc_mix, yc_mix) + (o_value, c_value, x_value, y_value, xc_value, yc_value)
        + (o_out, c_out, x_out, y_out, xc_out, yc_out)
    )
    c_in, c_fout = over_core(o_in), over_core(o_fout)
    xp = xp.reshape(T, D)
    forward = mix_forward(min(256, T), x, xp, bm, bv, qk, rel_matrix, mix_pieces)
    (u, h, r, v, z, p, mixed), x_in, x_fout, c_in, c_fout = join(forward, x_in, x_fout, c_in, c_fout)
    ffn_pieces = (o_in, c_in, x_in, over_core(x_in)) + (o_fout, c_fout, x_fout, over_core(x_fout))
    output, h1, act, dg, df, dum, dt, sum_d, sum_f = ffn_both(
        R, x, u, h, cotangent.reshape(T, D), live, norms, bf, bo, ffn_pieces
    )

    (sent_1, kept_1), (sent_2, kept_2) = send_core(dot_rows(act, dg)), send_core(dot_rows(h1, df))
    (sent_3, kept_3), (sent_4, kept_4) = send_core(dot_rows(mixed, dum[:, D:])), send_core(dot_rows(xp, dum))
    kept_3, kept_4, sent_1, sent_2 = join(kept_3, kept_4, sent_1, sent_2)
    sum_a = Sum(merge([add_half(sent_1, kept_1), add_half(sent_2, kept_2)], D))
    over_a = sum_a.send(x_step)
    sum_b = Sum(merge([add_half(sent_3, kept_3), add_half(sent_4, kept_4)], D))
    over_b = sum_b.send(y_step)
    back = mix_backward(min(256, T), dum, dt, r, v, z, p, qk, sum_d, sum_f, mix_pieces)
    (db, dv, dxp, dtok, early), over_a, over_b = join(back, over_a, over_b)
    sum_a.add(over_a)
    sum_b.add(over_b)
    over_a, over_b = sum_a.send(y_step), sum_b.send(x_step)
    sent_1, kept_1 = send_core(dot_rows(xp, db))
    dxp, kept_1, over_a, over_b = join(dxp, kept_1, over_a, over_b)
    sum_a.add(over_a)
    sum_b.add(over_b)
    rows_a = sum_a.value.shape[-2]
    sum_a.value = jnp.concatenate([sum_a.value, sum_b.value], axis=-2)
    over_a = sum_a.send(z_steps[0])
    dpe, back_ends, slice_start = ema_back_ends(dxp.reshape(G, L, D), pre, keep)
    dpe, back_ends, slice_start, over_a, sent_1, dv = join(dpe, back_ends, slice_start, over_a, sent_1, dv)
    sum_a.add(over_a)
    sum_c = Sum(add_half(sent_1, kept_1))
    over_a = sum_a.send(z_steps[1])
    entry = Carry(slice_start, decay, True)
    sent = entry.send(steps[0])
    sent_2, kept_2 = send_core(dot_rows(x, dv))
    kept_2, sent, over_a = join(kept_2, sent, over_a)
    over_c = sum_c.send(x_step)
    entry.add(steps[0], sent)
    sent, sent_2 = join(entry.send(steps[1]), sent_2)
    entry.add(steps[1], sent)
    sum_d_ = Sum(add_half(sent_2, kept_2))
    over_d = sum_d_.send(y_step)
    for step in steps[2:]:
        entry.add(step, entry.send(step))
    state_in = entry.entry
    consts = (dpe, x3, keep, inverse, weight, omega, finals, back_ends, state_in, dtok.reshape(G, L, D), factors)
    order = list(reversed(steps))

    def back_part(k, so_far):
        return ema_backward((k * sixth, sixth), tuple(so_far), *consts)

    so_far = back_part(0, ())
    *so_far, over_a, over_c = join(*so_far, over_a, over_c)
    sum_a.add(over_a)
    for mark in z_steps[2:]:
        sum_a.add(sum_a.send(mark))
    sum_c.add(over_c)
    over_c = sum_c.send(y_step)
    block = sum_a.value.astype(BF16)[None]
    more = exchange(block, "seq", order[0])
    so_far = back_part(1, so_far)
    *so_far, over_c, over_d, more = join(*so_far, over_c, over_d, more)
    sum_c.add(over_c)
    sum_d_.add(over_d)
    over_d = sum_d_.send(x_step)
    block = widen(block, more, order[0])
    more = exchange(block, "seq", order[1])
    so_far = back_part(2, so_far)
    *so_far, over_d, more = join(*so_far, over_d, more)
    sum_d_.add(over_d)
    block = widen(block, more, order[1])
    more = exchange(block, "seq", order[2])
    cols_c = sum_c.value.shape[-1]
    sum_c.value = jnp.concatenate([sum_c.value, sum_d_.value], axis=-1)
    over_c = sum_c.send(z_steps[0])
    so_far = back_part(3, so_far)
    *so_far, over_c = join(*so_far, over_c)
    sum_c.add(over_c)
    over_c = sum_c.send(z_steps[1])
    so_far = back_part(4, so_far)
    *so_far, over_c = join(*so_far, over_c)
    sum_c.add(over_c)
    for mark in z_steps[2:]:
        sum_c.add(sum_c.send(mark))
    small = sum_c.value.astype(BF16)[None]
    over_c = exchange(small, "seq", order[0])
    so_far = back_part(5, so_far)
    *so_far, over_c, more = join(*so_far, over_c, more)
    small = widen(small, over_c, order[0])
    block = widen(block, more, order[2])
    for step in order[3:]:
        block = widen(block, exchange(block, "seq", step), step)
    input_grad, late = so_far
    over_c = exchange(small, "seq", order[1])
    late = late.reshape(-1, n_wsh, D // n_wsh).transpose(1, 0, 2)
    sides = jnp.concatenate([early[:, k : k + D // n_wsh] for k in range(0, D, D // n_wsh)])
    late = jnp.concatenate([late, jnp.broadcast_to(sides, (n_wsh,) + sides.shape)], axis=1)
    late, over_c = join(sum_over_wsh(late), over_c)
    small = widen(small, over_c, order[1])
    over_c = exchange(small, "seq", order[2])
    late, over_c = join(sum_over_seq(late), over_c)
    small = widen(small, over_c, order[2])
    for step in order[3:]:
        small = widen(small, exchange(small, "seq", step), step)
    block, small = in_order(block), in_order(small)
    g_a, g_b = block[:, :rows_a].reshape(-1, D).astype(F32), block[:, rows_a:].reshape(-1, D).astype(F32)
    small = small.reshape(-1, small.shape[-1]).astype(F32)
    g_c, g_d = small[:, :cols_c], small[:, cols_c:]
    input_grad = input_grad.reshape(tokens.shape)

    FF = ffn_in.shape[1]
    sides = late[4 * H + 8 :].reshape(n_wsh, 16, -1)
    early = jnp.concatenate([sides[k] for k in range(n_wsh)], axis=1)
    spans = {}
    for name, start, row, col, size in sum_spots(D, Z, V, FF):
        spans[name, start] = early[row, col : col + size]

    def span_of(name):
        return jnp.concatenate([spans[key] for key in sorted(spans) if key[0] == name])

    j = lax.axis_index("wsh")
    qk_sums, row_sums = span_of("qk"), span_of("rows")
    smalls = []
    for part in (
        span_of("mix"), span_of("value"), span_of("ffn"), span_of("rel"),
        *(qk_sums[k * Z : k * Z + Z] for k in range(3)), *(row_sums[k * D : k * D + D] for k in range(5)),
    ):
        size = part.shape[0] // n_wsh
        smalls.append(lax.dynamic_slice(part, (j * size,), (size,)))
    (
        g_mix_bias, g_value_bias, g_ffn_in_bias, g_rel, g_gain_q, g_gain_k, g_shift, gain_1, gain_2, shift_1, shift_2,
        g_ffn_out_bias,
    ) = smalls
    late = late[: 4 * H + 1].T
    tall_rows, wide_rows = ffn_out.shape[0], ffn_in.shape[0]
    n_seq = lax.axis_size("seq")
    first_rows = tall_rows // n_seq

    def unmerge(merged):
        parts = merged.reshape(n_seq, -1, D)
        top = parts[:, :first_rows].reshape(tall_rows, D)
        sides = parts[:, first_rows:].reshape(n_seq, 2, wide_rows // n_seq, D)
        return top, jnp.concatenate([sides[:, k].reshape(wide_rows, D) for k in range(2)], axis=1)

    g_ffn_out, g_ffn_in = unmerge(g_a)
    g_out, g_edges = unmerge(g_b)
    g_mix = jnp.concatenate([g_edges[:, :D], g_c, g_edges[:, D:]], axis=1)
    return (
        output.reshape(tokens.shape), input_grad,
        late[:, 0:H], late[:, H : 2 * H], late[:, 2 * H : 3 * H], late[:, 3 * H : 4 * H], late[:, 4 * H],
        g_mix, g_mix_bias, g_d, g_value_bias,
        jnp.stack([g_gain_q, g_gain_k], axis=1), g_shift, g_rel, g_out,
        jnp.stack([gain_1, gain_2], axis=1), jnp.stack([shift_1, shift_2], axis=1),
        g_ffn_in, g_ffn_in_bias, g_ffn_out, g_ffn_out_bias,
    )


def solution(mesh):
    in_specs = (
        P(None, "wsh", "seq", None),
        P(None, "wsh", "seq", None),
        P(None, "wsh"),
        P("wsh", None),
        P("wsh", None),
        P("wsh", None),
        P("wsh", None),
        P("wsh"),
        P("wsh", None),
        P("wsh"),
        P("wsh", None),
        P("wsh"),
        P("wsh", None),
        P("wsh"),
        P("wsh"),
        P("wsh", None),
        P("wsh", None),
        P("wsh", None),
        P("wsh", None),
        P("wsh"),
        P("wsh", None),
        P("wsh"),
    )
    out_specs = (
        P(None, "wsh", "seq", None),
        P(None, "wsh", "seq", None),
        P("wsh", None),
        P("wsh", None),
        P("wsh", None),
        P("wsh", None),
        P("wsh"),
        P("wsh", None),
        P("wsh"),
        P("wsh", None),
        P("wsh"),
        P("wsh", None),
        P("wsh"),
        P("wsh"),
        P("wsh", None),
        P("wsh", None),
        P("wsh", None),
        P("wsh", None),
        P("wsh"),
        P("wsh", None),
        P("wsh"),
    )
    return jax.shard_map(body, mesh=mesh, in_specs=in_specs, out_specs=out_specs, check_vma=False)
```

```python
import functools

import jax
import jax.numpy as jnp
from jax import lax
from jax.experimental import pallas as pl
from jax.experimental.pallas import tpu as pltpu
from jax.sharding import PartitionSpec as P

BLOCK = 128
LANES = 128
CH = 8
PAD = 1
CHUNK = 768
STRIP = 32
EPSILON = 1e-05
VMEM_LIMIT = 62 * 1024 * 1024
F32 = jnp.float32
BF16 = jnp.bfloat16


def dot_rows(left_op, right_op):
    return jnp.einsum("ri,rj->ij", left_op, right_op, preferred_element_type=jnp.float32)


def skew_matrix(wrapped):
    lead = wrapped.shape[:-1]
    flat = jnp.tile(wrapped, (1,) * len(lead) + (BLOCK,))[..., : BLOCK * (2 * BLOCK - 1)]
    return flat.reshape(lead + (BLOCK, 2 * BLOCK - 1))[..., :BLOCK]


def power(v, n):
    k = 1
    while k < n:
        v = v * v
        k *= 2
    return v

def rows_of(scr, s, T):
    return scr[pl.ds(s, CH, stride=T+PAD), :]

def spread(scr, v, T):
    for k in range(CH):
        scr[k*(T+PAD):k*(T+PAD)+T, :] = v[k*T:(k+1)*T, :]

def collect(scr, T):
    return jnp.concatenate([scr[k*(T+PAD):k*(T+PAD)+T, :] for k in range(CH)], axis=0)

def ends_kernel(G, H, T, x_ref, q_ref, e_ref, s_ref, *scrs):
    for g in range(G):
        spread(scrs[g], x_ref[g].astype(F32), T)
    chunk_ends(G, H, T, q_ref, e_ref, s_ref, scrs, False)


def chunk_ends(G, H, T, q_ref, e_ref, s_ref, scrs, reverse):
    q = [jnp.broadcast_to(q_ref[h:h+1, :], (CH, LANES)) for h in range(H)]

    def step(s, states):
        rows = [rows_of(scr, T - 1 - s if reverse else s, T) for scr in scrs]
        return tuple(q[n % H] * states[n] + rows[n // H] for n in range(G * H))

    zero = jnp.zeros((CH, LANES), F32)
    states = lax.fori_loop(0, T, step, (zero,) * (G * H), unroll=min(T, 16))
    for n in range(G * H):
        e_ref[n // H, n % H * CH : (n % H + 1) * CH, :] = states[n]
    qT = power(q_ref[...], T)
    for g in range(G):
        c = jnp.zeros((H, LANES), F32)
        for k in reversed(range(CH)) if reverse else range(CH):
            c = qT * c + e_ref[g, pl.ds(k, H, stride=CH), :]
        s_ref[g] = c


def fwd_kernel(H, T, x_ref, q_ref, w_ref, om_ref, e_ref, c_ref, *refs):
    xp_ref, p_ref, f_ref, scr, cs, ps = refs[-6:]
    spread(scr, x_ref[0].astype(F32), T)
    qT = power(q_ref[...], T)
    c = c_ref[0]
    for k in range(CH):
        cs[pl.ds(k,H,stride=CH), :] = c
        c = qT*c + e_ref[0, pl.ds(k,H,stride=CH), :]
    q = [jnp.broadcast_to(q_ref[h:h+1, :], (CH, LANES)) for h in range(H)]
    w = [jnp.broadcast_to(w_ref[h:h+1, :], (CH, LANES)) for h in range(H)]
    om = jnp.broadcast_to(om_ref[...], (CH,LANES))
    def step(s, st):
        xs = rows_of(scr, s, T)
        st = tuple(q[h]*st[h] + xs for h in range(H))
        terms = [w[h]*st[h] for h in range(H)]
        while len(terms) > 1:
            terms = [terms[i]+terms[i+1] for i in range(0,len(terms)-1,2)] + ([terms[-1]] if len(terms)%2 else [])
        ps[pl.ds(s, CH, stride=T+PAD), :] = terms[0] + om*xs
        return st
    st = lax.fori_loop(0, T, step, tuple(cs[h*CH:(h+1)*CH, :] for h in range(H)), unroll=min(T, 32))
    for h in range(H):
        f_ref[0, h*CH:(h+1)*CH, :] = st[h]
    p = collect(ps, T)
    p_ref[0] = p
    xp_ref[0] = (p*jax.nn.sigmoid(p)).astype(xp_ref.dtype)

def bends_kernel(G, H, T, dxp_ref, p_ref, q_ref, d_ref, e_ref, s_ref, *scrs):
    for g in range(G):
        p = p_ref[g]
        sg = jax.nn.sigmoid(p)
        d = dxp_ref[g].astype(F32) * (sg*(1.0+p*(1.0-sg)))
        d_ref[g] = d
        spread(scrs[g], d, T)
    chunk_ends(G, H, T, q_ref, e_ref, s_ref, scrs, True)


def bwd_kernel(H, T, d_ref, x_ref, q_ref, qi_ref, w_ref, om_ref, f_ref, e_ref, c_ref, t_ref, k_ref, *refs):
    dx_ref, out_ref, s1_ref, s3_ref, go_ref, scr, cs, dx, ds = refs[-9:]
    g = pl.program_id(1)
    x = x_ref[0].astype(F32)
    spread(scr, x, T)
    dv = d_ref[0]
    spread(ds, dv, T)
    qT = power(q_ref[...], T)
    c = c_ref[0]
    for k in reversed(range(CH)):
        cs[pl.ds(k,H,stride=CH), :] = c
        c = qT*c + e_ref[0, pl.ds(k,H,stride=CH), :]
    om = jnp.broadcast_to(om_ref[...], (CH,LANES))
    HH = H//2
    zero = jnp.zeros((CH,LANES),F32)
    @pl.when(g==0)
    def _():
        go_ref[...] = jnp.zeros_like(go_ref)
        s1_ref[...] = jnp.zeros_like(s1_ref)
        s3_ref[...] = jnp.zeros_like(s3_ref)
    go_ref[...] += jnp.sum(dv*x, axis=0, keepdims=True)
    for half in range(2):
        hs = range(half*HH, half*HH+HH)
        q = [jnp.broadcast_to(q_ref[h:h+1, :], (CH, LANES)) for h in hs]
        qi = [jnp.broadcast_to(qi_ref[h:h+1, :], (CH, LANES)) for h in hs]
        w = [jnp.broadcast_to(w_ref[h:h+1, :], (CH, LANES)) for h in hs]
        def step(s, carry):
            l, st, a1, a3 = carry
            at = pl.ds(T-1-s, CH, stride=T+PAD)
            d = ds[at, :]
            xs = scr[at, :]
            a1 = tuple(a1[i] + d*st[i] for i in range(HH))
            l = tuple(q[i]*l[i] + d for i in range(HH))
            st = tuple((st[i]-xs)*qi[i] for i in range(HH))
            a3 = tuple(a3[i] + l[i]*st[i] for i in range(HH))
            terms = [w[i]*l[i] for i in range(HH)]
            while len(terms) > 1:
                terms = [terms[i]+terms[i+1] for i in range(0,len(terms)-1,2)]
            if half == 0:
                dx[at, :] = terms[0] + om*d
            else:
                dx[at, :] = dx[at, :] + terms[0]
            return l, st, a1, a3
        init = (tuple(cs[h*CH:(h+1)*CH,:] for h in hs), tuple(f_ref[0,h*CH:(h+1)*CH,:] for h in hs), (zero,)*HH, (zero,)*HH)
        l, st, a1, a3 = lax.fori_loop(0, T, step, init, unroll=min(T, 16))
        for i,h in enumerate(hs):
            s1_ref[h:h+1,:] += jnp.sum(a1[i],axis=0,keepdims=True)
            s3_ref[h:h+1,:] += jnp.sum(a3[i],axis=0,keepdims=True)
    dx_ref[0] = (t_ref[0] + collect(dx, T).astype(dx_ref.dtype).astype(F32)).astype(dx_ref.dtype)

    @pl.when(g == pl.num_programs(1) - 1)
    def _():
        s1, s3 = s1_ref[...], s3_ref[...]
        out_ref[0:H, :] = k_ref[0:H, :] * s1 + k_ref[H : 2 * H, :] * s3
        out_ref[H : 2 * H, :] = k_ref[2 * H : 3 * H, :] * s3
        out_ref[2 * H : 3 * H, :] = k_ref[3 * H : 4 * H, :] * s1
        out_ref[3 * H : 4 * H, :] = k_ref[4 * H : 5 * H, :] * s1
        out_ref[4 * H : 4 * H + 8, :] = jnp.broadcast_to(go_ref[...], (8, LANES))


def specs(L, H, first=0):
    blk = pl.BlockSpec((1, L, LANES), lambda c, g: (g, 0, c + first))
    par = pl.BlockSpec((H, LANES), lambda c, g: (0, c + first))
    one = pl.BlockSpec((1, LANES), lambda c, g: (0, c + first))
    st = pl.BlockSpec((1, H * CH, LANES), lambda c, g: (g, 0, c + first))
    car = pl.BlockSpec((1, H, LANES), lambda c, g: (g, 0, c + first))
    return blk, par, one, st, car


def all_specs(G, L, H):
    blk = pl.BlockSpec((G, L, LANES), lambda c: (0, 0, c))
    par = pl.BlockSpec((H, LANES), lambda c: (0, c))
    st = pl.BlockSpec((G, H * CH, LANES), lambda c: (0, 0, c))
    car = pl.BlockSpec((G, H, LANES), lambda c: (0, 0, c))
    return blk, par, st, car


def ema_ends(x, q):
    G, L, C = x.shape
    H = q.shape[0]
    blk, par, st, car = all_specs(G, L, H)
    return pl.pallas_call(
        functools.partial(ends_kernel, G, H, L // CH),
        grid=(C // LANES,),
        in_specs=[blk, par],
        out_specs=[st, car],
        out_shape=[jax.ShapeDtypeStruct((G, H * CH, C), F32), jax.ShapeDtypeStruct((G, H, C), F32)],
        scratch_shapes=[pltpu.VMEM((L + CH * PAD, LANES), F32)] * G,
        cost_estimate=cost_of(0, 11),
        name="ema_ends",
    )(x, q)


def ema_forward(span, so_far, x, q, w, om, e, c):
    G, L, C = x.shape
    H = q.shape[0]
    first, count = span
    blk, par, one, st, car = specs(L, H, first)
    return pl.pallas_call(
        functools.partial(fwd_kernel, H, L // CH),
        grid=(count, G),
        in_specs=[blk, par, par, one, st, car] + [pl.BlockSpec(memory_space=pl.ANY)] * len(so_far),
        out_specs=[blk, blk, st],
        out_shape=[
            jax.ShapeDtypeStruct((G, L, C), BF16), jax.ShapeDtypeStruct((G, L, C), F32),
            jax.ShapeDtypeStruct((G, H * CH, C), F32),
        ],
        scratch_shapes=[
            pltpu.VMEM((L + CH * PAD, LANES), F32), pltpu.VMEM((H * CH, LANES), F32),
            pltpu.VMEM((L + CH * PAD, LANES), F32),
        ],
        input_output_aliases={6 + k: k for k in range(len(so_far))},
        cost_estimate=cost_of(0, 3 * count),
        name="ema_forward",
    )(x, q, w, om, e, c, *so_far)


def ema_back_ends(dxp, p, q):
    G, L, C = p.shape
    H = q.shape[0]
    blk, par, st, car = all_specs(G, L, H)
    return pl.pallas_call(
        functools.partial(bends_kernel, G, H, L // CH),
        grid=(C // LANES,),
        in_specs=[blk, blk, par],
        out_specs=[blk, st, car],
        out_shape=[
            jax.ShapeDtypeStruct((G, L, C), F32), jax.ShapeDtypeStruct((G, H * CH, C), F32),
            jax.ShapeDtypeStruct((G, H, C), F32),
        ],
        scratch_shapes=[pltpu.VMEM((L + CH * PAD, LANES), F32)] * G,
        cost_estimate=cost_of(0, 15),
        name="ema_back_ends",
    )(dxp, p, q)


def ema_backward(span, so_far, d, x, q, qi, w, om, f, e, c, t, k):
    G, L, C = x.shape
    H = q.shape[0]
    first, count = span
    blk, par, one, st, car = specs(L, H, first)
    factors = pl.BlockSpec((5 * H, LANES), lambda c, g: (0, c + first))
    sums = pl.BlockSpec((4 * H + 8, LANES), lambda c, g: (0, c + first))
    return pl.pallas_call(
        functools.partial(bwd_kernel, H, L // CH),
        grid=(count, G),
        in_specs=[blk, blk, par, par, par, one, st, st, car, blk, factors]
        + [pl.BlockSpec(memory_space=pl.ANY)] * len(so_far),
        out_specs=[blk, sums],
        out_shape=[
            jax.ShapeDtypeStruct((G, L, C), BF16), jax.ShapeDtypeStruct((4 * H + 8, C), F32),
        ],
        scratch_shapes=[
            pltpu.VMEM((H, LANES), F32), pltpu.VMEM((H, LANES), F32), pltpu.VMEM((1, LANES), F32),
            pltpu.VMEM((L + CH * PAD, LANES), F32), pltpu.VMEM((H * CH, LANES), F32),
            pltpu.VMEM((L + CH * PAD, LANES), F32), pltpu.VMEM((L + CH * PAD, LANES), F32),
        ],
        input_output_aliases={11 + n: n for n in range(len(so_far))},
        cost_estimate=cost_of(0, 8 * count),
        name="ema_backward",
    )(d, x, q, qi, w, om, f, e, c, t, k, *so_far)


def sig(v):
    return 0.5 * jnp.tanh(0.5 * v) + 0.5


def dot_nn(left_op, right_op):
    return jnp.dot(left_op, right_op, preferred_element_type=F32)


def dot_nt(left_op, right_op):
    return lax.dot_general(left_op, right_op, (((1,), (1,)), ((), ())), preferred_element_type=F32)


def dot_tn(left_op, right_op):
    return lax.dot_general(left_op, right_op, (((0,), (0,)), ((), ())), preferred_element_type=F32)


def piece_copies(pieces, target):
    j = lax.axis_index("wsh")
    bit = lax.rem(lax.axis_index("seq"), 2)
    rows = target.shape[0] // 4
    half = rows // 2
    if len(pieces) == 4:
        starts = [(j ^ k) * rows for k in range(4)]
    else:
        low, high = bit * half, (1 - bit) * half
        starts = [j * rows, (j ^ 1) * rows]
        starts += [(j ^ 2) * rows + low, (j ^ 2) * rows + high, (j ^ 3) * rows + low, (j ^ 3) * rows + high]
    return [
        (piece, target.at[pl.ds(pl.multiple_of(start, 32), piece.shape[0]), :])
        for piece, start in zip(pieces, starts)
    ]


def bring(groups, sem):
    @pl.when(pl.program_id(0) == 0)
    def _():
        copies = []
        for pieces, target in groups:
            for source, spot in piece_copies(pieces, target):
                copies.append(pltpu.make_async_copy(source, spot, sem.at[len(copies)]))
        for copy in copies:
            copy.start()
        for copy in copies:
            copy.wait()


def fold(rows):
    total = rows[:8]
    for k in range(8, STRIP, 8):
        total = total + rows[k : k + 8]
    return total


def add_sums(ref, at, rows):
    ref[:, at] += jnp.sum(rows, axis=0, keepdims=True)


def mix_fwd_kernel(R, dims, x_ref, xp_ref, bm_ref, bv_ref, qk_ref, rel_ref, *refs):
    D, Z, V = dims
    pieces, refs = refs[:18], refs[18:]
    u_ref, h_ref, r_ref, v_ref, z_ref, p_ref, m_ref, xt_ref, wm, wv, wo, sem = refs
    bring(((pieces[:6], wm), (pieces[6:12], wv), (pieces[12:], wo)), sem)
    xp = xp_ref[...]
    x = x_ref[...]
    xt_ref[...] = xp.T
    z = dot_nn(xp, wm[:, D : D + Z]) + bm_ref[:, D : D + Z]
    z_ref[...] = z
    shared = z * sig(z)
    query = (shared * qk_ref[0:1, :] + qk_ref[2:3, :]).astype(BF16)
    key = (shared * qk_ref[1:2, :]).astype(BF16)
    probs = []
    row = lax.broadcasted_iota(jnp.int32, (BLOCK, BLOCK), 0)
    col = lax.broadcasted_iota(jnp.int32, (BLOCK, BLOCK), 1)
    for b in range(R // BLOCK):
        at = slice(b * BLOCK, (b + 1) * BLOCK)
        score = dot_nt(query[at], key[at]) * Z ** (-0.5) + rel_ref[...]
        score = jnp.where(row >= col, score, -1e30)
        grown = jnp.exp(score - jnp.max(score, axis=-1, keepdims=True))
        prob = grown / jnp.sum(grown, axis=-1, keepdims=True)
        p_ref[at, :] = prob
        probs.append(prob.astype(BF16))
    for c in range(0, V, CHUNK):
        at = slice(c, c + CHUNK)
        rat = slice(D + Z + c, D + Z + c + CHUNK)
        v = dot_nn(x, wv[:, at]) + bv_ref[:, at]
        v_ref[:, at] = v
        value = (v * sig(v)).astype(BF16)
        r = dot_nn(xp, wm[:, rat]) + bm_ref[:, rat]
        r_ref[:, at] = r
        reset = r * sig(r)
        for b in range(0, R // BLOCK, 2):
            rows = slice(b * BLOCK, (b + 2) * BLOCK)
            m_ref[rows, at] = (reset[rows] * dot_nn(pair_of(probs[b], probs[b + 1]), value[rows])).astype(BF16)
    u_ref[...] = dot_nn(xp, wm[:, :D]) + bm_ref[:, :D]
    h_ref[...] = dot_nn(xp, wm[:, D + Z + V :]) + bm_ref[:, D + Z + V :] + dot_nn(m_ref[...], wo[...])


def slope_of(pre, logistic):
    return logistic * (1.0 + pre * (1.0 - logistic))


def mean_of(rows):
    return jnp.mean(rows, axis=-1, keepdims=True)


def ffn_kernel(R, dims, x_ref, u_ref, h_ref, cot_ref, len_ref, gn_ref, bf_ref, bo_ref, *refs):
    D, FF, L = dims
    pieces, refs = refs[:8], refs[8:]
    (
        o_ref, h1_ref, act_ref, dg_ref, df_ref, dum_ref, dt_ref, sd_ref, sf_ref,
        wi, wo, f_scr, n1_scr, a_scr, i1_scr, sem,
    ) = refs
    bring(((pieces[:4], wi), (pieces[4:], wo)), sem)

    @pl.when(pl.program_id(0) == 0)
    def _():
        sd_ref[...] = jnp.zeros_like(sd_ref)
        sf_ref[...] = jnp.zeros_like(sf_ref)

    g1, g2, b1, b2 = (gn_ref[k : k + 1, :] for k in range(4))
    part = min(256, R)

    def strips(s):
        return [slice(k, k + STRIP) for k in range(s * part, (s + 1) * part, STRIP)]

    def first(s):
        for at in strips(s):
            x = x_ref[at, :].astype(F32)
            h = h_ref[at, :]
            y = x + sig(u_ref[at, :]) * (h * sig(h) - x)
            center = y - mean_of(y)
            inverse = lax.rsqrt(mean_of(center * center) + EPSILON)
            n1 = center * inverse
            n1_scr[at, :] = n1
            i1_scr[at, :] = jnp.broadcast_to(inverse, (STRIP, LANES))
            h1_ref[at, :] = (n1 * g1 + b1).astype(BF16)

    def spread(s):
        rows = slice(s * part, (s + 1) * part)
        for c in range(0, FF, CHUNK):
            at = slice(c, c + CHUNK)
            f = dot_nn(h1_ref[rows, :], wi[:, at]) + bf_ref[:, at]
            f_scr[rows, at] = f
            act_ref[rows, at] = (f * sig(f)).astype(BF16)

    def narrow(s):
        rows = slice(s * part, (s + 1) * part)
        a_scr[rows, :] = dot_nn(act_ref[rows, :], wo[...])

    def second(s):
        zero = jnp.zeros((8, D), F32)
        s_gain, s_shift, s_bias = zero, zero, zero
        for at in strips(s):
            y2 = n1_scr[at, :] * g1 + b1 + a_scr[at, :] + bo_ref[...]
            center = y2 - mean_of(y2)
            inverse = lax.rsqrt(mean_of(center * center) + EPSILON)
            n2 = center * inverse
            row = pl.program_id(0) * R + at.start
            place = lax.rem(row, L) + lax.axis_index("seq") * L
            place = place + lax.broadcasted_iota(jnp.int32, (STRIP, 1), 0)
            live = (place < len_ref[row // L]).astype(F32)
            o_ref[at, :] = ((n2 * g2 + b2) * live).astype(BF16)
            dn = cot_ref[at, :].astype(F32) * live
            w = dn * g2
            dy2 = inverse * (w - mean_of(w) - n2 * mean_of(w * n2))
            a_scr[at, :] = dy2
            dg_ref[at, :] = dy2.astype(BF16)
            s_gain, s_shift, s_bias = s_gain + fold(dn * n2), s_shift + fold(dn), s_bias + fold(dy2)
        sd_ref[1:2, :] += jnp.sum(s_gain, axis=0, keepdims=True)
        sd_ref[3:4, :] += jnp.sum(s_shift, axis=0, keepdims=True)
        sd_ref[4:5, :] += jnp.sum(s_bias, axis=0, keepdims=True)

    def spread_back(s):
        rows = slice(s * part, (s + 1) * part)
        for c in range(0, FF, CHUNK):
            at = slice(c, c + CHUNK)
            f = f_scr[rows, at]
            df = (dot_nt(dg_ref[rows, :], wo[at, :]) * slope_of(f, sig(f))).astype(BF16)
            df_ref[rows, at] = df
            add_sums(sf_ref, at, df.astype(F32))

    def narrow_back(s):
        rows = slice(s * part, (s + 1) * part)
        a_scr[rows, :] += dot_nt(df_ref[rows, :], wi[...])

    def third(s):
        zero = jnp.zeros((8, D), F32)
        s_gain, s_shift = zero, zero
        for at in strips(s):
            dh1 = a_scr[at, :]
            n1 = n1_scr[at, :]
            w = dh1 * g1
            dy = i1_scr[at, 0:1] * (w - mean_of(w) - n1 * mean_of(w * n1))
            x = x_ref[at, :].astype(F32)
            h = h_ref[at, :]
            sh = sig(h)
            gate = sig(u_ref[at, :])
            rest = 1.0 - gate
            dyg = dy * gate
            dum_ref[at, :D] = (dyg * (h * sh - x) * rest).astype(BF16)
            dum_ref[at, D:] = (dyg * slope_of(h, sh)).astype(BF16)
            dt_ref[at, :] = dy * rest
            s_gain, s_shift = s_gain + fold(dh1 * n1), s_shift + fold(dh1)
        sd_ref[0:1, :] += jnp.sum(s_gain, axis=0, keepdims=True)
        sd_ref[2:3, :] += jnp.sum(s_shift, axis=0, keepdims=True)

    stages = (first, spread, narrow, second, spread_back, narrow_back, third)
    count = R // part
    for tick in range(len(stages) + count - 1):
        for s in range(count):
            if 0 <= tick - s < len(stages):
                stages[tick - s](s)


def pair_of(top, bottom):
    none = jnp.zeros_like(top)
    return jnp.concatenate([jnp.concatenate([top, none], axis=1), jnp.concatenate([none, bottom], axis=1)], axis=0)


def sum_spots(D, Z, V, FF):
    spans = [("mix", D, Z), ("rel", 0, 2 * BLOCK), ("qk", 0, 3 * Z), ("mix", 0, D), ("mix", D + Z + V, D)]
    spans += [("mix", D + Z + k, D) for k in range(0, V, D)] + [("value", k, D) for k in range(0, V, D)]
    spans += [("ffn", k, D) for k in range(0, FF, D)] + [("rows", k * D, D) for k in range(5)]
    spots, place = [], 0
    for name, start, size in spans:
        spots.append((name, start, place // D, place % D, size))
        place += size
    return spots


def mix_bwd_kernel(R, dims, dum_ref, dt_ref, r_ref, v_ref, z_ref, p_ref, qk_ref, sd_ref, sf_ref, *refs):
    D, Z, V = dims
    pieces, refs = refs[:18], refs[18:]
    db_ref, dv_ref, dxp_ref, do_ref, all_ref, sm_ref, sv_ref, sq_ref, ss_ref, wm, wv, wo, acc, sem = refs
    bring(((pieces[:6], wm), (pieces[6:12], wv), (pieces[12:], wo)), sem)

    @pl.when(pl.program_id(0) == 0)
    def _():
        for ref in (sm_ref, sv_ref, sq_ref, ss_ref):
            ref[...] = jnp.zeros_like(ref)

    last = D + Z + V
    blocks = [slice(b * BLOCK, (b + 1) * BLOCK) for b in range(R // BLOCK)]
    full = [p_ref[rows, :] for rows in blocks]
    probs = [prob.astype(BF16) for prob in full]
    pairs = [slice(k, k + 2 * BLOCK) for k in range(0, R, 2 * BLOCK)]
    double = [pair_of(probs[2 * k], probs[2 * k + 1]) for k in range(len(pairs))]
    wide = [jnp.zeros((2 * BLOCK, 2 * BLOCK), F32) for _ in pairs]
    size = 512

    def head(c):
        return dot_nt(dum_ref[:, D:], wo[c : c + size, :])

    def chunk(c, dmix):
        at = slice(c, c + size)
        rat = slice(D + Z + c, D + Z + c + size)
        zat = slice(Z + c, Z + c + size)
        sum_r = jnp.zeros((1, size), F32)
        sum_v = jnp.zeros((1, size), F32)
        for b, rows in enumerate(pairs):
            r = r_ref[rows, at]
            v = v_ref[rows, at]
            sr = sig(r)
            sv = sig(v)
            value = (v * sv).astype(BF16)
            datt = (dmix[rows] * (r * sr)).astype(BF16)
            dr = (dmix[rows] * slope_of(r, sr) * dot_nn(double[b], value)).astype(BF16)
            db_ref[rows, zat] = dr
            sum_r += jnp.sum(dr.astype(F32), axis=0, keepdims=True)
            wide[b] += dot_nt(datt, value)
            dv = (dot_tn(double[b], datt) * slope_of(v, sv)).astype(BF16)
            dv_ref[rows, at] = dv
            sum_v += jnp.sum(dv.astype(F32), axis=0, keepdims=True)
        sm_ref[:, rat] += sum_r
        sv_ref[:, at] += sum_v

    def give(c):
        at = slice(c, c + size)
        rat = slice(D + Z + c, D + Z + c + size)
        zat = slice(Z + c, Z + c + size)
        acc[...] += dot_nt(db_ref[:, zat], wm[:, rat])
        do_ref[...] += dot_nt(dv_ref[:, at], wv[:, at])

    starts = list(range(0, V, size))
    dmix = head(starts[0])
    acc[...] = dot_nt(dum_ref[:, :D], wm[:, :D]) + dot_nt(dum_ref[:, D:], wm[:, last:])
    do_ref[...] = dt_ref[...]
    chunk(starts[0], dmix)
    for n, c in enumerate(starts[1:]):
        dmix = head(c)
        give(starts[n])
        chunk(c, dmix)
    add_sums(sm_ref, slice(0, D), dum_ref[:, :D].astype(F32))
    add_sums(sm_ref, slice(last, D + last), dum_ref[:, D:].astype(F32))
    for b, rows in enumerate(blocks):
        z = z_ref[rows, :]
        sz = sig(z)
        shared = z * sz
        query = (shared * qk_ref[0:1, :] + qk_ref[2:3, :]).astype(BF16)
        key = (shared * qk_ref[1:2, :]).astype(BF16)
        side = slice(b % 2 * BLOCK, b % 2 * BLOCK + BLOCK)
        dprob = wide[b // 2][side, side]
        inner = jnp.sum(full[b] * dprob, axis=-1, keepdims=True)
        ds = (full[b] * (dprob - inner)).astype(BF16)
        ss_ref[...] += ds.astype(F32)
        dq = dot_nn(ds, key) * Z ** (-0.5)
        dk = dot_tn(ds, query) * Z ** (-0.5)
        sq_ref[0:1, :] += jnp.sum(dq * shared, axis=0, keepdims=True)
        sq_ref[1:2, :] += jnp.sum(dk * shared, axis=0, keepdims=True)
        sq_ref[2:3, :] += jnp.sum(dq, axis=0, keepdims=True)
        dz = (dq * qk_ref[0:1, :] + dk * qk_ref[1:2, :]) * slope_of(z, sz)
        dz = dz.astype(BF16)
        db_ref[rows, :Z] = dz
        add_sums(sm_ref, slice(D, D + Z), dz.astype(F32))
    give(starts[-1])
    dxp_ref[...] = (acc[...] + dot_nt(db_ref[:, :Z], wm[:, D : D + Z])).astype(BF16)

    @pl.when(pl.program_id(0) == pl.num_programs(0) - 1)
    def _():
        moved = jnp.concatenate([ss_ref[...].T, jnp.zeros((BLOCK, BLOCK), F32)], axis=1)
        row = lax.broadcasted_iota(jnp.int32, moved.shape, 0)
        step = 1
        while step < BLOCK:
            moved = jnp.where(jnp.bitwise_and(row, step) == 0, pltpu.roll(moved, step, 1), moved)
            step *= 2
        spots = sum_spots(D, Z, V, sf_ref.shape[1])
        sums = {
            "mix": sm_ref[...], "value": sv_ref[...], "ffn": sf_ref[...], "rel": jnp.sum(moved, axis=0, keepdims=True),
            "qk": jnp.concatenate([sq_ref[k : k + 1, :] for k in range(3)], axis=1),
            "rows": jnp.concatenate([sd_ref[k : k + 1, :] for k in range(5)], axis=1),
        }
        all_ref[...] = jnp.zeros_like(all_ref)
        for name, start, row, col, size in spots:
            all_ref[row : row + 1, col : col + size] = sums[name][:, start : start + size]


def cost_of(flops, microseconds):
    return pl.CostEstimate(flops=flops, bytes_accessed=microseconds * 3_600_000, transcendentals=0)


def any_specs(n):
    return [pl.BlockSpec(memory_space=pl.ANY)] * n


def tile(R, n):
    return pl.BlockSpec((R, n), lambda t: (t, 0))


def fixed(r, n):
    return pl.BlockSpec((r, n), lambda t: (0, 0))


def shape(r, n, dtype=F32):
    return jax.ShapeDtypeStruct((r, n), dtype)


def mix_forward(R, x, xp, bm, bv, qk, rel, pieces):
    T, D = x.shape
    V = bv.shape[1]
    Z = qk.shape[1]
    E = bm.shape[1]
    return pl.pallas_call(
        functools.partial(mix_fwd_kernel, R, (D, Z, V)),
        grid=(T // R,),
        in_specs=[tile(R, D), tile(R, D), fixed(1, E), fixed(1, V), fixed(8, Z), fixed(BLOCK, BLOCK)]
        + any_specs(18),
        out_specs=[
            tile(R, D), tile(R, D), tile(R, V), tile(R, V), tile(R, Z), tile(R, BLOCK), tile(R, V),
            pl.BlockSpec((D, R), lambda t: (0, t)),
        ],
        out_shape=[
            shape(T, D), shape(T, D), shape(T, V), shape(T, V), shape(T, Z), shape(T, BLOCK), shape(T, V, BF16),
            shape(D, T, BF16),
        ],
        scratch_shapes=[
            pltpu.VMEM((D, E), BF16), pltpu.VMEM((D, V), BF16), pltpu.VMEM((V, D), BF16),
            pltpu.SemaphoreType.DMA((18,)),
        ],
        compiler_params=pltpu.CompilerParams(vmem_limit_bytes=VMEM_LIMIT),
        cost_estimate=cost_of(2 * T * D * (E + 2 * V), 33),
        name="mix_forward",
    )(x, xp, bm, bv, qk, rel, *pieces)


def ffn_both(R, L, x, u, h, cot, lengths, norms, bf, bo, pieces):
    T, D = x.shape
    FF = bf.shape[1]
    return pl.pallas_call(
        functools.partial(ffn_kernel, R, (D, FF, L)),
        grid=(T // R,),
        in_specs=[
            tile(R, D), tile(R, D), tile(R, D), tile(R, D), pl.BlockSpec(memory_space=pltpu.SMEM),
            fixed(8, D), fixed(1, FF), fixed(1, D)]
        + any_specs(8),
        out_specs=[
            tile(R, D), tile(R, D), tile(R, FF), tile(R, D), tile(R, FF), tile(R, 2 * D), tile(R, D),
            fixed(8, D), fixed(1, FF),
        ],
        out_shape=[
            shape(T, D, BF16), shape(T, D, BF16), shape(T, FF, BF16), shape(T, D, BF16), shape(T, FF, BF16),
            shape(T, 2 * D, BF16), shape(T, D), shape(8, D), shape(1, FF),
        ],
        scratch_shapes=[
            pltpu.VMEM((D, FF), BF16), pltpu.VMEM((FF, D), BF16), pltpu.VMEM((R, FF), F32), pltpu.VMEM((R, D), F32),
            pltpu.VMEM((R, D), F32), pltpu.VMEM((R, 128), F32), pltpu.SemaphoreType.DMA((12,)),
        ],
        compiler_params=pltpu.CompilerParams(vmem_limit_bytes=VMEM_LIMIT),
        cost_estimate=cost_of(2 * T * D * 4 * FF, 50),
        name="ffn_both",
    )(x, u, h, cot, lengths, norms, bf, bo, *pieces)


def mix_backward(R, dum, dt, r, v, z, p, qk, sum_d, sum_f, pieces):
    T, D = dt.shape
    V = r.shape[1]
    Z = qk.shape[1]
    E = 2 * D + Z + V
    return pl.pallas_call(
        functools.partial(mix_bwd_kernel, R, (D, Z, V)),
        grid=(T // R,),
        in_specs=[
            tile(R, 2 * D), tile(R, D), tile(R, V), tile(R, V), tile(R, Z), tile(R, BLOCK), fixed(8, Z),
            fixed(8, D), fixed(1, sum_f.shape[1]),
        ]
        + any_specs(18),
        out_specs=[
            tile(R, Z + V), tile(R, V), tile(R, D), tile(R, D), fixed(16, D),
        ],
        out_shape=[
            shape(T, Z + V, BF16), shape(T, V, BF16), shape(T, D, BF16), shape(T, D), shape(16, D),
        ],
        scratch_shapes=[
            pltpu.VMEM((1, E), F32), pltpu.VMEM((1, V), F32), pltpu.VMEM((8, Z), F32), pltpu.VMEM((BLOCK, BLOCK), F32),
            pltpu.VMEM((D, E), BF16), pltpu.VMEM((D, V), BF16), pltpu.VMEM((V, D), BF16), pltpu.VMEM((R, D), F32),
            pltpu.SemaphoreType.DMA((18,)),
        ],
        compiler_params=pltpu.CompilerParams(vmem_limit_bytes=VMEM_LIMIT),
        cost_estimate=cost_of(2 * T * D * (E + 2 * V), 40),
        name="mix_backward",
    )(dum, dt, r, v, z, p, qk, sum_d, sum_f, *pieces)


def exchange(value, axis, step):
    return lax.ppermute(value, axis, [(k, k ^ step) for k in range(lax.axis_size(axis))])


def join(*values):
    return lax.optimization_barrier(values)


def own_half(own):
    half = own.shape[0] // 2
    return lax.dynamic_slice_in_dim(own, lax.rem(lax.axis_index("seq"), 2) * half, half, 0)


def over_x(value):
    return exchange(value, "wsh", 2)


def over_y(value):
    return exchange(value, "seq", 1)


def over_core(value):
    return exchange(value, "wsh", 1)


def gather_small(own):
    j = lax.axis_index("wsh")
    four = jnp.stack([own] + [exchange(own, "wsh", d) for d in range(1, 4)])
    return jnp.stack([lax.dynamic_index_in_dim(four, j ^ k, 0, False) for k in range(4)])


class Carry:
    def __init__(self, states, decay, reverse):
        self.entry, self.total = jnp.zeros_like(states), states
        self.own, self.window, self.reverse = jnp.ones_like(decay), decay, reverse

    def send(self, step):
        return exchange(self.total, "seq", step)

    def add(self, step, sent):
        bit = lax.rem(lax.axis_index("seq") // step, 2)
        later = (bit == 0) if self.reverse else (bit == 1)
        self.entry = jnp.where(later, self.entry + self.own * sent, self.entry)
        self.total = jnp.where(later, self.total + self.window * sent, sent + self.window * self.total)
        self.own = jnp.where(later, self.own * self.window, self.own)
        self.window = self.window * self.window


def pick(value, dim, bit):
    return lax.dynamic_index_in_dim(value, bit, dim, False)


def send_half(value, dim, mark):
    axis, step = mark
    bit = lax.rem(lax.axis_index(axis) // step, 2)
    return exchange(pick(value, dim, 1 - bit).astype(BF16), axis, step), pick(value, dim, bit)


def add_half(sent, kept):
    return kept + sent.astype(F32)


def seq_steps():
    return [2**k for k in range(lax.axis_size("seq").bit_length() - 1)]


def send_core(grad):
    rows, cols = grad.shape
    bits = (2,) * len(seq_steps())
    rest = rows // lax.axis_size("wsh") // lax.axis_size("seq")
    return send_half(grad.reshape((2, 2) + bits + (rest, cols)), 1, ("wsh", 1))


def merge(parts, cols):
    pieces = []
    for part in parts:
        for c in range(0, part.shape[-1], cols):
            pieces.append(part[..., c : c + cols])
    return jnp.concatenate(pieces, axis=-2)


class Sum:
    def __init__(self, value):
        self.value = value
        self.marks = [("wsh", 2)] + [("seq", s) for s in reversed(seq_steps())]

    def send(self, mark):
        dim = self.marks.index(mark)
        self.marks.pop(dim)
        sent, self.kept = send_half(self.value, dim, mark)
        return sent

    def add(self, sent):
        self.value = add_half(sent, self.kept)


def widen(block, other, step):
    bit = lax.rem(lax.axis_index("seq") // step, 2)
    first = jnp.where(bit == 0, block, other)
    second = jnp.where(bit == 0, other, block)
    return jnp.concatenate([first, second], axis=0)


def in_order(block):
    bits = block.shape[0].bit_length() - 1
    split = block.reshape((2,) * bits + block.shape[1:])
    turned = split.transpose(tuple(reversed(range(bits))) + (bits, bits + 1))
    return turned.reshape(block.shape)


def sum_over_wsh(value):
    j = lax.axis_index("wsh")
    total = lax.dynamic_index_in_dim(value, j, 0, False)
    for d in range(1, 4):
        total = total + exchange(lax.dynamic_index_in_dim(value, j ^ d, 0, False), "wsh", d)
    return total


def sum_over_seq(total):
    for step in reversed(seq_steps()):
        total = total + exchange(total, "seq", step)
    return total


def body(
    tokens, cotangent, lengths, ema_alpha, ema_delta, ema_beta, ema_eta, ema_omega, mix_weight, mix_bias,
    value_weight, value_bias, qk_gain, qk_bias, rel_bias, out_weight, norm_gain, norm_bias, ffn_in, ffn_in_bias,
    ffn_out, ffn_out_bias,
):
    micro, seqs, L, D = tokens.shape
    G = micro * seqs
    T = G * L
    H = ema_alpha.shape[1]
    R = min(512, T)
    n_wsh = lax.axis_size("wsh")
    i = lax.axis_index("seq")
    Z = qk_gain.shape[0] * n_wsh
    V = value_weight.shape[1]
    FF = ffn_in.shape[1]

    flat_parts = (mix_bias, value_bias, ffn_in_bias, rel_bias, qk_gain[:, 0], qk_gain[:, 1], qk_bias)
    flat = jnp.concatenate(flat_parts).reshape(ema_alpha.shape[0], -1)
    chan = jnp.concatenate(
        [ema_alpha, ema_delta, ema_beta, ema_eta, ema_omega[:, None], norm_gain, norm_bias, ffn_out_bias[:, None], flat],
        axis=1,
    )
    chan, o_mix, o_value, o_out, o_in, o_fout = join(chan, mix_weight, value_weight, out_weight, ffn_in, ffn_out)
    chan = gather_small(chan)
    flat = chan[:, :, 4 * H + 6 :].reshape(n_wsh, -1).astype(F32)
    chan = chan[:, :, : 4 * H + 6].reshape(D, -1).T.astype(F32)
    rate = jax.nn.sigmoid(chan[0:H])
    damp = jax.nn.sigmoid(chan[H : 2 * H])
    beta = chan[2 * H : 3 * H]
    eta = chan[3 * H : 4 * H]
    omega = chan[4 * H : 4 * H + 1]
    keep = 1.0 - rate * damp
    weight = eta * beta * rate
    decay = power(keep, L)
    inward = eta * beta * rate
    x3 = tokens.reshape(G, L, D)
    x = tokens.reshape(T, D)
    y_step, z_steps = ("seq", 1), [("seq", s) for s in seq_steps()[1:]]
    x_step = ("wsh", 2)
    sixth = D // LANES // 6
    steps = seq_steps()
    half = D // LANES // 2

    x_mix = over_x(own_half(o_mix))
    c_mix, c_value = over_core(o_mix), over_core(o_value)
    ends, slice_end = ema_ends(x3, keep)
    ends, slice_end, c_mix, c_value, o_value, o_out = join(ends, slice_end, c_mix, c_value, o_value, o_out)
    x_value, x_out = over_x(own_half(o_value)), over_x(own_half(o_out))
    entry = Carry(slice_end, decay, False)
    sent, x_mix, chan, flat, rate, damp, inward, keep_later = join(
        entry.send(steps[0]), x_mix, chan, flat, rate, damp, inward, keep
    )
    vectors, start = [], 0
    for part in flat_parts:
        vectors.append(flat[:, start : start + part.shape[0]].reshape(1, -1))
        start += part.shape[0]
    bm, bv, bf, rel, gain_q, gain_k, shift_q = vectors
    norms = jnp.concatenate([chan[4 * H + 1 : 4 * H + 5], jnp.zeros((4, D), F32)])
    bo = chan[4 * H + 5 : 4 * H + 6]
    qk = jnp.concatenate([gain_q, gain_k, shift_q, jnp.zeros((5, Z), F32)])
    rel_matrix = skew_matrix(jnp.roll(rel[0, ::-1], BLOCK))
    inverse = 1.0 / keep_later
    factors = jnp.concatenate(
        [
            inward * (1.0 - rate), -inward * (1.0 - rate) * damp * rate, -inward * rate * damp * (1.0 - damp),
            rate * eta, rate * beta,
        ]
    )
    entry.add(steps[0], sent)
    y_mix, xc_mix = over_y(x_mix), over_core(x_mix)
    for step in steps[1:]:
        entry.add(step, entry.send(step))
    state_in, x_value, xc_mix, rel_matrix, norms, bo, qk, inverse, factors, bm = join(
        entry.entry, x_value, xc_mix, rel_matrix, norms, bo, qk, inverse, factors, bm
    )
    y_value, xc_value = over_y(x_value), over_core(x_value)
    so_far = ema_forward((0, half), (), x3, keep, weight, omega, ends, state_in)
    *so_far, y_mix, x_out, xc_value, o_out, o_in, o_fout = join(*so_far, y_mix, x_out, xc_value, o_out, o_in, o_fout)
    y_out, xc_out, yc_mix = over_y(x_out), over_core(x_out), over_core(y_mix)
    c_out = over_core(o_out)
    x_in = over_x(o_in)
    xp, pre, finals = ema_forward((half, half), tuple(so_far), x3, keep, weight, omega, ends, state_in)
    xp, y_value, y_out, xc_out, yc_mix, c_out, o_fout = join(xp, y_value, y_out, xc_out, yc_mix, c_out, o_fout)
    yc_value, yc_out = over_core(y_value), over_core(y_out)
    x_fout = over_x(o_fout)
    mix_pieces = (
        (o_mix, c_mix, x_mix, y_mix, xc_mix, yc_mix) + (o_value, c_value, x_value, y_value, xc_value, yc_value)
        + (o_out, c_out, x_out, y_out, xc_out, yc_out)
    )
    c_in, c_fout = over_core(o_in), over_core(o_fout)
    xp = xp.reshape(T, D)
    forward = mix_forward(min(256, T), x, xp, bm, bv, qk, rel_matrix, mix_pieces)
    (u, h, r, v, z, p, mixed, xt), x_in, x_fout, c_in, c_fout = join(forward, x_in, x_fout, c_in, c_fout)
    ffn_pieces = (o_in, c_in, x_in, over_core(x_in)) + (o_fout, c_fout, x_fout, over_core(x_fout))
    output, h1, act, dg, df, dum, dt, sum_d, sum_f = ffn_both(
        R, L, x, u, h, cotangent.reshape(T, D), lengths.reshape(G), norms, bf, bo, ffn_pieces
    )

    (sent_1, kept_1), (sent_2, kept_2) = send_core(dot_rows(act, dg)), send_core(dot_rows(h1, df))
    (sent_3, kept_3), (sent_4, kept_4) = send_core(dot_rows(mixed, dum[:, D:])), send_core(dot_nn(xt, dum))
    kept_3, kept_4, sent_1, sent_2 = join(kept_3, kept_4, sent_1, sent_2)
    sum_a = Sum(merge([add_half(sent_1, kept_1), add_half(sent_2, kept_2)], D))
    over_a = sum_a.send(x_step)
    sum_b = Sum(merge([add_half(sent_3, kept_3), add_half(sent_4, kept_4)], D))
    over_b = sum_b.send(y_step)
    back = mix_backward(min(256, T), dum, dt, r, v, z, p, qk, sum_d, sum_f, mix_pieces)
    (db, dv, dxp, dtok, early), over_a, over_b = join(back, over_a, over_b)
    sum_a.add(over_a)
    sum_b.add(over_b)
    over_a, over_b = sum_a.send(y_step), sum_b.send(x_step)
    sent_1, kept_1 = send_core(dot_nn(xt, db))
    dxp, kept_1, over_a, over_b = join(dxp, kept_1, over_a, over_b)
    sum_a.add(over_a)
    sum_b.add(over_b)
    rows_a = sum_a.value.shape[-2]
    sum_a.value = jnp.concatenate([sum_a.value, sum_b.value], axis=-2)
    over_a = sum_a.send(z_steps[0])
    dpe, back_ends, slice_start = ema_back_ends(dxp.reshape(G, L, D), pre, keep)
    dpe, back_ends, slice_start, over_a, sent_1, dv = join(dpe, back_ends, slice_start, over_a, sent_1, dv)
    sum_a.add(over_a)
    sum_c = Sum(add_half(sent_1, kept_1))
    over_a = sum_a.send(z_steps[1])
    entry = Carry(slice_start, decay, True)
    sent = entry.send(steps[0])
    sent_2, kept_2 = send_core(dot_rows(x, dv))
    kept_2, sent, over_a = join(kept_2, sent, over_a)
    over_c = sum_c.send(x_step)
    entry.add(steps[0], sent)
    sent, sent_2 = join(entry.send(steps[1]), sent_2)
    entry.add(steps[1], sent)
    sum_d_ = Sum(add_half(sent_2, kept_2))
    over_d = sum_d_.send(y_step)
    for step in steps[2:]:
        entry.add(step, entry.send(step))
    state_in = entry.entry
    consts = (dpe, x3, keep, inverse, weight, omega, finals, back_ends, state_in, dtok.reshape(G, L, D), factors)
    order = list(reversed(steps))

    def back_part(k, so_far):
        return ema_backward((k * sixth, sixth), tuple(so_far), *consts)

    so_far = back_part(0, ())
    *so_far, over_a, over_c = join(*so_far, over_a, over_c)
    sum_a.add(over_a)
    for mark in z_steps[2:]:
        sum_a.add(sum_a.send(mark))
    sum_c.add(over_c)
    over_c = sum_c.send(y_step)
    block = sum_a.value.astype(BF16)[None]
    more = exchange(block, "seq", order[0])
    so_far = back_part(1, so_far)
    *so_far, over_c, over_d, more = join(*so_far, over_c, over_d, more)
    sum_c.add(over_c)
    sum_d_.add(over_d)
    over_d = sum_d_.send(x_step)
    block = widen(block, more, order[0])
    more = exchange(block, "seq", order[1])
    so_far = back_part(2, so_far)
    *so_far, over_d, more = join(*so_far, over_d, more)
    sum_d_.add(over_d)
    *so_far, block = join(*so_far, widen(block, more, order[1]))
    more = exchange(block, "seq", order[2])
    cols_c = sum_c.value.shape[-1]
    sum_c.value = jnp.concatenate([sum_c.value, sum_d_.value], axis=-1)
    over_c = sum_c.send(z_steps[0])
    so_far = back_part(3, so_far)
    *so_far, over_c = join(*so_far, over_c)
    sum_c.add(over_c)
    over_c = sum_c.send(z_steps[1])
    so_far = back_part(4, so_far)
    *so_far, over_c = join(*so_far, over_c)
    sum_c.add(over_c)
    for mark in z_steps[2:]:
        sum_c.add(sum_c.send(mark))
    small = sum_c.value.astype(BF16)[None]
    over_c = exchange(small, "seq", order[0])
    so_far = back_part(5, so_far)
    *so_far, over_c, more = join(*so_far, over_c, more)
    small = widen(small, over_c, order[0])
    block = widen(block, more, order[2])
    for step in order[3:]:
        block = widen(block, exchange(block, "seq", step), step)
    input_grad, late = so_far
    over_c = exchange(small, "seq", order[1])
    late = late.reshape(-1, n_wsh, D // n_wsh).transpose(1, 0, 2)
    sides = jnp.concatenate([early[:, k : k + D // n_wsh] for k in range(0, D, D // n_wsh)])
    late = jnp.concatenate([late, jnp.broadcast_to(sides, (n_wsh,) + sides.shape)], axis=1)
    late, over_c = join(sum_over_wsh(late), over_c)
    small = widen(small, over_c, order[1])
    over_c = exchange(small, "seq", order[2])
    late, over_c = join(sum_over_seq(late), over_c)
    small = widen(small, over_c, order[2])
    for step in order[3:]:
        small = widen(small, exchange(small, "seq", step), step)
    block, small = in_order(block), in_order(small)
    g_a, g_b = block[:, :rows_a].reshape(-1, D).astype(F32), block[:, rows_a:].reshape(-1, D).astype(F32)
    small = small.reshape(-1, small.shape[-1]).astype(F32)
    g_c, g_d = small[:, :cols_c], small[:, cols_c:]
    input_grad = input_grad.reshape(tokens.shape)

    FF = ffn_in.shape[1]
    sides = late[4 * H + 8 :].reshape(n_wsh, 16, -1)
    early = jnp.concatenate([sides[k] for k in range(n_wsh)], axis=1)
    spans = {}
    for name, start, row, col, size in sum_spots(D, Z, V, FF):
        spans[name, start] = early[row, col : col + size]

    def span_of(name):
        return jnp.concatenate([spans[key] for key in sorted(spans) if key[0] == name])

    j = lax.axis_index("wsh")
    qk_sums, row_sums = span_of("qk"), span_of("rows")
    smalls = []
    for part in (
        span_of("mix"), span_of("value"), span_of("ffn"), span_of("rel"),
        *(qk_sums[k * Z : k * Z + Z] for k in range(3)), *(row_sums[k * D : k * D + D] for k in range(5)),
    ):
        size = part.shape[0] // n_wsh
        smalls.append(lax.dynamic_slice(part, (j * size,), (size,)))
    (
        g_mix_bias, g_value_bias, g_ffn_in_bias, g_rel, g_gain_q, g_gain_k, g_shift, gain_1, gain_2, shift_1, shift_2,
        g_ffn_out_bias,
    ) = smalls
    late = late[: 4 * H + 1].T
    tall_rows, wide_rows = ffn_out.shape[0], ffn_in.shape[0]
    n_seq = lax.axis_size("seq")
    first_rows = tall_rows // n_seq

    def unmerge(merged):
        parts = merged.reshape(n_seq, -1, D)
        top = parts[:, :first_rows].reshape(tall_rows, D)
        sides = parts[:, first_rows:].reshape(n_seq, 2, wide_rows // n_seq, D)
        return top, jnp.concatenate([sides[:, k].reshape(wide_rows, D) for k in range(2)], axis=1)

    g_ffn_out, g_ffn_in = unmerge(g_a)
    g_out, g_edges = unmerge(g_b)
    g_mix = jnp.concatenate([g_edges[:, :D], g_c, g_edges[:, D:]], axis=1)
    return (
        output.reshape(tokens.shape), input_grad,
        late[:, 0:H], late[:, H : 2 * H], late[:, 2 * H : 3 * H], late[:, 3 * H : 4 * H], late[:, 4 * H],
        g_mix, g_mix_bias, g_d, g_value_bias,
        jnp.stack([g_gain_q, g_gain_k], axis=1), g_shift, g_rel, g_out,
        jnp.stack([gain_1, gain_2], axis=1), jnp.stack([shift_1, shift_2], axis=1),
        g_ffn_in, g_ffn_in_bias, g_ffn_out, g_ffn_out_bias,
    )


def solution(mesh):
    in_specs = (
        P(None, "wsh", "seq", None),
        P(None, "wsh", "seq", None),
        P(None, "wsh"),
        P("wsh", None),
        P("wsh", None),
        P("wsh", None),
        P("wsh", None),
        P("wsh"),
        P("wsh", None),
        P("wsh"),
        P("wsh", None),
        P("wsh"),
        P("wsh", None),
        P("wsh"),
        P("wsh"),
        P("wsh", None),
        P("wsh", None),
        P("wsh", None),
        P("wsh", None),
        P("wsh"),
        P("wsh", None),
        P("wsh"),
    )
    out_specs = (
        P(None, "wsh", "seq", None),
        P(None, "wsh", "seq", None),
        P("wsh", None),
        P("wsh", None),
        P("wsh", None),
        P("wsh", None),
        P("wsh"),
        P("wsh", None),
        P("wsh"),
        P("wsh", None),
        P("wsh"),
        P("wsh", None),
        P("wsh"),
        P("wsh"),
        P("wsh", None),
        P("wsh", None),
        P("wsh", None),
        P("wsh", None),
        P("wsh"),
        P("wsh", None),
        P("wsh"),
    )
    return jax.shard_map(body, mesh=mesh, in_specs=in_specs, out_specs=out_specs, check_vma=False)
```

```python
import functools

import jax
import jax.numpy as jnp
from jax import lax
from jax.experimental import pallas as pl
from jax.experimental.pallas import tpu as pltpu
from jax.sharding import PartitionSpec as P

BLOCK = 128
LANES = 128
CH = 8
PAD = 1
CHUNK = 768
STRIP = 32
EPSILON = 1e-05
VMEM_LIMIT = 62 * 1024 * 1024
F32 = jnp.float32
BF16 = jnp.bfloat16


def dot_rows(left_op, right_op):
    return jnp.einsum("ri,rj->ij", left_op, right_op, preferred_element_type=jnp.float32)


def skew_matrix(wrapped):
    lead = wrapped.shape[:-1]
    flat = jnp.tile(wrapped, (1,) * len(lead) + (BLOCK,))[..., : BLOCK * (2 * BLOCK - 1)]
    return flat.reshape(lead + (BLOCK, 2 * BLOCK - 1))[..., :BLOCK]


def power(v, n):
    k = 1
    while k < n:
        v = v * v
        k *= 2
    return v

def rows_of(scr, s, T):
    return scr[pl.ds(s, CH, stride=T+PAD), :]

def spread(scr, v, T):
    for k in range(CH):
        scr[k*(T+PAD):k*(T+PAD)+T, :] = v[k*T:(k+1)*T, :]

def collect(scr, T):
    return jnp.concatenate([scr[k*(T+PAD):k*(T+PAD)+T, :] for k in range(CH)], axis=0)

def ends_kernel(G, H, T, x_ref, q_ref, e_ref, s_ref, *scrs):
    for g in range(G):
        spread(scrs[g], x_ref[g].astype(F32), T)
    chunk_ends(G, H, T, q_ref, e_ref, s_ref, scrs, False)


def chunk_ends(G, H, T, q_ref, e_ref, s_ref, scrs, reverse):
    q = [jnp.broadcast_to(q_ref[h:h+1, :], (CH, LANES)) for h in range(H)]

    def step(s, states):
        rows = [rows_of(scr, T - 1 - s if reverse else s, T) for scr in scrs]
        return tuple(q[n % H] * states[n] + rows[n // H] for n in range(G * H))

    zero = jnp.zeros((CH, LANES), F32)
    states = lax.fori_loop(0, T, step, (zero,) * (G * H), unroll=min(T, 16))
    for n in range(G * H):
        e_ref[n // H, n % H * CH : (n % H + 1) * CH, :] = states[n]
    qT = power(q_ref[...], T)
    for g in range(G):
        c = jnp.zeros((H, LANES), F32)
        for k in reversed(range(CH)) if reverse else range(CH):
            c = qT * c + e_ref[g, pl.ds(k, H, stride=CH), :]
        s_ref[g] = c


def fwd_kernel(H, T, x_ref, q_ref, w_ref, om_ref, e_ref, c_ref, *refs):
    xp_ref, p_ref, f_ref, scr, cs, ps = refs[-6:]
    spread(scr, x_ref[0].astype(F32), T)
    qT = power(q_ref[...], T)
    c = c_ref[0]
    for k in range(CH):
        cs[pl.ds(k,H,stride=CH), :] = c
        c = qT*c + e_ref[0, pl.ds(k,H,stride=CH), :]
    q = [jnp.broadcast_to(q_ref[h:h+1, :], (CH, LANES)) for h in range(H)]
    w = [jnp.broadcast_to(w_ref[h:h+1, :], (CH, LANES)) for h in range(H)]
    om = jnp.broadcast_to(om_ref[...], (CH,LANES))
    def step(s, st):
        xs = rows_of(scr, s, T)
        st = tuple(q[h]*st[h] + xs for h in range(H))
        terms = [w[h]*st[h] for h in range(H)]
        while len(terms) > 1:
            terms = [terms[i]+terms[i+1] for i in range(0,len(terms)-1,2)] + ([terms[-1]] if len(terms)%2 else [])
        ps[pl.ds(s, CH, stride=T+PAD), :] = terms[0] + om*xs
        return st
    st = lax.fori_loop(0, T, step, tuple(cs[h*CH:(h+1)*CH, :] for h in range(H)), unroll=min(T, 32))
    for h in range(H):
        f_ref[0, h*CH:(h+1)*CH, :] = st[h]
    p = collect(ps, T)
    p_ref[0] = p
    xp_ref[0] = (p*jax.nn.sigmoid(p)).astype(xp_ref.dtype)

def bends_kernel(G, H, T, dxp_ref, p_ref, q_ref, d_ref, e_ref, s_ref, *scrs):
    for g in range(G):
        p = p_ref[g]
        sg = jax.nn.sigmoid(p)
        d = dxp_ref[g].astype(F32) * (sg*(1.0+p*(1.0-sg)))
        d_ref[g] = d
        spread(scrs[g], d, T)
    chunk_ends(G, H, T, q_ref, e_ref, s_ref, scrs, True)


def bwd_kernel(H, T, d_ref, x_ref, q_ref, qi_ref, w_ref, om_ref, f_ref, e_ref, c_ref, t_ref, k_ref, *refs):
    dx_ref, out_ref, s1_ref, s3_ref, go_ref, scr, cs, dx, ds = refs[-9:]
    g = pl.program_id(1)
    x = x_ref[0].astype(F32)
    spread(scr, x, T)
    dv = d_ref[0]
    spread(ds, dv, T)
    qT = power(q_ref[...], T)
    c = c_ref[0]
    for k in reversed(range(CH)):
        cs[pl.ds(k,H,stride=CH), :] = c
        c = qT*c + e_ref[0, pl.ds(k,H,stride=CH), :]
    om = jnp.broadcast_to(om_ref[...], (CH,LANES))
    HH = H//2
    zero = jnp.zeros((CH,LANES),F32)
    @pl.when(g==0)
    def _():
        go_ref[...] = jnp.zeros_like(go_ref)
        s1_ref[...] = jnp.zeros_like(s1_ref)
        s3_ref[...] = jnp.zeros_like(s3_ref)
    go_ref[...] += jnp.sum(dv*x, axis=0, keepdims=True)
    for half in range(2):
        hs = range(half*HH, half*HH+HH)
        q = [jnp.broadcast_to(q_ref[h:h+1, :], (CH, LANES)) for h in hs]
        qi = [jnp.broadcast_to(qi_ref[h:h+1, :], (CH, LANES)) for h in hs]
        w = [jnp.broadcast_to(w_ref[h:h+1, :], (CH, LANES)) for h in hs]
        def step(s, carry):
            l, st, a1, a3 = carry
            at = pl.ds(T-1-s, CH, stride=T+PAD)
            d = ds[at, :]
            xs = scr[at, :]
            a1 = tuple(a1[i] + d*st[i] for i in range(HH))
            l = tuple(q[i]*l[i] + d for i in range(HH))
            st = tuple((st[i]-xs)*qi[i] for i in range(HH))
            a3 = tuple(a3[i] + l[i]*st[i] for i in range(HH))
            terms = [w[i]*l[i] for i in range(HH)]
            while len(terms) > 1:
                terms = [terms[i]+terms[i+1] for i in range(0,len(terms)-1,2)]
            if half == 0:
                dx[at, :] = terms[0] + om*d
            else:
                dx[at, :] = dx[at, :] + terms[0]
            return l, st, a1, a3
        init = (tuple(cs[h*CH:(h+1)*CH,:] for h in hs), tuple(f_ref[0,h*CH:(h+1)*CH,:] for h in hs), (zero,)*HH, (zero,)*HH)
        l, st, a1, a3 = lax.fori_loop(0, T, step, init, unroll=min(T, 16))
        for i,h in enumerate(hs):
            s1_ref[h:h+1,:] += jnp.sum(a1[i],axis=0,keepdims=True)
            s3_ref[h:h+1,:] += jnp.sum(a3[i],axis=0,keepdims=True)
    dx_ref[0] = (t_ref[0] + collect(dx, T).astype(dx_ref.dtype).astype(F32)).astype(dx_ref.dtype)

    @pl.when(g == pl.num_programs(1) - 1)
    def _():
        s1, s3 = s1_ref[...], s3_ref[...]
        out_ref[0:H, :] = k_ref[0:H, :] * s1 + k_ref[H : 2 * H, :] * s3
        out_ref[H : 2 * H, :] = k_ref[2 * H : 3 * H, :] * s3
        out_ref[2 * H : 3 * H, :] = k_ref[3 * H : 4 * H, :] * s1
        out_ref[3 * H : 4 * H, :] = k_ref[4 * H : 5 * H, :] * s1
        out_ref[4 * H : 4 * H + 8, :] = jnp.broadcast_to(go_ref[...], (8, LANES))


def specs(L, H, first=0):
    blk = pl.BlockSpec((1, L, LANES), lambda c, g: (g, 0, c + first))
    par = pl.BlockSpec((H, LANES), lambda c, g: (0, c + first))
    one = pl.BlockSpec((1, LANES), lambda c, g: (0, c + first))
    st = pl.BlockSpec((1, H * CH, LANES), lambda c, g: (g, 0, c + first))
    car = pl.BlockSpec((1, H, LANES), lambda c, g: (g, 0, c + first))
    return blk, par, one, st, car


def all_specs(G, L, H):
    blk = pl.BlockSpec((G, L, LANES), lambda c: (0, 0, c))
    par = pl.BlockSpec((H, LANES), lambda c: (0, c))
    st = pl.BlockSpec((G, H * CH, LANES), lambda c: (0, 0, c))
    car = pl.BlockSpec((G, H, LANES), lambda c: (0, 0, c))
    return blk, par, st, car


def ema_ends(x, q):
    G, L, C = x.shape
    H = q.shape[0]
    blk, par, st, car = all_specs(G, L, H)
    return pl.pallas_call(
        functools.partial(ends_kernel, G, H, L // CH),
        grid=(C // LANES,),
        in_specs=[blk, par],
        out_specs=[st, car],
        out_shape=[jax.ShapeDtypeStruct((G, H * CH, C), F32), jax.ShapeDtypeStruct((G, H, C), F32)],
        scratch_shapes=[pltpu.VMEM((L + CH * PAD, LANES), F32)] * G,
        cost_estimate=cost_of(0, 11),
        name="ema_ends",
    )(x, q)


def ema_forward(span, so_far, x, q, w, om, e, c):
    G, L, C = x.shape
    H = q.shape[0]
    first, count = span
    blk, par, one, st, car = specs(L, H, first)
    return pl.pallas_call(
        functools.partial(fwd_kernel, H, L // CH),
        grid=(count, G),
        in_specs=[blk, par, par, one, st, car] + [pl.BlockSpec(memory_space=pl.ANY)] * len(so_far),
        out_specs=[blk, blk, st],
        out_shape=[
            jax.ShapeDtypeStruct((G, L, C), BF16), jax.ShapeDtypeStruct((G, L, C), F32),
            jax.ShapeDtypeStruct((G, H * CH, C), F32),
        ],
        scratch_shapes=[
            pltpu.VMEM((L + CH * PAD, LANES), F32), pltpu.VMEM((H * CH, LANES), F32),
            pltpu.VMEM((L + CH * PAD, LANES), F32),
        ],
        input_output_aliases={6 + k: k for k in range(len(so_far))},
        cost_estimate=cost_of(0, 3 * count),
        name="ema_forward",
    )(x, q, w, om, e, c, *so_far)


def ema_back_ends(dxp, p, q):
    G, L, C = p.shape
    H = q.shape[0]
    blk, par, st, car = all_specs(G, L, H)
    return pl.pallas_call(
        functools.partial(bends_kernel, G, H, L // CH),
        grid=(C // LANES,),
        in_specs=[blk, blk, par],
        out_specs=[blk, st, car],
        out_shape=[
            jax.ShapeDtypeStruct((G, L, C), F32), jax.ShapeDtypeStruct((G, H * CH, C), F32),
            jax.ShapeDtypeStruct((G, H, C), F32),
        ],
        scratch_shapes=[pltpu.VMEM((L + CH * PAD, LANES), F32)] * G,
        cost_estimate=cost_of(0, 15),
        name="ema_back_ends",
    )(dxp, p, q)


def ema_backward(span, so_far, d, x, q, qi, w, om, f, e, c, t, k):
    G, L, C = x.shape
    H = q.shape[0]
    first, count = span
    blk, par, one, st, car = specs(L, H, first)
    factors = pl.BlockSpec((5 * H, LANES), lambda c, g: (0, c + first))
    sums = pl.BlockSpec((4 * H + 8, LANES), lambda c, g: (0, c + first))
    return pl.pallas_call(
        functools.partial(bwd_kernel, H, L // CH),
        grid=(count, G),
        in_specs=[blk, blk, par, par, par, one, st, st, car, blk, factors]
        + [pl.BlockSpec(memory_space=pl.ANY)] * len(so_far),
        out_specs=[blk, sums],
        out_shape=[
            jax.ShapeDtypeStruct((G, L, C), BF16), jax.ShapeDtypeStruct((4 * H + 8, C), F32),
        ],
        scratch_shapes=[
            pltpu.VMEM((H, LANES), F32), pltpu.VMEM((H, LANES), F32), pltpu.VMEM((1, LANES), F32),
            pltpu.VMEM((L + CH * PAD, LANES), F32), pltpu.VMEM((H * CH, LANES), F32),
            pltpu.VMEM((L + CH * PAD, LANES), F32), pltpu.VMEM((L + CH * PAD, LANES), F32),
        ],
        input_output_aliases={11 + n: n for n in range(len(so_far))},
        cost_estimate=cost_of(0, 8 * count),
        name="ema_backward",
    )(d, x, q, qi, w, om, f, e, c, t, k, *so_far)


def sig(v):
    return 0.5 * jnp.tanh(0.5 * v) + 0.5


def dot_nn(left_op, right_op):
    return jnp.dot(left_op, right_op, preferred_element_type=F32)


def dot_nt(left_op, right_op):
    return lax.dot_general(left_op, right_op, (((1,), (1,)), ((), ())), preferred_element_type=F32)


def dot_tn(left_op, right_op):
    return lax.dot_general(left_op, right_op, (((0,), (0,)), ((), ())), preferred_element_type=F32)


def piece_copies(pieces, target):
    j = lax.axis_index("wsh")
    bit = lax.rem(lax.axis_index("seq"), 2)
    rows = target.shape[0] // 4
    half = rows // 2
    if len(pieces) == 4:
        starts = [(j ^ k) * rows for k in range(4)]
    else:
        low, high = bit * half, (1 - bit) * half
        starts = [j * rows, (j ^ 1) * rows]
        starts += [(j ^ 2) * rows + low, (j ^ 2) * rows + high, (j ^ 3) * rows + low, (j ^ 3) * rows + high]
    return [
        (piece, target.at[pl.ds(pl.multiple_of(start, 32), piece.shape[0]), :])
        for piece, start in zip(pieces, starts)
    ]


def bring(groups, sem):
    @pl.when(pl.program_id(0) == 0)
    def _():
        copies = []
        for pieces, target in groups:
            for source, spot in piece_copies(pieces, target):
                copies.append(pltpu.make_async_copy(source, spot, sem.at[len(copies)]))
        for copy in copies:
            copy.start()
        for copy in copies:
            copy.wait()


def fold(rows):
    total = rows[:8]
    for k in range(8, STRIP, 8):
        total = total + rows[k : k + 8]
    return total


def add_sums(ref, at, rows):
    ref[:, at] += jnp.sum(rows, axis=0, keepdims=True)


def mix_fwd_kernel(R, dims, x_ref, xp_ref, bm_ref, bv_ref, qk_ref, rel_ref, *refs):
    D, Z, V = dims
    pieces, refs = refs[:18], refs[18:]
    u_ref, h_ref, r_ref, v_ref, z_ref, p_ref, m_ref, xt_ref, wm, wv, wo, sem = refs
    bring(((pieces[:6], wm), (pieces[6:12], wv), (pieces[12:], wo)), sem)
    xp = xp_ref[...]
    x = x_ref[...]
    xt_ref[...] = xp.T
    z = dot_nn(xp, wm[:, D : D + Z]) + bm_ref[:, D : D + Z]
    z_ref[...] = z
    shared = z * sig(z)
    query = (shared * qk_ref[0:1, :] + qk_ref[2:3, :]).astype(BF16)
    key = (shared * qk_ref[1:2, :]).astype(BF16)
    probs = []
    row = lax.broadcasted_iota(jnp.int32, (BLOCK, BLOCK), 0)
    col = lax.broadcasted_iota(jnp.int32, (BLOCK, BLOCK), 1)
    for b in range(R // BLOCK):
        at = slice(b * BLOCK, (b + 1) * BLOCK)
        score = dot_nt(query[at], key[at]) * Z ** (-0.5) + rel_ref[...]
        score = jnp.where(row >= col, score, -1e30)
        grown = jnp.exp(score - jnp.max(score, axis=-1, keepdims=True))
        prob = grown / jnp.sum(grown, axis=-1, keepdims=True)
        p_ref[at, :] = prob
        probs.append(prob.astype(BF16))
    for c in range(0, V, CHUNK):
        at = slice(c, c + CHUNK)
        rat = slice(D + Z + c, D + Z + c + CHUNK)
        v = dot_nn(x, wv[:, at]) + bv_ref[:, at]
        v_ref[:, at] = v
        value = (v * sig(v)).astype(BF16)
        r = dot_nn(xp, wm[:, rat]) + bm_ref[:, rat]
        r_ref[:, at] = r
        reset = r * sig(r)
        for b in range(0, R // BLOCK, 2):
            rows = slice(b * BLOCK, (b + 2) * BLOCK)
            m_ref[rows, at] = (reset[rows] * dot_nn(pair_of(probs[b], probs[b + 1]), value[rows])).astype(BF16)
    u_ref[...] = dot_nn(xp, wm[:, :D]) + bm_ref[:, :D]
    h_ref[...] = dot_nn(xp, wm[:, D + Z + V :]) + bm_ref[:, D + Z + V :] + dot_nn(m_ref[...], wo[...])


def slope_of(pre, logistic):
    return logistic * (1.0 + pre * (1.0 - logistic))


def mean_of(rows):
    return jnp.mean(rows, axis=-1, keepdims=True)


def ffn_kernel(R, dims, x_ref, u_ref, h_ref, cot_ref, len_ref, gn_ref, bf_ref, bo_ref, *refs):
    D, FF, L = dims
    pieces, refs = refs[:8], refs[8:]
    (
        o_ref, h1_ref, act_ref, dg_ref, df_ref, dum_ref, dt_ref, sd_ref, sf_ref,
        wi, wo, f_scr, n1_scr, a_scr, i1_scr, sem,
    ) = refs
    bring(((pieces[:4], wi), (pieces[4:], wo)), sem)

    @pl.when(pl.program_id(0) == 0)
    def _():
        sd_ref[...] = jnp.zeros_like(sd_ref)
        sf_ref[...] = jnp.zeros_like(sf_ref)

    g1, g2, b1, b2 = (gn_ref[k : k + 1, :] for k in range(4))
    part = min(256, R)

    def strips(s):
        return [slice(k, k + STRIP) for k in range(s * part, (s + 1) * part, STRIP)]

    def first(s):
        for at in strips(s):
            x = x_ref[at, :].astype(F32)
            h = h_ref[at, :]
            y = x + sig(u_ref[at, :]) * (h * sig(h) - x)
            center = y - mean_of(y)
            inverse = lax.rsqrt(mean_of(center * center) + EPSILON)
            n1 = center * inverse
            n1_scr[at, :] = n1
            i1_scr[at, :] = jnp.broadcast_to(inverse, (STRIP, LANES))
            h1_ref[at, :] = (n1 * g1 + b1).astype(BF16)

    def spread(s):
        rows = slice(s * part, (s + 1) * part)
        for c in range(0, FF, CHUNK):
            at = slice(c, c + CHUNK)
            f = dot_nn(h1_ref[rows, :], wi[:, at]) + bf_ref[:, at]
            f_scr[rows, at] = f
            act_ref[rows, at] = (f * sig(f)).astype(BF16)

    def narrow(s):
        rows = slice(s * part, (s + 1) * part)
        a_scr[rows, :] = dot_nn(act_ref[rows, :], wo[...])

    def second(s):
        zero = jnp.zeros((8, D), F32)
        s_gain, s_shift, s_bias = zero, zero, zero
        for at in strips(s):
            y2 = n1_scr[at, :] * g1 + b1 + a_scr[at, :] + bo_ref[...]
            center = y2 - mean_of(y2)
            inverse = lax.rsqrt(mean_of(center * center) + EPSILON)
            n2 = center * inverse
            row = pl.program_id(0) * R + at.start
            place = lax.rem(row, L) + lax.axis_index("seq") * L
            place = place + lax.broadcasted_iota(jnp.int32, (STRIP, 1), 0)
            live = (place < len_ref[row // L]).astype(F32)
            o_ref[at, :] = ((n2 * g2 + b2) * live).astype(BF16)
            dn = cot_ref[at, :].astype(F32) * live
            w = dn * g2
            dy2 = inverse * (w - mean_of(w) - n2 * mean_of(w * n2))
            a_scr[at, :] = dy2
            dg_ref[at, :] = dy2.astype(BF16)
            s_gain, s_shift, s_bias = s_gain + fold(dn * n2), s_shift + fold(dn), s_bias + fold(dy2)
        sd_ref[1:2, :] += jnp.sum(s_gain, axis=0, keepdims=True)
        sd_ref[3:4, :] += jnp.sum(s_shift, axis=0, keepdims=True)
        sd_ref[4:5, :] += jnp.sum(s_bias, axis=0, keepdims=True)

    def spread_back(s):
        rows = slice(s * part, (s + 1) * part)
        for c in range(0, FF, CHUNK):
            at = slice(c, c + CHUNK)
            f = f_scr[rows, at]
            df = (dot_nt(dg_ref[rows, :], wo[at, :]) * slope_of(f, sig(f))).astype(BF16)
            df_ref[rows, at] = df
            add_sums(sf_ref, at, df.astype(F32))

    def narrow_back(s):
        rows = slice(s * part, (s + 1) * part)
        a_scr[rows, :] += dot_nt(df_ref[rows, :], wi[...])

    def third(s):
        zero = jnp.zeros((8, D), F32)
        s_gain, s_shift = zero, zero
        for at in strips(s):
            dh1 = a_scr[at, :]
            n1 = n1_scr[at, :]
            w = dh1 * g1
            dy = i1_scr[at, 0:1] * (w - mean_of(w) - n1 * mean_of(w * n1))
            x = x_ref[at, :].astype(F32)
            h = h_ref[at, :]
            sh = sig(h)
            gate = sig(u_ref[at, :])
            rest = 1.0 - gate
            dyg = dy * gate
            dum_ref[at, :D] = (dyg * (h * sh - x) * rest).astype(BF16)
            dum_ref[at, D:] = (dyg * slope_of(h, sh)).astype(BF16)
            dt_ref[at, :] = dy * rest
            s_gain, s_shift = s_gain + fold(dh1 * n1), s_shift + fold(dh1)
        sd_ref[0:1, :] += jnp.sum(s_gain, axis=0, keepdims=True)
        sd_ref[2:3, :] += jnp.sum(s_shift, axis=0, keepdims=True)

    stages = (first, spread, narrow, second, spread_back, narrow_back, third)
    count = R // part
    for tick in range(len(stages) + count - 1):
        for s in range(count):
            if 0 <= tick - s < len(stages):
                stages[tick - s](s)


def pair_of(top, bottom):
    none = jnp.zeros_like(top)
    return jnp.concatenate([jnp.concatenate([top, none], axis=1), jnp.concatenate([none, bottom], axis=1)], axis=0)


def sum_spots(D, Z, V, FF):
    spans = [("mix", D, Z), ("rel", 0, 2 * BLOCK), ("qk", 0, 3 * Z), ("mix", 0, D), ("mix", D + Z + V, D)]
    spans += [("mix", D + Z + k, D) for k in range(0, V, D)] + [("value", k, D) for k in range(0, V, D)]
    spans += [("ffn", k, D) for k in range(0, FF, D)] + [("rows", k * D, D) for k in range(5)]
    spots, place = [], 0
    for name, start, size in spans:
        spots.append((name, start, place // D, place % D, size))
        place += size
    return spots


def mix_bwd_kernel(R, dims, dum_ref, dt_ref, r_ref, v_ref, z_ref, p_ref, qk_ref, sd_ref, sf_ref, *refs):
    D, Z, V = dims
    pieces, refs = refs[:18], refs[18:]
    db_ref, dv_ref, dxp_ref, do_ref, all_ref, sm_ref, sv_ref, sq_ref, ss_ref, wm, wv, wo, acc, sem = refs
    bring(((pieces[:6], wm), (pieces[6:12], wv), (pieces[12:], wo)), sem)

    @pl.when(pl.program_id(0) == 0)
    def _():
        for ref in (sm_ref, sv_ref, sq_ref, ss_ref):
            ref[...] = jnp.zeros_like(ref)

    last = D + Z + V
    blocks = [slice(b * BLOCK, (b + 1) * BLOCK) for b in range(R // BLOCK)]
    full = [p_ref[rows, :] for rows in blocks]
    probs = [prob.astype(BF16) for prob in full]
    pairs = [slice(k, k + 2 * BLOCK) for k in range(0, R, 2 * BLOCK)]
    double = [pair_of(probs[2 * k], probs[2 * k + 1]) for k in range(len(pairs))]
    wide = [jnp.zeros((2 * BLOCK, 2 * BLOCK), F32) for _ in pairs]
    size = 512

    def head(c):
        return dot_nt(dum_ref[:, D:], wo[c : c + size, :])

    def chunk(c, dmix):
        at = slice(c, c + size)
        rat = slice(D + Z + c, D + Z + c + size)
        zat = slice(Z + c, Z + c + size)
        sum_r = jnp.zeros((1, size), F32)
        sum_v = jnp.zeros((1, size), F32)
        for b, rows in enumerate(pairs):
            r = r_ref[rows, at]
            v = v_ref[rows, at]
            sr = sig(r)
            sv = sig(v)
            value = (v * sv).astype(BF16)
            datt = (dmix[rows] * (r * sr)).astype(BF16)
            dr = (dmix[rows] * slope_of(r, sr) * dot_nn(double[b], value)).astype(BF16)
            db_ref[rows, zat] = dr
            sum_r += jnp.sum(dr.astype(F32), axis=0, keepdims=True)
            wide[b] += dot_nt(datt, value)
            dv = (dot_tn(double[b], datt) * slope_of(v, sv)).astype(BF16)
            dv_ref[rows, at] = dv
            sum_v += jnp.sum(dv.astype(F32), axis=0, keepdims=True)
        sm_ref[:, rat] += sum_r
        sv_ref[:, at] += sum_v

    def give(c):
        at = slice(c, c + size)
        rat = slice(D + Z + c, D + Z + c + size)
        zat = slice(Z + c, Z + c + size)
        acc[...] += dot_nt(db_ref[:, zat], wm[:, rat])
        do_ref[...] += dot_nt(dv_ref[:, at], wv[:, at])

    starts = list(range(0, V, size))
    dmix = head(starts[0])
    acc[...] = dot_nt(dum_ref[:, :D], wm[:, :D]) + dot_nt(dum_ref[:, D:], wm[:, last:])
    do_ref[...] = dt_ref[...]
    chunk(starts[0], dmix)
    for n, c in enumerate(starts[1:]):
        dmix = head(c)
        give(starts[n])
        chunk(c, dmix)
    add_sums(sm_ref, slice(0, D), dum_ref[:, :D].astype(F32))
    add_sums(sm_ref, slice(last, D + last), dum_ref[:, D:].astype(F32))
    for b, rows in enumerate(blocks):
        z = z_ref[rows, :]
        sz = sig(z)
        shared = z * sz
        query = (shared * qk_ref[0:1, :] + qk_ref[2:3, :]).astype(BF16)
        key = (shared * qk_ref[1:2, :]).astype(BF16)
        side = slice(b % 2 * BLOCK, b % 2 * BLOCK + BLOCK)
        dprob = wide[b // 2][side, side]
        inner = jnp.sum(full[b] * dprob, axis=-1, keepdims=True)
        ds = (full[b] * (dprob - inner)).astype(BF16)
        ss_ref[...] += ds.astype(F32)
        dq = dot_nn(ds, key) * Z ** (-0.5)
        dk = dot_tn(ds, query) * Z ** (-0.5)
        sq_ref[0:1, :] += jnp.sum(dq * shared, axis=0, keepdims=True)
        sq_ref[1:2, :] += jnp.sum(dk * shared, axis=0, keepdims=True)
        sq_ref[2:3, :] += jnp.sum(dq, axis=0, keepdims=True)
        dz = (dq * qk_ref[0:1, :] + dk * qk_ref[1:2, :]) * slope_of(z, sz)
        dz = dz.astype(BF16)
        db_ref[rows, :Z] = dz
        add_sums(sm_ref, slice(D, D + Z), dz.astype(F32))
    give(starts[-1])
    dxp_ref[...] = (acc[...] + dot_nt(db_ref[:, :Z], wm[:, D : D + Z])).astype(BF16)

    @pl.when(pl.program_id(0) == pl.num_programs(0) - 1)
    def _():
        moved = jnp.concatenate([ss_ref[...].T, jnp.zeros((BLOCK, BLOCK), F32)], axis=1)
        row = lax.broadcasted_iota(jnp.int32, moved.shape, 0)
        step = 1
        while step < BLOCK:
            moved = jnp.where(jnp.bitwise_and(row, step) == 0, pltpu.roll(moved, step, 1), moved)
            step *= 2
        spots = sum_spots(D, Z, V, sf_ref.shape[1])
        sums = {
            "mix": sm_ref[...], "value": sv_ref[...], "ffn": sf_ref[...], "rel": jnp.sum(moved, axis=0, keepdims=True),
            "qk": jnp.concatenate([sq_ref[k : k + 1, :] for k in range(3)], axis=1),
            "rows": jnp.concatenate([sd_ref[k : k + 1, :] for k in range(5)], axis=1),
        }
        all_ref[...] = jnp.zeros_like(all_ref)
        for name, start, row, col, size in spots:
            all_ref[row : row + 1, col : col + size] = sums[name][:, start : start + size]


def cost_of(flops, microseconds):
    return pl.CostEstimate(flops=flops, bytes_accessed=microseconds * 3_600_000, transcendentals=0)


def any_specs(n):
    return [pl.BlockSpec(memory_space=pl.ANY)] * n


def tile(R, n):
    return pl.BlockSpec((R, n), lambda t: (t, 0))


def fixed(r, n):
    return pl.BlockSpec((r, n), lambda t: (0, 0))


def shape(r, n, dtype=F32):
    return jax.ShapeDtypeStruct((r, n), dtype)


def mix_forward(R, x, xp, bm, bv, qk, rel, pieces):
    T, D = x.shape
    V = bv.shape[1]
    Z = qk.shape[1]
    E = bm.shape[1]
    return pl.pallas_call(
        functools.partial(mix_fwd_kernel, R, (D, Z, V)),
        grid=(T // R,),
        in_specs=[tile(R, D), tile(R, D), fixed(1, E), fixed(1, V), fixed(8, Z), fixed(BLOCK, BLOCK)]
        + any_specs(18),
        out_specs=[
            tile(R, D), tile(R, D), tile(R, V), tile(R, V), tile(R, Z), tile(R, BLOCK), tile(R, V),
            pl.BlockSpec((D, R), lambda t: (0, t)),
        ],
        out_shape=[
            shape(T, D), shape(T, D), shape(T, V), shape(T, V), shape(T, Z), shape(T, BLOCK), shape(T, V, BF16),
            shape(D, T, BF16),
        ],
        scratch_shapes=[
            pltpu.VMEM((D, E), BF16), pltpu.VMEM((D, V), BF16), pltpu.VMEM((V, D), BF16),
            pltpu.SemaphoreType.DMA((18,)),
        ],
        compiler_params=pltpu.CompilerParams(vmem_limit_bytes=VMEM_LIMIT),
        cost_estimate=cost_of(2 * T * D * (E + 2 * V), 33),
        name="mix_forward",
    )(x, xp, bm, bv, qk, rel, *pieces)


def ffn_both(R, L, x, u, h, cot, lengths, norms, bf, bo, pieces):
    T, D = x.shape
    FF = bf.shape[1]
    return pl.pallas_call(
        functools.partial(ffn_kernel, R, (D, FF, L)),
        grid=(T // R,),
        in_specs=[
            tile(R, D), tile(R, D), tile(R, D), tile(R, D), pl.BlockSpec(memory_space=pltpu.SMEM),
            fixed(8, D), fixed(1, FF), fixed(1, D)]
        + any_specs(8),
        out_specs=[
            tile(R, D), tile(R, D), tile(R, FF), tile(R, D), tile(R, FF), tile(R, 2 * D), tile(R, D),
            fixed(8, D), fixed(1, FF),
        ],
        out_shape=[
            shape(T, D, BF16), shape(T, D, BF16), shape(T, FF, BF16), shape(T, D, BF16), shape(T, FF, BF16),
            shape(T, 2 * D, BF16), shape(T, D), shape(8, D), shape(1, FF),
        ],
        scratch_shapes=[
            pltpu.VMEM((D, FF), BF16), pltpu.VMEM((FF, D), BF16), pltpu.VMEM((R, FF), F32), pltpu.VMEM((R, D), F32),
            pltpu.VMEM((R, D), F32), pltpu.VMEM((R, 128), F32), pltpu.SemaphoreType.DMA((12,)),
        ],
        compiler_params=pltpu.CompilerParams(vmem_limit_bytes=VMEM_LIMIT),
        cost_estimate=cost_of(2 * T * D * 4 * FF, 50),
        name="ffn_both",
    )(x, u, h, cot, lengths, norms, bf, bo, *pieces)


def mix_backward(R, dum, dt, r, v, z, p, qk, sum_d, sum_f, pieces):
    T, D = dt.shape
    V = r.shape[1]
    Z = qk.shape[1]
    E = 2 * D + Z + V
    return pl.pallas_call(
        functools.partial(mix_bwd_kernel, R, (D, Z, V)),
        grid=(T // R,),
        in_specs=[
            tile(R, 2 * D), tile(R, D), tile(R, V), tile(R, V), tile(R, Z), tile(R, BLOCK), fixed(8, Z),
            fixed(8, D), fixed(1, sum_f.shape[1]),
        ]
        + any_specs(18),
        out_specs=[
            tile(R, Z + V), tile(R, V), tile(R, D), tile(R, D), fixed(16, D),
        ],
        out_shape=[
            shape(T, Z + V, BF16), shape(T, V, BF16), shape(T, D, BF16), shape(T, D), shape(16, D),
        ],
        scratch_shapes=[
            pltpu.VMEM((1, E), F32), pltpu.VMEM((1, V), F32), pltpu.VMEM((8, Z), F32), pltpu.VMEM((BLOCK, BLOCK), F32),
            pltpu.VMEM((D, E), BF16), pltpu.VMEM((D, V), BF16), pltpu.VMEM((V, D), BF16), pltpu.VMEM((R, D), F32),
            pltpu.SemaphoreType.DMA((18,)),
        ],
        compiler_params=pltpu.CompilerParams(vmem_limit_bytes=VMEM_LIMIT),
        cost_estimate=cost_of(2 * T * D * (E + 2 * V), 40),
        name="mix_backward",
    )(dum, dt, r, v, z, p, qk, sum_d, sum_f, *pieces)


def exchange(value, axis, step):
    return lax.ppermute(value, axis, [(k, k ^ step) for k in range(lax.axis_size(axis))])


def join(*values):
    return lax.optimization_barrier(values)


def own_half(own):
    half = own.shape[0] // 2
    return lax.dynamic_slice_in_dim(own, lax.rem(lax.axis_index("seq"), 2) * half, half, 0)


def over_x(value):
    return exchange(value, "wsh", 2)


def over_y(value):
    return exchange(value, "seq", 1)


def over_core(value):
    return exchange(value, "wsh", 1)


def gather_small(own):
    j = lax.axis_index("wsh")
    four = jnp.stack([own] + [exchange(own, "wsh", d) for d in range(1, 4)])
    return jnp.stack([lax.dynamic_index_in_dim(four, j ^ k, 0, False) for k in range(4)])


class Carry:
    def __init__(self, states, decay, reverse):
        self.entry, self.total = jnp.zeros_like(states), states
        self.own, self.window, self.reverse = jnp.ones_like(decay), decay, reverse

    def send(self, step):
        return exchange(self.total, "seq", step)

    def add(self, step, sent):
        bit = lax.rem(lax.axis_index("seq") // step, 2)
        later = (bit == 0) if self.reverse else (bit == 1)
        self.entry = jnp.where(later, self.entry + self.own * sent, self.entry)
        self.total = jnp.where(later, self.total + self.window * sent, sent + self.window * self.total)
        self.own = jnp.where(later, self.own * self.window, self.own)
        self.window = self.window * self.window


def pick(value, dim, bit):
    return lax.dynamic_index_in_dim(value, bit, dim, False)


def send_half(value, dim, mark):
    axis, step = mark
    bit = lax.rem(lax.axis_index(axis) // step, 2)
    return exchange(pick(value, dim, 1 - bit).astype(BF16), axis, step), pick(value, dim, bit)


def add_half(sent, kept):
    return kept + sent.astype(F32)


def seq_steps():
    return [2**k for k in range(lax.axis_size("seq").bit_length() - 1)]


def send_core(grad):
    rows, cols = grad.shape
    bits = (2,) * len(seq_steps())
    rest = rows // lax.axis_size("wsh") // lax.axis_size("seq")
    return send_half(grad.reshape((2, 2) + bits + (rest, cols)), 1, ("wsh", 1))


def merge(parts, cols):
    pieces = []
    for part in parts:
        for c in range(0, part.shape[-1], cols):
            pieces.append(part[..., c : c + cols])
    return jnp.concatenate(pieces, axis=-2)


class Sum:
    def __init__(self, value):
        self.value = value
        self.marks = [("wsh", 2)] + [("seq", s) for s in reversed(seq_steps())]

    def send(self, mark):
        dim = self.marks.index(mark)
        self.marks.pop(dim)
        sent, self.kept = send_half(self.value, dim, mark)
        return sent

    def add(self, sent):
        self.value = add_half(sent, self.kept)


def widen(block, other, step):
    bit = lax.rem(lax.axis_index("seq") // step, 2)
    first = jnp.where(bit == 0, block, other)
    second = jnp.where(bit == 0, other, block)
    return jnp.concatenate([first, second], axis=0)


def in_order(block):
    bits = block.shape[0].bit_length() - 1
    split = block.reshape((2,) * bits + block.shape[1:])
    turned = split.transpose(tuple(reversed(range(bits))) + (bits, bits + 1))
    return turned.reshape(block.shape)


def sum_over_wsh(value):
    j = lax.axis_index("wsh")
    total = lax.dynamic_index_in_dim(value, j, 0, False)
    for d in range(1, 4):
        total = total + exchange(lax.dynamic_index_in_dim(value, j ^ d, 0, False), "wsh", d)
    return total


def sum_over_seq(total):
    for step in reversed(seq_steps()):
        total = total + exchange(total, "seq", step)
    return total


def body(
    tokens, cotangent, lengths, ema_alpha, ema_delta, ema_beta, ema_eta, ema_omega, mix_weight, mix_bias,
    value_weight, value_bias, qk_gain, qk_bias, rel_bias, out_weight, norm_gain, norm_bias, ffn_in, ffn_in_bias,
    ffn_out, ffn_out_bias,
):
    micro, seqs, L, D = tokens.shape
    G = micro * seqs
    T = G * L
    H = ema_alpha.shape[1]
    R = min(512, T)
    n_wsh = lax.axis_size("wsh")
    i = lax.axis_index("seq")
    Z = qk_gain.shape[0] * n_wsh
    V = value_weight.shape[1]
    FF = ffn_in.shape[1]

    flat_parts = (mix_bias, value_bias, ffn_in_bias, rel_bias, qk_gain[:, 0], qk_gain[:, 1], qk_bias)
    flat = jnp.concatenate(flat_parts).reshape(ema_alpha.shape[0], -1)
    chan = jnp.concatenate(
        [ema_alpha, ema_delta, ema_beta, ema_eta, ema_omega[:, None], norm_gain, norm_bias, ffn_out_bias[:, None], flat],
        axis=1,
    )
    chan, o_mix, o_value, o_out, o_in, o_fout = join(chan, mix_weight, value_weight, out_weight, ffn_in, ffn_out)
    chan = gather_small(chan)
    flat = chan[:, :, 4 * H + 6 :].reshape(n_wsh, -1).astype(F32)
    chan = chan[:, :, : 4 * H + 6].reshape(D, -1).T.astype(F32)
    rate = jax.nn.sigmoid(chan[0:H])
    damp = jax.nn.sigmoid(chan[H : 2 * H])
    beta = chan[2 * H : 3 * H]
    eta = chan[3 * H : 4 * H]
    omega = chan[4 * H : 4 * H + 1]
    keep = 1.0 - rate * damp
    weight = eta * beta * rate
    decay = power(keep, L)
    inward = eta * beta * rate
    x3 = tokens.reshape(G, L, D)
    x = tokens.reshape(T, D)
    y_step, z_steps = ("seq", 1), [("seq", s) for s in seq_steps()[1:]]
    x_step = ("wsh", 2)
    sixth = D // LANES // 6
    steps = seq_steps()
    third = D // LANES // 3

    x_mix = over_x(own_half(o_mix))
    c_mix, c_value = over_core(o_mix), over_core(o_value)
    ends, slice_end = ema_ends(x3, keep)
    ends, slice_end, c_mix, c_value, o_value, o_out = join(ends, slice_end, c_mix, c_value, o_value, o_out)
    x_value, x_out = over_x(own_half(o_value)), over_x(own_half(o_out))
    entry = Carry(slice_end, decay, False)
    sent, x_mix, chan, flat, rate, damp, inward, keep_later = join(
        entry.send(steps[0]), x_mix, chan, flat, rate, damp, inward, keep
    )
    vectors, start = [], 0
    for part in flat_parts:
        vectors.append(flat[:, start : start + part.shape[0]].reshape(1, -1))
        start += part.shape[0]
    bm, bv, bf, rel, gain_q, gain_k, shift_q = vectors
    norms = jnp.concatenate([chan[4 * H + 1 : 4 * H + 5], jnp.zeros((4, D), F32)])
    bo = chan[4 * H + 5 : 4 * H + 6]
    qk = jnp.concatenate([gain_q, gain_k, shift_q, jnp.zeros((5, Z), F32)])
    rel_matrix = skew_matrix(jnp.roll(rel[0, ::-1], BLOCK))
    inverse = 1.0 / keep_later
    factors = jnp.concatenate(
        [
            inward * (1.0 - rate), -inward * (1.0 - rate) * damp * rate, -inward * rate * damp * (1.0 - damp),
            rate * eta, rate * beta,
        ]
    )
    entry.add(steps[0], sent)
    y_mix, xc_mix = over_y(x_mix), over_core(x_mix)
    for step in steps[1:]:
        entry.add(step, entry.send(step))
    state_in, x_value, xc_mix, rel_matrix, norms, bo, qk, inverse, factors, bm = join(
        entry.entry, x_value, xc_mix, rel_matrix, norms, bo, qk, inverse, factors, bm
    )
    y_value, xc_value = over_y(x_value), over_core(x_value)
    so_far = ema_forward((0, third), (), x3, keep, weight, omega, ends, state_in)
    *so_far, y_mix, x_out, xc_value, o_out, o_in, o_fout = join(*so_far, y_mix, x_out, xc_value, o_out, o_in, o_fout)
    y_out, xc_out, yc_mix = over_y(x_out), over_core(x_out), over_core(y_mix)
    c_out = over_core(o_out)
    x_in = over_x(o_in)
    xp, pre, finals = ema_forward((third, 2 * third), tuple(so_far), x3, keep, weight, omega, ends, state_in)
    xp, y_value, y_out, xc_out, yc_mix, c_out, o_fout = join(xp, y_value, y_out, xc_out, yc_mix, c_out, o_fout)
    yc_value, yc_out = over_core(y_value), over_core(y_out)
    x_fout = over_x(o_fout)
    mix_pieces = (
        (o_mix, c_mix, x_mix, y_mix, xc_mix, yc_mix) + (o_value, c_value, x_value, y_value, xc_value, yc_value)
        + (o_out, c_out, x_out, y_out, xc_out, yc_out)
    )
    c_in, c_fout = over_core(o_in), over_core(o_fout)
    xp = xp.reshape(T, D)
    forward = mix_forward(min(256, T), x, xp, bm, bv, qk, rel_matrix, mix_pieces)
    (u, h, r, v, z, p, mixed, xt), x_in, x_fout, c_in, c_fout = join(forward, x_in, x_fout, c_in, c_fout)
    ffn_pieces = (o_in, c_in, x_in, over_core(x_in)) + (o_fout, c_fout, x_fout, over_core(x_fout))
    output, h1, act, dg, df, dum, dt, sum_d, sum_f = ffn_both(
        R, L, x, u, h, cotangent.reshape(T, D), lengths.reshape(G), norms, bf, bo, ffn_pieces
    )

    (sent_1, kept_1), (sent_2, kept_2) = send_core(dot_rows(act, dg)), send_core(dot_rows(h1, df))
    (sent_3, kept_3), (sent_4, kept_4) = send_core(dot_rows(mixed, dum[:, D:])), send_core(dot_nn(xt, dum))
    kept_3, kept_4, sent_1, sent_2 = join(kept_3, kept_4, sent_1, sent_2)
    sum_a = Sum(merge([add_half(sent_1, kept_1), add_half(sent_2, kept_2)], D))
    over_a = sum_a.send(x_step)
    sum_b = Sum(merge([add_half(sent_3, kept_3), add_half(sent_4, kept_4)], D))
    over_b = sum_b.send(y_step)
    back = mix_backward(min(256, T), dum, dt, r, v, z, p, qk, sum_d, sum_f, mix_pieces)
    (db, dv, dxp, dtok, early), over_a, over_b = join(back, over_a, over_b)
    sum_a.add(over_a)
    sum_b.add(over_b)
    over_a, over_b = sum_a.send(y_step), sum_b.send(x_step)
    sent_1, kept_1 = send_core(dot_nn(xt, db))
    dxp, kept_1, over_a, over_b = join(dxp, kept_1, over_a, over_b)
    sum_a.add(over_a)
    sum_b.add(over_b)
    rows_a = sum_a.value.shape[-2]
    sum_a.value = jnp.concatenate([sum_a.value, sum_b.value], axis=-2)
    over_a = sum_a.send(z_steps[0])
    dpe, back_ends, slice_start = ema_back_ends(dxp.reshape(G, L, D), pre, keep)
    dpe, back_ends, slice_start, over_a, sent_1, dv = join(dpe, back_ends, slice_start, over_a, sent_1, dv)
    sum_a.add(over_a)
    sum_c = Sum(add_half(sent_1, kept_1))
    over_a = sum_a.send(z_steps[1])
    entry = Carry(slice_start, decay, True)
    sent = entry.send(steps[0])
    sent_2, kept_2 = send_core(dot_rows(x, dv))
    kept_2, sent, over_a = join(kept_2, sent, over_a)
    over_c = sum_c.send(x_step)
    entry.add(steps[0], sent)
    sent, sent_2 = join(entry.send(steps[1]), sent_2)
    entry.add(steps[1], sent)
    sum_d_ = Sum(add_half(sent_2, kept_2))
    over_d = sum_d_.send(y_step)
    for step in steps[2:]:
        entry.add(step, entry.send(step))
    state_in = entry.entry
    consts = (dpe, x3, keep, inverse, weight, omega, finals, back_ends, state_in, dtok.reshape(G, L, D), factors)
    order = list(reversed(steps))

    def back_part(k, so_far):
        return ema_backward((k * sixth, sixth), tuple(so_far), *consts)

    so_far = back_part(0, ())
    *so_far, over_a, over_c = join(*so_far, over_a, over_c)
    sum_a.add(over_a)
    for mark in z_steps[2:]:
        sum_a.add(sum_a.send(mark))
    sum_c.add(over_c)
    over_c = sum_c.send(y_step)
    block = sum_a.value.astype(BF16)[None]
    more = exchange(block, "seq", order[0])
    so_far = back_part(1, so_far)
    *so_far, over_c, over_d, more = join(*so_far, over_c, over_d, more)
    sum_c.add(over_c)
    sum_d_.add(over_d)
    over_d = sum_d_.send(x_step)
    block = widen(block, more, order[0])
    more = exchange(block, "seq", order[1])
    so_far = back_part(2, so_far)
    *so_far, over_d, more = join(*so_far, over_d, more)
    sum_d_.add(over_d)
    *so_far, block = join(*so_far, widen(block, more, order[1]))
    more = exchange(block, "seq", order[2])
    cols_c = sum_c.value.shape[-1]
    sum_c.value = jnp.concatenate([sum_c.value, sum_d_.value], axis=-1)
    over_c = sum_c.send(z_steps[0])
    so_far = back_part(3, so_far)
    *so_far, over_c = join(*so_far, over_c)
    sum_c.add(over_c)
    over_c = sum_c.send(z_steps[1])
    so_far = back_part(4, so_far)
    *so_far, over_c = join(*so_far, over_c)
    sum_c.add(over_c)
    for mark in z_steps[2:]:
        sum_c.add(sum_c.send(mark))
    small = sum_c.value.astype(BF16)[None]
    over_c = exchange(small, "seq", order[0])
    so_far = back_part(5, so_far)
    *so_far, over_c, more = join(*so_far, over_c, more)
    small = widen(small, over_c, order[0])
    block = widen(block, more, order[2])
    for step in order[3:]:
        block = widen(block, exchange(block, "seq", step), step)
    input_grad, late = so_far
    over_c = exchange(small, "seq", order[1])
    late = late.reshape(-1, n_wsh, D // n_wsh).transpose(1, 0, 2)
    sides = jnp.concatenate([early[:, k : k + D // n_wsh] for k in range(0, D, D // n_wsh)])
    late = jnp.concatenate([late, jnp.broadcast_to(sides, (n_wsh,) + sides.shape)], axis=1)
    late, over_c = join(sum_over_wsh(late), over_c)
    small = widen(small, over_c, order[1])
    over_c = exchange(small, "seq", order[2])
    late, over_c = join(sum_over_seq(late), over_c)
    small = widen(small, over_c, order[2])
    for step in order[3:]:
        small = widen(small, exchange(small, "seq", step), step)
    block, small = in_order(block), in_order(small)
    g_a, g_b = block[:, :rows_a].reshape(-1, D).astype(F32), block[:, rows_a:].reshape(-1, D).astype(F32)
    small = small.reshape(-1, small.shape[-1]).astype(F32)
    g_c, g_d = small[:, :cols_c], small[:, cols_c:]
    input_grad = input_grad.reshape(tokens.shape)

    FF = ffn_in.shape[1]
    sides = late[4 * H + 8 :].reshape(n_wsh, 16, -1)
    early = jnp.concatenate([sides[k] for k in range(n_wsh)], axis=1)
    spans = {}
    for name, start, row, col, size in sum_spots(D, Z, V, FF):
        spans[name, start] = early[row, col : col + size]

    def span_of(name):
        return jnp.concatenate([spans[key] for key in sorted(spans) if key[0] == name])

    j = lax.axis_index("wsh")
    qk_sums, row_sums = span_of("qk"), span_of("rows")
    smalls = []
    for part in (
        span_of("mix"), span_of("value"), span_of("ffn"), span_of("rel"),
        *(qk_sums[k * Z : k * Z + Z] for k in range(3)), *(row_sums[k * D : k * D + D] for k in range(5)),
    ):
        size = part.shape[0] // n_wsh
        smalls.append(lax.dynamic_slice(part, (j * size,), (size,)))
    (
        g_mix_bias, g_value_bias, g_ffn_in_bias, g_rel, g_gain_q, g_gain_k, g_shift, gain_1, gain_2, shift_1, shift_2,
        g_ffn_out_bias,
    ) = smalls
    late = late[: 4 * H + 1].T
    tall_rows, wide_rows = ffn_out.shape[0], ffn_in.shape[0]
    n_seq = lax.axis_size("seq")
    first_rows = tall_rows // n_seq

    def unmerge(merged):
        parts = merged.reshape(n_seq, -1, D)
        top = parts[:, :first_rows].reshape(tall_rows, D)
        sides = parts[:, first_rows:].reshape(n_seq, 2, wide_rows // n_seq, D)
        return top, jnp.concatenate([sides[:, k].reshape(wide_rows, D) for k in range(2)], axis=1)

    g_ffn_out, g_ffn_in = unmerge(g_a)
    g_out, g_edges = unmerge(g_b)
    g_mix = jnp.concatenate([g_edges[:, :D], g_c, g_edges[:, D:]], axis=1)
    return (
        output.reshape(tokens.shape), input_grad,
        late[:, 0:H], late[:, H : 2 * H], late[:, 2 * H : 3 * H], late[:, 3 * H : 4 * H], late[:, 4 * H],
        g_mix, g_mix_bias, g_d, g_value_bias,
        jnp.stack([g_gain_q, g_gain_k], axis=1), g_shift, g_rel, g_out,
        jnp.stack([gain_1, gain_2], axis=1), jnp.stack([shift_1, shift_2], axis=1),
        g_ffn_in, g_ffn_in_bias, g_ffn_out, g_ffn_out_bias,
    )


def solution(mesh):
    in_specs = (
        P(None, "wsh", "seq", None),
        P(None, "wsh", "seq", None),
        P(None, "wsh"),
        P("wsh", None),
        P("wsh", None),
        P("wsh", None),
        P("wsh", None),
        P("wsh"),
        P("wsh", None),
        P("wsh"),
        P("wsh", None),
        P("wsh"),
        P("wsh", None),
        P("wsh"),
        P("wsh"),
        P("wsh", None),
        P("wsh", None),
        P("wsh", None),
        P("wsh", None),
        P("wsh"),
        P("wsh", None),
        P("wsh"),
    )
    out_specs = (
        P(None, "wsh", "seq", None),
        P(None, "wsh", "seq", None),
        P("wsh", None),
        P("wsh", None),
        P("wsh", None),
        P("wsh", None),
        P("wsh"),
        P("wsh", None),
        P("wsh"),
        P("wsh", None),
        P("wsh"),
        P("wsh", None),
        P("wsh"),
        P("wsh"),
        P("wsh", None),
        P("wsh", None),
        P("wsh", None),
        P("wsh", None),
        P("wsh"),
        P("wsh", None),
        P("wsh"),
    )
    return jax.shard_map(body, mesh=mesh, in_specs=in_specs, out_specs=out_specs, check_vma=False)
```

```python
import functools

import jax
import jax.numpy as jnp
from jax import lax
from jax.experimental import pallas as pl
from jax.experimental.pallas import tpu as pltpu
from jax.sharding import PartitionSpec as P

BLOCK = 128
LANES = 128
CH = 8
PAD = 1
CHUNK = 768
STRIP = 32
EPSILON = 1e-05
VMEM_LIMIT = 62 * 1024 * 1024
F32 = jnp.float32
BF16 = jnp.bfloat16


def dot_rows(left_op, right_op):
    return jnp.einsum("ri,rj->ij", left_op, right_op, preferred_element_type=jnp.float32)


def skew_matrix(wrapped):
    lead = wrapped.shape[:-1]
    flat = jnp.tile(wrapped, (1,) * len(lead) + (BLOCK,))[..., : BLOCK * (2 * BLOCK - 1)]
    return flat.reshape(lead + (BLOCK, 2 * BLOCK - 1))[..., :BLOCK]


def power(v, n):
    k = 1
    while k < n:
        v = v * v
        k *= 2
    return v

def rows_of(scr, s, T):
    return scr[pl.ds(s, CH, stride=T+PAD), :]

def spread(scr, v, T):
    for k in range(CH):
        scr[k*(T+PAD):k*(T+PAD)+T, :] = v[k*T:(k+1)*T, :]

def collect(scr, T):
    return jnp.concatenate([scr[k*(T+PAD):k*(T+PAD)+T, :] for k in range(CH)], axis=0)

def ends_kernel(G, H, T, x_ref, q_ref, e_ref, s_ref, *scrs):
    for g in range(G):
        spread(scrs[g], x_ref[g].astype(F32), T)
    chunk_ends(G, H, T, q_ref, e_ref, s_ref, scrs, False)


def chunk_ends(G, H, T, q_ref, e_ref, s_ref, scrs, reverse):
    q = [jnp.broadcast_to(q_ref[h:h+1, :], (CH, LANES)) for h in range(H)]

    def step(s, states):
        rows = [rows_of(scr, T - 1 - s if reverse else s, T) for scr in scrs]
        return tuple(q[n % H] * states[n] + rows[n // H] for n in range(G * H))

    zero = jnp.zeros((CH, LANES), F32)
    states = lax.fori_loop(0, T, step, (zero,) * (G * H), unroll=min(T, 16))
    for n in range(G * H):
        e_ref[n // H, n % H * CH : (n % H + 1) * CH, :] = states[n]
    qT = power(q_ref[...], T)
    for g in range(G):
        c = jnp.zeros((H, LANES), F32)
        for k in reversed(range(CH)) if reverse else range(CH):
            c = qT * c + e_ref[g, pl.ds(k, H, stride=CH), :]
        s_ref[g] = c


def fwd_kernel(H, T, x_ref, q_ref, w_ref, om_ref, e_ref, c_ref, *refs):
    xp_ref, p_ref, f_ref, scr, cs, ps = refs[-6:]
    spread(scr, x_ref[0].astype(F32), T)
    qT = power(q_ref[...], T)
    c = c_ref[0]
    for k in range(CH):
        cs[pl.ds(k,H,stride=CH), :] = c
        c = qT*c + e_ref[0, pl.ds(k,H,stride=CH), :]
    q = [jnp.broadcast_to(q_ref[h:h+1, :], (CH, LANES)) for h in range(H)]
    w = [jnp.broadcast_to(w_ref[h:h+1, :], (CH, LANES)) for h in range(H)]
    om = jnp.broadcast_to(om_ref[...], (CH,LANES))
    def step(s, st):
        xs = rows_of(scr, s, T)
        st = tuple(q[h]*st[h] + xs for h in range(H))
        terms = [w[h]*st[h] for h in range(H)]
        while len(terms) > 1:
            terms = [terms[i]+terms[i+1] for i in range(0,len(terms)-1,2)] + ([terms[-1]] if len(terms)%2 else [])
        ps[pl.ds(s, CH, stride=T+PAD), :] = terms[0] + om*xs
        return st
    st = lax.fori_loop(0, T, step, tuple(cs[h*CH:(h+1)*CH, :] for h in range(H)), unroll=min(T, 32))
    for h in range(H):
        f_ref[0, h*CH:(h+1)*CH, :] = st[h]
    p = collect(ps, T)
    p_ref[0] = p
    xp_ref[0] = (p*jax.nn.sigmoid(p)).astype(xp_ref.dtype)

def bends_kernel(G, H, T, dxp_ref, p_ref, q_ref, d_ref, e_ref, s_ref, *scrs):
    for g in range(G):
        p = p_ref[g]
        sg = jax.nn.sigmoid(p)
        d = dxp_ref[g].astype(F32) * (sg*(1.0+p*(1.0-sg)))
        d_ref[g] = d
        spread(scrs[g], d, T)
    chunk_ends(G, H, T, q_ref, e_ref, s_ref, scrs, True)


def bwd_kernel(H, T, d_ref, x_ref, q_ref, qi_ref, w_ref, om_ref, f_ref, e_ref, c_ref, t_ref, k_ref, *refs):
    dx_ref, out_ref, s1_ref, s3_ref, go_ref, scr, cs, dx, ds = refs[-9:]
    g = pl.program_id(1)
    x = x_ref[0].astype(F32)
    spread(scr, x, T)
    dv = d_ref[0]
    spread(ds, dv, T)
    qT = power(q_ref[...], T)
    c = c_ref[0]
    for k in reversed(range(CH)):
        cs[pl.ds(k,H,stride=CH), :] = c
        c = qT*c + e_ref[0, pl.ds(k,H,stride=CH), :]
    om = jnp.broadcast_to(om_ref[...], (CH,LANES))
    HH = H//2
    zero = jnp.zeros((CH,LANES),F32)
    @pl.when(g==0)
    def _():
        go_ref[...] = jnp.zeros_like(go_ref)
        s1_ref[...] = jnp.zeros_like(s1_ref)
        s3_ref[...] = jnp.zeros_like(s3_ref)
    go_ref[...] += jnp.sum(dv*x, axis=0, keepdims=True)
    for half in range(2):
        hs = range(half*HH, half*HH+HH)
        q = [jnp.broadcast_to(q_ref[h:h+1, :], (CH, LANES)) for h in hs]
        qi = [jnp.broadcast_to(qi_ref[h:h+1, :], (CH, LANES)) for h in hs]
        w = [jnp.broadcast_to(w_ref[h:h+1, :], (CH, LANES)) for h in hs]
        def step(s, carry):
            l, st, a1, a3 = carry
            at = pl.ds(T-1-s, CH, stride=T+PAD)
            d = ds[at, :]
            xs = scr[at, :]
            a1 = tuple(a1[i] + d*st[i] for i in range(HH))
            l = tuple(q[i]*l[i] + d for i in range(HH))
            st = tuple((st[i]-xs)*qi[i] for i in range(HH))
            a3 = tuple(a3[i] + l[i]*st[i] for i in range(HH))
            terms = [w[i]*l[i] for i in range(HH)]
            while len(terms) > 1:
                terms = [terms[i]+terms[i+1] for i in range(0,len(terms)-1,2)]
            if half == 0:
                dx[at, :] = terms[0] + om*d
            else:
                dx[at, :] = dx[at, :] + terms[0]
            return l, st, a1, a3
        init = (tuple(cs[h*CH:(h+1)*CH,:] for h in hs), tuple(f_ref[0,h*CH:(h+1)*CH,:] for h in hs), (zero,)*HH, (zero,)*HH)
        l, st, a1, a3 = lax.fori_loop(0, T, step, init, unroll=min(T, 16))
        for i,h in enumerate(hs):
            s1_ref[h:h+1,:] += jnp.sum(a1[i],axis=0,keepdims=True)
            s3_ref[h:h+1,:] += jnp.sum(a3[i],axis=0,keepdims=True)
    dx_ref[0] = (t_ref[0] + collect(dx, T).astype(dx_ref.dtype).astype(F32)).astype(dx_ref.dtype)

    @pl.when(g == pl.num_programs(1) - 1)
    def _():
        s1, s3 = s1_ref[...], s3_ref[...]
        out_ref[0:H, :] = k_ref[0:H, :] * s1 + k_ref[H : 2 * H, :] * s3
        out_ref[H : 2 * H, :] = k_ref[2 * H : 3 * H, :] * s3
        out_ref[2 * H : 3 * H, :] = k_ref[3 * H : 4 * H, :] * s1
        out_ref[3 * H : 4 * H, :] = k_ref[4 * H : 5 * H, :] * s1
        out_ref[4 * H : 4 * H + 8, :] = jnp.broadcast_to(go_ref[...], (8, LANES))


def specs(L, H, first=0):
    blk = pl.BlockSpec((1, L, LANES), lambda c, g: (g, 0, c + first))
    par = pl.BlockSpec((H, LANES), lambda c, g: (0, c + first))
    one = pl.BlockSpec((1, LANES), lambda c, g: (0, c + first))
    st = pl.BlockSpec((1, H * CH, LANES), lambda c, g: (g, 0, c + first))
    car = pl.BlockSpec((1, H, LANES), lambda c, g: (g, 0, c + first))
    return blk, par, one, st, car


def all_specs(G, L, H):
    blk = pl.BlockSpec((G, L, LANES), lambda c: (0, 0, c))
    par = pl.BlockSpec((H, LANES), lambda c: (0, c))
    st = pl.BlockSpec((G, H * CH, LANES), lambda c: (0, 0, c))
    car = pl.BlockSpec((G, H, LANES), lambda c: (0, 0, c))
    return blk, par, st, car


def ema_ends(x, q):
    G, L, C = x.shape
    H = q.shape[0]
    blk, par, st, car = all_specs(G, L, H)
    return pl.pallas_call(
        functools.partial(ends_kernel, G, H, L // CH),
        grid=(C // LANES,),
        in_specs=[blk, par],
        out_specs=[st, car],
        out_shape=[jax.ShapeDtypeStruct((G, H * CH, C), F32), jax.ShapeDtypeStruct((G, H, C), F32)],
        scratch_shapes=[pltpu.VMEM((L + CH * PAD, LANES), F32)] * G,
        cost_estimate=cost_of(0, 11),
        name="ema_ends",
    )(x, q)


def ema_forward(span, so_far, x, q, w, om, e, c):
    G, L, C = x.shape
    H = q.shape[0]
    first, count = span
    blk, par, one, st, car = specs(L, H, first)
    return pl.pallas_call(
        functools.partial(fwd_kernel, H, L // CH),
        grid=(count, G),
        in_specs=[blk, par, par, one, st, car] + [pl.BlockSpec(memory_space=pl.ANY)] * len(so_far),
        out_specs=[blk, blk, st],
        out_shape=[
            jax.ShapeDtypeStruct((G, L, C), BF16), jax.ShapeDtypeStruct((G, L, C), F32),
            jax.ShapeDtypeStruct((G, H * CH, C), F32),
        ],
        scratch_shapes=[
            pltpu.VMEM((L + CH * PAD, LANES), F32), pltpu.VMEM((H * CH, LANES), F32),
            pltpu.VMEM((L + CH * PAD, LANES), F32),
        ],
        input_output_aliases={6 + k: k for k in range(len(so_far))},
        cost_estimate=cost_of(0, 3 * count),
        name="ema_forward",
    )(x, q, w, om, e, c, *so_far)


def ema_back_ends(dxp, p, q):
    G, L, C = p.shape
    H = q.shape[0]
    blk, par, st, car = all_specs(G, L, H)
    return pl.pallas_call(
        functools.partial(bends_kernel, G, H, L // CH),
        grid=(C // LANES,),
        in_specs=[blk, blk, par],
        out_specs=[blk, st, car],
        out_shape=[
            jax.ShapeDtypeStruct((G, L, C), F32), jax.ShapeDtypeStruct((G, H * CH, C), F32),
            jax.ShapeDtypeStruct((G, H, C), F32),
        ],
        scratch_shapes=[pltpu.VMEM((L + CH * PAD, LANES), F32)] * G,
        cost_estimate=cost_of(0, 15),
        name="ema_back_ends",
    )(dxp, p, q)


def ema_backward(span, so_far, d, x, q, qi, w, om, f, e, c, t, k):
    G, L, C = x.shape
    H = q.shape[0]
    first, count = span
    blk, par, one, st, car = specs(L, H, first)
    factors = pl.BlockSpec((5 * H, LANES), lambda c, g: (0, c + first))
    sums = pl.BlockSpec((4 * H + 8, LANES), lambda c, g: (0, c + first))
    return pl.pallas_call(
        functools.partial(bwd_kernel, H, L // CH),
        grid=(count, G),
        in_specs=[blk, blk, par, par, par, one, st, st, car, blk, factors]
        + [pl.BlockSpec(memory_space=pl.ANY)] * len(so_far),
        out_specs=[blk, sums],
        out_shape=[
            jax.ShapeDtypeStruct((G, L, C), BF16), jax.ShapeDtypeStruct((4 * H + 8, C), F32),
        ],
        scratch_shapes=[
            pltpu.VMEM((H, LANES), F32), pltpu.VMEM((H, LANES), F32), pltpu.VMEM((1, LANES), F32),
            pltpu.VMEM((L + CH * PAD, LANES), F32), pltpu.VMEM((H * CH, LANES), F32),
            pltpu.VMEM((L + CH * PAD, LANES), F32), pltpu.VMEM((L + CH * PAD, LANES), F32),
        ],
        input_output_aliases={11 + n: n for n in range(len(so_far))},
        cost_estimate=cost_of(0, 8 * count),
        name="ema_backward",
    )(d, x, q, qi, w, om, f, e, c, t, k, *so_far)


def sig(v):
    return 0.5 * jnp.tanh(0.5 * v) + 0.5


def dot_nn(left_op, right_op):
    return jnp.dot(left_op, right_op, preferred_element_type=F32)


def dot_nt(left_op, right_op):
    return lax.dot_general(left_op, right_op, (((1,), (1,)), ((), ())), preferred_element_type=F32)


def dot_tn(left_op, right_op):
    return lax.dot_general(left_op, right_op, (((0,), (0,)), ((), ())), preferred_element_type=F32)


def piece_copies(pieces, target):
    j = lax.axis_index("wsh")
    bit = lax.rem(lax.axis_index("seq"), 2)
    rows = target.shape[0] // 4
    half = rows // 2
    if len(pieces) == 4:
        starts = [(j ^ k) * rows for k in range(4)]
    else:
        low, high = bit * half, (1 - bit) * half
        starts = [j * rows, (j ^ 1) * rows]
        starts += [(j ^ 2) * rows + low, (j ^ 2) * rows + high, (j ^ 3) * rows + low, (j ^ 3) * rows + high]
    return [
        (piece, target.at[pl.ds(pl.multiple_of(start, 32), piece.shape[0]), :])
        for piece, start in zip(pieces, starts)
    ]


def bring(groups, sem):
    @pl.when(pl.program_id(0) == 0)
    def _():
        copies = []
        for pieces, target in groups:
            for source, spot in piece_copies(pieces, target):
                copies.append(pltpu.make_async_copy(source, spot, sem.at[len(copies)]))
        for copy in copies:
            copy.start()
        for copy in copies:
            copy.wait()


def fold(rows):
    total = rows[:8]
    for k in range(8, STRIP, 8):
        total = total + rows[k : k + 8]
    return total


def add_sums(ref, at, rows):
    ref[:, at] += jnp.sum(rows, axis=0, keepdims=True)


def mix_fwd_kernel(R, dims, x_ref, xp_ref, bm_ref, bv_ref, qk_ref, rel_ref, *refs):
    D, Z, V = dims
    pieces, refs = refs[:18], refs[18:]
    u_ref, h_ref, r_ref, v_ref, z_ref, p_ref, m_ref, xt_ref, wm, wv, wo, sem = refs
    bring(((pieces[:6], wm), (pieces[6:12], wv), (pieces[12:], wo)), sem)
    xp = xp_ref[...]
    x = x_ref[...]
    xt_ref[...] = xp.T
    z = dot_nn(xp, wm[:, D : D + Z]) + bm_ref[:, D : D + Z]
    z_ref[...] = z
    shared = z * sig(z)
    query = (shared * qk_ref[0:1, :] + qk_ref[2:3, :]).astype(BF16)
    key = (shared * qk_ref[1:2, :]).astype(BF16)
    probs = []
    row = lax.broadcasted_iota(jnp.int32, (BLOCK, BLOCK), 0)
    col = lax.broadcasted_iota(jnp.int32, (BLOCK, BLOCK), 1)
    for b in range(R // BLOCK):
        at = slice(b * BLOCK, (b + 1) * BLOCK)
        score = dot_nt(query[at], key[at]) * Z ** (-0.5) + rel_ref[...]
        score = jnp.where(row >= col, score, -1e30)
        grown = jnp.exp(score - jnp.max(score, axis=-1, keepdims=True))
        prob = grown / jnp.sum(grown, axis=-1, keepdims=True)
        p_ref[at, :] = prob
        probs.append(prob.astype(BF16))
    for c in range(0, V, CHUNK):
        at = slice(c, c + CHUNK)
        rat = slice(D + Z + c, D + Z + c + CHUNK)
        v = dot_nn(x, wv[:, at]) + bv_ref[:, at]
        v_ref[:, at] = v
        value = (v * sig(v)).astype(BF16)
        r = dot_nn(xp, wm[:, rat]) + bm_ref[:, rat]
        r_ref[:, at] = r
        reset = r * sig(r)
        for b in range(0, R // BLOCK, 2):
            rows = slice(b * BLOCK, (b + 2) * BLOCK)
            m_ref[rows, at] = (reset[rows] * dot_nn(pair_of(probs[b], probs[b + 1]), value[rows])).astype(BF16)
    u_ref[...] = dot_nn(xp, wm[:, :D]) + bm_ref[:, :D]
    h_ref[...] = dot_nn(xp, wm[:, D + Z + V :]) + bm_ref[:, D + Z + V :] + dot_nn(m_ref[...], wo[...])


def slope_of(pre, logistic):
    return logistic * (1.0 + pre * (1.0 - logistic))


def mean_of(rows):
    return jnp.mean(rows, axis=-1, keepdims=True)


def ffn_kernel(R, dims, x_ref, u_ref, h_ref, cot_ref, len_ref, gn_ref, bf_ref, bo_ref, *refs):
    D, FF, L = dims
    pieces, refs = refs[:8], refs[8:]
    (
        o_ref, h1_ref, act_ref, dg_ref, df_ref, dum_ref, dt_ref, sd_ref, sf_ref,
        wi, wo, f_scr, n1_scr, a_scr, i1_scr, sem,
    ) = refs
    bring(((pieces[:4], wi), (pieces[4:], wo)), sem)

    @pl.when(pl.program_id(0) == 0)
    def _():
        sd_ref[...] = jnp.zeros_like(sd_ref)
        sf_ref[...] = jnp.zeros_like(sf_ref)

    g1, g2, b1, b2 = (gn_ref[k : k + 1, :] for k in range(4))
    part = min(256, R)

    def strips(s):
        return [slice(k, k + STRIP) for k in range(s * part, (s + 1) * part, STRIP)]

    def first(s):
        for at in strips(s):
            x = x_ref[at, :].astype(F32)
            h = h_ref[at, :]
            y = x + sig(u_ref[at, :]) * (h * sig(h) - x)
            center = y - mean_of(y)
            inverse = lax.rsqrt(mean_of(center * center) + EPSILON)
            n1 = center * inverse
            n1_scr[at, :] = n1
            i1_scr[at, :] = jnp.broadcast_to(inverse, (STRIP, LANES))
            h1_ref[at, :] = (n1 * g1 + b1).astype(BF16)

    def spread(s):
        rows = slice(s * part, (s + 1) * part)
        for c in range(0, FF, CHUNK):
            at = slice(c, c + CHUNK)
            f = dot_nn(h1_ref[rows, :], wi[:, at]) + bf_ref[:, at]
            f_scr[rows, at] = f
            act_ref[rows, at] = (f * sig(f)).astype(BF16)

    def narrow(s):
        rows = slice(s * part, (s + 1) * part)
        a_scr[rows, :] = dot_nn(act_ref[rows, :], wo[...])

    def second(s):
        zero = jnp.zeros((8, D), F32)
        s_gain, s_shift, s_bias = zero, zero, zero
        for at in strips(s):
            y2 = n1_scr[at, :] * g1 + b1 + a_scr[at, :] + bo_ref[...]
            center = y2 - mean_of(y2)
            inverse = lax.rsqrt(mean_of(center * center) + EPSILON)
            n2 = center * inverse
            row = pl.program_id(0) * R + at.start
            place = lax.rem(row, L) + lax.axis_index("seq") * L
            place = place + lax.broadcasted_iota(jnp.int32, (STRIP, 1), 0)
            live = (place < len_ref[row // L]).astype(F32)
            o_ref[at, :] = ((n2 * g2 + b2) * live).astype(BF16)
            dn = cot_ref[at, :].astype(F32) * live
            w = dn * g2
            dy2 = inverse * (w - mean_of(w) - n2 * mean_of(w * n2))
            a_scr[at, :] = dy2
            dg_ref[at, :] = dy2.astype(BF16)
            s_gain, s_shift, s_bias = s_gain + fold(dn * n2), s_shift + fold(dn), s_bias + fold(dy2)
        sd_ref[1:2, :] += jnp.sum(s_gain, axis=0, keepdims=True)
        sd_ref[3:4, :] += jnp.sum(s_shift, axis=0, keepdims=True)
        sd_ref[4:5, :] += jnp.sum(s_bias, axis=0, keepdims=True)

    def spread_back(s):
        rows = slice(s * part, (s + 1) * part)
        for c in range(0, FF, CHUNK):
            at = slice(c, c + CHUNK)
            f = f_scr[rows, at]
            df = (dot_nt(dg_ref[rows, :], wo[at, :]) * slope_of(f, sig(f))).astype(BF16)
            df_ref[rows, at] = df
            add_sums(sf_ref, at, df.astype(F32))

    def narrow_back(s):
        rows = slice(s * part, (s + 1) * part)
        a_scr[rows, :] += dot_nt(df_ref[rows, :], wi[...])

    def third(s):
        zero = jnp.zeros((8, D), F32)
        s_gain, s_shift = zero, zero
        for at in strips(s):
            dh1 = a_scr[at, :]
            n1 = n1_scr[at, :]
            w = dh1 * g1
            dy = i1_scr[at, 0:1] * (w - mean_of(w) - n1 * mean_of(w * n1))
            x = x_ref[at, :].astype(F32)
            h = h_ref[at, :]
            sh = sig(h)
            gate = sig(u_ref[at, :])
            rest = 1.0 - gate
            dyg = dy * gate
            dum_ref[at, :D] = (dyg * (h * sh - x) * rest).astype(BF16)
            dum_ref[at, D:] = (dyg * slope_of(h, sh)).astype(BF16)
            dt_ref[at, :] = dy * rest
            s_gain, s_shift = s_gain + fold(dh1 * n1), s_shift + fold(dh1)
        sd_ref[0:1, :] += jnp.sum(s_gain, axis=0, keepdims=True)
        sd_ref[2:3, :] += jnp.sum(s_shift, axis=0, keepdims=True)

    stages = (first, spread, narrow, second, spread_back, narrow_back, third)
    count = R // part
    for tick in range(len(stages) + count - 1):
        for s in range(count):
            if 0 <= tick - s < len(stages):
                stages[tick - s](s)


def pair_of(top, bottom):
    none = jnp.zeros_like(top)
    return jnp.concatenate([jnp.concatenate([top, none], axis=1), jnp.concatenate([none, bottom], axis=1)], axis=0)


def sum_spots(D, Z, V, FF):
    spans = [("mix", D, Z), ("rel", 0, 2 * BLOCK), ("qk", 0, 3 * Z), ("mix", 0, D), ("mix", D + Z + V, D)]
    spans += [("mix", D + Z + k, D) for k in range(0, V, D)] + [("value", k, D) for k in range(0, V, D)]
    spans += [("ffn", k, D) for k in range(0, FF, D)] + [("rows", k * D, D) for k in range(5)]
    spots, place = [], 0
    for name, start, size in spans:
        spots.append((name, start, place // D, place % D, size))
        place += size
    return spots


def mix_bwd_kernel(R, dims, dum_ref, dt_ref, r_ref, v_ref, z_ref, p_ref, qk_ref, sd_ref, sf_ref, *refs):
    D, Z, V = dims
    pieces, refs = refs[:18], refs[18:]
    db_ref, dv_ref, dxp_ref, do_ref, all_ref, sm_ref, sv_ref, sq_ref, ss_ref, wm, wv, wo, acc, sem = refs
    bring(((pieces[:6], wm), (pieces[6:12], wv), (pieces[12:], wo)), sem)

    @pl.when(pl.program_id(0) == 0)
    def _():
        for ref in (sm_ref, sv_ref, sq_ref, ss_ref):
            ref[...] = jnp.zeros_like(ref)

    last = D + Z + V
    blocks = [slice(b * BLOCK, (b + 1) * BLOCK) for b in range(R // BLOCK)]
    full = [p_ref[rows, :] for rows in blocks]
    probs = [prob.astype(BF16) for prob in full]
    pairs = [slice(k, k + 2 * BLOCK) for k in range(0, R, 2 * BLOCK)]
    double = [pair_of(probs[2 * k], probs[2 * k + 1]) for k in range(len(pairs))]
    wide = [jnp.zeros((2 * BLOCK, 2 * BLOCK), F32) for _ in pairs]
    size = 512

    def head(c):
        return dot_nt(dum_ref[:, D:], wo[c : c + size, :])

    def chunk(c, dmix):
        at = slice(c, c + size)
        rat = slice(D + Z + c, D + Z + c + size)
        zat = slice(Z + c, Z + c + size)
        sum_r = jnp.zeros((1, size), F32)
        sum_v = jnp.zeros((1, size), F32)
        for b, rows in enumerate(pairs):
            r = r_ref[rows, at]
            v = v_ref[rows, at]
            sr = sig(r)
            sv = sig(v)
            value = (v * sv).astype(BF16)
            datt = (dmix[rows] * (r * sr)).astype(BF16)
            dr = (dmix[rows] * slope_of(r, sr) * dot_nn(double[b], value)).astype(BF16)
            db_ref[rows, zat] = dr
            sum_r += jnp.sum(dr.astype(F32), axis=0, keepdims=True)
            wide[b] += dot_nt(datt, value)
            dv = (dot_tn(double[b], datt) * slope_of(v, sv)).astype(BF16)
            dv_ref[rows, at] = dv
            sum_v += jnp.sum(dv.astype(F32), axis=0, keepdims=True)
        sm_ref[:, rat] += sum_r
        sv_ref[:, at] += sum_v

    def give(c):
        at = slice(c, c + size)
        rat = slice(D + Z + c, D + Z + c + size)
        zat = slice(Z + c, Z + c + size)
        acc[...] += dot_nt(db_ref[:, zat], wm[:, rat])
        do_ref[...] += dot_nt(dv_ref[:, at], wv[:, at])

    starts = list(range(0, V, size))
    dmix = head(starts[0])
    acc[...] = dot_nt(dum_ref[:, :D], wm[:, :D]) + dot_nt(dum_ref[:, D:], wm[:, last:])
    do_ref[...] = dt_ref[...]
    chunk(starts[0], dmix)
    for n, c in enumerate(starts[1:]):
        dmix = head(c)
        give(starts[n])
        chunk(c, dmix)
    add_sums(sm_ref, slice(0, D), dum_ref[:, :D].astype(F32))
    add_sums(sm_ref, slice(last, D + last), dum_ref[:, D:].astype(F32))
    for b, rows in enumerate(blocks):
        z = z_ref[rows, :]
        sz = sig(z)
        shared = z * sz
        query = (shared * qk_ref[0:1, :] + qk_ref[2:3, :]).astype(BF16)
        key = (shared * qk_ref[1:2, :]).astype(BF16)
        side = slice(b % 2 * BLOCK, b % 2 * BLOCK + BLOCK)
        dprob = wide[b // 2][side, side]
        inner = jnp.sum(full[b] * dprob, axis=-1, keepdims=True)
        ds = (full[b] * (dprob - inner)).astype(BF16)
        ss_ref[...] += ds.astype(F32)
        dq = dot_nn(ds, key) * Z ** (-0.5)
        dk = dot_tn(ds, query) * Z ** (-0.5)
        sq_ref[0:1, :] += jnp.sum(dq * shared, axis=0, keepdims=True)
        sq_ref[1:2, :] += jnp.sum(dk * shared, axis=0, keepdims=True)
        sq_ref[2:3, :] += jnp.sum(dq, axis=0, keepdims=True)
        dz = (dq * qk_ref[0:1, :] + dk * qk_ref[1:2, :]) * slope_of(z, sz)
        dz = dz.astype(BF16)
        db_ref[rows, :Z] = dz
        add_sums(sm_ref, slice(D, D + Z), dz.astype(F32))
    give(starts[-1])
    dxp_ref[...] = (acc[...] + dot_nt(db_ref[:, :Z], wm[:, D : D + Z])).astype(BF16)

    @pl.when(pl.program_id(0) == pl.num_programs(0) - 1)
    def _():
        moved = jnp.concatenate([ss_ref[...].T, jnp.zeros((BLOCK, BLOCK), F32)], axis=1)
        row = lax.broadcasted_iota(jnp.int32, moved.shape, 0)
        step = 1
        while step < BLOCK:
            moved = jnp.where(jnp.bitwise_and(row, step) == 0, pltpu.roll(moved, step, 1), moved)
            step *= 2
        spots = sum_spots(D, Z, V, sf_ref.shape[1])
        sums = {
            "mix": sm_ref[...], "value": sv_ref[...], "ffn": sf_ref[...], "rel": jnp.sum(moved, axis=0, keepdims=True),
            "qk": jnp.concatenate([sq_ref[k : k + 1, :] for k in range(3)], axis=1),
            "rows": jnp.concatenate([sd_ref[k : k + 1, :] for k in range(5)], axis=1),
        }
        all_ref[...] = jnp.zeros_like(all_ref)
        for name, start, row, col, size in spots:
            all_ref[row : row + 1, col : col + size] = sums[name][:, start : start + size]


def cost_of(flops, microseconds):
    return pl.CostEstimate(flops=flops, bytes_accessed=microseconds * 3_600_000, transcendentals=0)


def any_specs(n):
    return [pl.BlockSpec(memory_space=pl.ANY)] * n


def tile(R, n):
    return pl.BlockSpec((R, n), lambda t: (t, 0))


def fixed(r, n):
    return pl.BlockSpec((r, n), lambda t: (0, 0))


def shape(r, n, dtype=F32):
    return jax.ShapeDtypeStruct((r, n), dtype)


def mix_forward(R, x, xp, bm, bv, qk, rel, pieces):
    T, D = x.shape
    V = bv.shape[1]
    Z = qk.shape[1]
    E = bm.shape[1]
    return pl.pallas_call(
        functools.partial(mix_fwd_kernel, R, (D, Z, V)),
        grid=(T // R,),
        in_specs=[tile(R, D), tile(R, D), fixed(1, E), fixed(1, V), fixed(8, Z), fixed(BLOCK, BLOCK)]
        + any_specs(18),
        out_specs=[
            tile(R, D), tile(R, D), tile(R, V), tile(R, V), tile(R, Z), tile(R, BLOCK), tile(R, V),
            pl.BlockSpec((D, R), lambda t: (0, t)),
        ],
        out_shape=[
            shape(T, D), shape(T, D), shape(T, V), shape(T, V), shape(T, Z), shape(T, BLOCK), shape(T, V, BF16),
            shape(D, T, BF16),
        ],
        scratch_shapes=[
            pltpu.VMEM((D, E), BF16), pltpu.VMEM((D, V), BF16), pltpu.VMEM((V, D), BF16),
            pltpu.SemaphoreType.DMA((18,)),
        ],
        compiler_params=pltpu.CompilerParams(vmem_limit_bytes=VMEM_LIMIT),
        cost_estimate=cost_of(2 * T * D * (E + 2 * V), 33),
        name="mix_forward",
    )(x, xp, bm, bv, qk, rel, *pieces)


def ffn_both(R, L, x, u, h, cot, lengths, norms, bf, bo, pieces):
    T, D = x.shape
    FF = bf.shape[1]
    return pl.pallas_call(
        functools.partial(ffn_kernel, R, (D, FF, L)),
        grid=(T // R,),
        in_specs=[
            tile(R, D), tile(R, D), tile(R, D), tile(R, D), pl.BlockSpec(memory_space=pltpu.SMEM),
            fixed(8, D), fixed(1, FF), fixed(1, D)]
        + any_specs(8),
        out_specs=[
            tile(R, D), tile(R, D), tile(R, FF), tile(R, D), tile(R, FF), tile(R, 2 * D), tile(R, D),
            fixed(8, D), fixed(1, FF),
        ],
        out_shape=[
            shape(T, D, BF16), shape(T, D, BF16), shape(T, FF, BF16), shape(T, D, BF16), shape(T, FF, BF16),
            shape(T, 2 * D, BF16), shape(T, D), shape(8, D), shape(1, FF),
        ],
        scratch_shapes=[
            pltpu.VMEM((D, FF), BF16), pltpu.VMEM((FF, D), BF16), pltpu.VMEM((R, FF), F32), pltpu.VMEM((R, D), F32),
            pltpu.VMEM((R, D), F32), pltpu.VMEM((R, 128), F32), pltpu.SemaphoreType.DMA((12,)),
        ],
        compiler_params=pltpu.CompilerParams(vmem_limit_bytes=VMEM_LIMIT),
        cost_estimate=cost_of(2 * T * D * 4 * FF, 50),
        name="ffn_both",
    )(x, u, h, cot, lengths, norms, bf, bo, *pieces)


def mix_backward(R, dum, dt, r, v, z, p, qk, sum_d, sum_f, pieces):
    T, D = dt.shape
    V = r.shape[1]
    Z = qk.shape[1]
    E = 2 * D + Z + V
    return pl.pallas_call(
        functools.partial(mix_bwd_kernel, R, (D, Z, V)),
        grid=(T // R,),
        in_specs=[
            tile(R, 2 * D), tile(R, D), tile(R, V), tile(R, V), tile(R, Z), tile(R, BLOCK), fixed(8, Z),
            fixed(8, D), fixed(1, sum_f.shape[1]),
        ]
        + any_specs(18),
        out_specs=[
            tile(R, Z + V), tile(R, V), tile(R, D), tile(R, D), fixed(16, D),
        ],
        out_shape=[
            shape(T, Z + V, BF16), shape(T, V, BF16), shape(T, D, BF16), shape(T, D), shape(16, D),
        ],
        scratch_shapes=[
            pltpu.VMEM((1, E), F32), pltpu.VMEM((1, V), F32), pltpu.VMEM((8, Z), F32), pltpu.VMEM((BLOCK, BLOCK), F32),
            pltpu.VMEM((D, E), BF16), pltpu.VMEM((D, V), BF16), pltpu.VMEM((V, D), BF16), pltpu.VMEM((R, D), F32),
            pltpu.SemaphoreType.DMA((18,)),
        ],
        compiler_params=pltpu.CompilerParams(vmem_limit_bytes=VMEM_LIMIT),
        cost_estimate=cost_of(2 * T * D * (E + 2 * V), 40),
        name="mix_backward",
    )(dum, dt, r, v, z, p, qk, sum_d, sum_f, *pieces)


def exchange(value, axis, step):
    return lax.ppermute(value, axis, [(k, k ^ step) for k in range(lax.axis_size(axis))])


def join(*values):
    return lax.optimization_barrier(values)


def own_half(own):
    half = own.shape[0] // 2
    return lax.dynamic_slice_in_dim(own, lax.rem(lax.axis_index("seq"), 2) * half, half, 0)


def over_x(value):
    return exchange(value, "wsh", 2)


def over_y(value):
    return exchange(value, "seq", 1)


def over_core(value):
    return exchange(value, "wsh", 1)


def gather_small(own):
    j = lax.axis_index("wsh")
    four = jnp.stack([own] + [exchange(own, "wsh", d) for d in range(1, 4)])
    return jnp.stack([lax.dynamic_index_in_dim(four, j ^ k, 0, False) for k in range(4)])


class Carry:
    def __init__(self, states, decay, reverse):
        self.entry, self.total = jnp.zeros_like(states), states
        self.own, self.window, self.reverse = jnp.ones_like(decay), decay, reverse

    def send(self, step):
        return exchange(self.total, "seq", step)

    def add(self, step, sent):
        bit = lax.rem(lax.axis_index("seq") // step, 2)
        later = (bit == 0) if self.reverse else (bit == 1)
        self.entry = jnp.where(later, self.entry + self.own * sent, self.entry)
        self.total = jnp.where(later, self.total + self.window * sent, sent + self.window * self.total)
        self.own = jnp.where(later, self.own * self.window, self.own)
        self.window = self.window * self.window


def pick(value, dim, bit):
    return lax.dynamic_index_in_dim(value, bit, dim, False)


def send_half(value, dim, mark):
    axis, step = mark
    bit = lax.rem(lax.axis_index(axis) // step, 2)
    return exchange(pick(value, dim, 1 - bit).astype(BF16), axis, step), pick(value, dim, bit)


def add_half(sent, kept):
    return kept + sent.astype(F32)


def seq_steps():
    return [2**k for k in range(lax.axis_size("seq").bit_length() - 1)]


def send_core(grad):
    rows, cols = grad.shape
    bits = (2,) * len(seq_steps())
    rest = rows // lax.axis_size("wsh") // lax.axis_size("seq")
    return send_half(grad.reshape((2, 2) + bits + (rest, cols)), 1, ("wsh", 1))


def merge(parts, cols):
    pieces = []
    for part in parts:
        for c in range(0, part.shape[-1], cols):
            pieces.append(part[..., c : c + cols])
    return jnp.concatenate(pieces, axis=-2)


class Sum:
    def __init__(self, value):
        self.value = value
        self.marks = [("wsh", 2)] + [("seq", s) for s in reversed(seq_steps())]

    def send(self, mark):
        dim = self.marks.index(mark)
        self.marks.pop(dim)
        sent, self.kept = send_half(self.value, dim, mark)
        return sent

    def add(self, sent):
        self.value = add_half(sent, self.kept)


def widen(block, other, step):
    bit = lax.rem(lax.axis_index("seq") // step, 2)
    first = jnp.where(bit == 0, block, other)
    second = jnp.where(bit == 0, other, block)
    return jnp.concatenate([first, second], axis=0)


def in_order(block):
    bits = block.shape[0].bit_length() - 1
    split = block.reshape((2,) * bits + block.shape[1:])
    turned = split.transpose(tuple(reversed(range(bits))) + (bits, bits + 1))
    return turned.reshape(block.shape)


def sum_over_wsh(value):
    j = lax.axis_index("wsh")
    total = lax.dynamic_index_in_dim(value, j, 0, False)
    for d in range(1, 4):
        total = total + exchange(lax.dynamic_index_in_dim(value, j ^ d, 0, False), "wsh", d)
    return total


def sum_over_seq(total):
    for step in reversed(seq_steps()):
        total = total + exchange(total, "seq", step)
    return total


def body(
    tokens, cotangent, lengths, ema_alpha, ema_delta, ema_beta, ema_eta, ema_omega, mix_weight, mix_bias,
    value_weight, value_bias, qk_gain, qk_bias, rel_bias, out_weight, norm_gain, norm_bias, ffn_in, ffn_in_bias,
    ffn_out, ffn_out_bias,
):
    micro, seqs, L, D = tokens.shape
    G = micro * seqs
    T = G * L
    H = ema_alpha.shape[1]
    R = min(512, T)
    n_wsh = lax.axis_size("wsh")
    i = lax.axis_index("seq")
    Z = qk_gain.shape[0] * n_wsh
    V = value_weight.shape[1]
    FF = ffn_in.shape[1]

    flat_parts = (mix_bias, value_bias, ffn_in_bias, rel_bias, qk_gain[:, 0], qk_gain[:, 1], qk_bias)
    flat = jnp.concatenate(flat_parts).reshape(ema_alpha.shape[0], -1)
    chan = jnp.concatenate(
        [ema_alpha, ema_delta, ema_beta, ema_eta, ema_omega[:, None], norm_gain, norm_bias, ffn_out_bias[:, None], flat],
        axis=1,
    )
    chan, o_mix, o_value, o_out, o_in, o_fout = join(chan, mix_weight, value_weight, out_weight, ffn_in, ffn_out)
    chan = gather_small(chan)
    flat = chan[:, :, 4 * H + 6 :].reshape(n_wsh, -1).astype(F32)
    chan = chan[:, :, : 4 * H + 6].reshape(D, -1).T.astype(F32)
    rate = jax.nn.sigmoid(chan[0:H])
    damp = jax.nn.sigmoid(chan[H : 2 * H])
    beta = chan[2 * H : 3 * H]
    eta = chan[3 * H : 4 * H]
    omega = chan[4 * H : 4 * H + 1]
    keep = 1.0 - rate * damp
    weight = eta * beta * rate
    decay = power(keep, L)
    inward = eta * beta * rate
    x3 = tokens.reshape(G, L, D)
    x = tokens.reshape(T, D)
    y_step, z_steps = ("seq", 1), [("seq", s) for s in seq_steps()[1:]]
    x_step = ("wsh", 2)
    sixth = D // LANES // 6
    steps = seq_steps()
    third = D // LANES // 3

    x_mix = over_x(own_half(o_mix))
    c_mix, c_value = over_core(o_mix), over_core(o_value)
    ends, slice_end = ema_ends(x3, keep)
    ends, slice_end, c_mix, c_value, o_value, o_out = join(ends, slice_end, c_mix, c_value, o_value, o_out)
    x_value, x_out = over_x(own_half(o_value)), over_x(own_half(o_out))
    entry = Carry(slice_end, decay, False)
    sent, x_mix, chan, flat, rate, damp, inward, keep_later = join(
        entry.send(steps[0]), x_mix, chan, flat, rate, damp, inward, keep
    )
    vectors, start = [], 0
    for part in flat_parts:
        vectors.append(flat[:, start : start + part.shape[0]].reshape(1, -1))
        start += part.shape[0]
    bm, bv, bf, rel, gain_q, gain_k, shift_q = vectors
    norms = jnp.concatenate([chan[4 * H + 1 : 4 * H + 5], jnp.zeros((4, D), F32)])
    bo = chan[4 * H + 5 : 4 * H + 6]
    qk = jnp.concatenate([gain_q, gain_k, shift_q, jnp.zeros((5, Z), F32)])
    rel_matrix = skew_matrix(jnp.roll(rel[0, ::-1], BLOCK))
    inverse = 1.0 / keep_later
    factors = jnp.concatenate(
        [
            inward * (1.0 - rate), -inward * (1.0 - rate) * damp * rate, -inward * rate * damp * (1.0 - damp),
            rate * eta, rate * beta,
        ]
    )
    entry.add(steps[0], sent)
    y_mix, xc_mix = over_y(x_mix), over_core(x_mix)
    for step in steps[1:]:
        entry.add(step, entry.send(step))
    state_in, x_value, xc_mix, rel_matrix, norms, bo, qk, inverse, factors, bm = join(
        entry.entry, x_value, xc_mix, rel_matrix, norms, bo, qk, inverse, factors, bm
    )
    y_value, xc_value = over_y(x_value), over_core(x_value)
    so_far = ema_forward((0, third), (), x3, keep, weight, omega, ends, state_in)
    *so_far, y_mix, x_out, xc_value, o_out, o_in, o_fout = join(*so_far, y_mix, x_out, xc_value, o_out, o_in, o_fout)
    y_out, xc_out, yc_mix = over_y(x_out), over_core(x_out), over_core(y_mix)
    c_out = over_core(o_out)
    x_in = over_x(o_in)
    xp, pre, finals = ema_forward((third, 2 * third), tuple(so_far), x3, keep, weight, omega, ends, state_in)
    xp, y_value, y_out, xc_out, yc_mix, c_out, o_fout = join(xp, y_value, y_out, xc_out, yc_mix, c_out, o_fout)
    yc_value, yc_out = over_core(y_value), over_core(y_out)
    x_fout = over_x(o_fout)
    mix_pieces = (
        (o_mix, c_mix, x_mix, y_mix, xc_mix, yc_mix) + (o_value, c_value, x_value, y_value, xc_value, yc_value)
        + (o_out, c_out, x_out, y_out, xc_out, yc_out)
    )
    c_in, c_fout = over_core(o_in), over_core(o_fout)
    xp = xp.reshape(T, D)
    forward = mix_forward(min(256, T), x, xp, bm, bv, qk, rel_matrix, mix_pieces)
    (u, h, r, v, z, p, mixed, xt), x_in, x_fout, c_in, c_fout = join(forward, x_in, x_fout, c_in, c_fout)
    ffn_pieces = (o_in, c_in, x_in, over_core(x_in)) + (o_fout, c_fout, x_fout, over_core(x_fout))
    output, h1, act, dg, df, dum, dt, sum_d, sum_f = ffn_both(
        R, L, x, u, h, cotangent.reshape(T, D), lengths.reshape(G), norms, bf, bo, ffn_pieces
    )

    (sent_1, kept_1), (sent_2, kept_2) = send_core(dot_rows(act, dg)), send_core(dot_rows(h1, df))
    (sent_3, kept_3), (sent_4, kept_4) = send_core(dot_rows(mixed, dum[:, D:])), send_core(dot_nn(xt, dum))
    kept_3, kept_4, sent_1, sent_2 = join(kept_3, kept_4, sent_1, sent_2)
    sum_a = Sum(merge([add_half(sent_1, kept_1), add_half(sent_2, kept_2)], D))
    over_a = sum_a.send(x_step)
    sum_b = Sum(merge([add_half(sent_3, kept_3), add_half(sent_4, kept_4)], D))
    over_b = sum_b.send(y_step)
    back = mix_backward(min(256, T), dum, dt, r, v, z, p, qk, sum_d, sum_f, mix_pieces)
    (db, dv, dxp, dtok, early), over_a, over_b = join(back, over_a, over_b)
    sum_a.add(over_a)
    sum_b.add(over_b)
    over_a, over_b = sum_a.send(y_step), sum_b.send(x_step)
    sent_1, kept_1 = send_core(dot_nn(xt, db))
    dxp, kept_1, over_a, over_b = join(dxp, kept_1, over_a, over_b)
    sum_a.add(over_a)
    sum_b.add(over_b)
    rows_a = sum_a.value.shape[-2]
    sum_a.value = jnp.concatenate([sum_a.value, sum_b.value], axis=-2)
    over_a = sum_a.send(z_steps[0])
    dpe, back_ends, slice_start = ema_back_ends(dxp.reshape(G, L, D), pre, keep)
    dpe, back_ends, slice_start, over_a, sent_1, dv = join(dpe, back_ends, slice_start, over_a, sent_1, dv)
    sum_a.add(over_a)
    sum_c = Sum(add_half(sent_1, kept_1))
    over_a = sum_a.send(z_steps[1])
    entry = Carry(slice_start, decay, True)
    sent = entry.send(steps[0])
    sent_2, kept_2 = send_core(dot_rows(x, dv))
    kept_2, sent, over_a = join(kept_2, sent, over_a)
    over_c = sum_c.send(x_step)
    entry.add(steps[0], sent)
    sent, sent_2 = join(entry.send(steps[1]), sent_2)
    entry.add(steps[1], sent)
    sum_d_ = Sum(add_half(sent_2, kept_2))
    over_d = sum_d_.send(x_step)
    for step in steps[2:]:
        entry.add(step, entry.send(step))
    state_in = entry.entry
    consts = (dpe, x3, keep, inverse, weight, omega, finals, back_ends, state_in, dtok.reshape(G, L, D), factors)
    order = list(reversed(steps))

    def back_part(k, so_far):
        return ema_backward((k * sixth, sixth), tuple(so_far), *consts)

    so_far = back_part(0, ())
    *so_far, over_a, over_c = join(*so_far, over_a, over_c)
    sum_a.add(over_a)
    for mark in z_steps[2:]:
        sum_a.add(sum_a.send(mark))
    sum_c.add(over_c)
    over_c = sum_c.send(y_step)
    block = sum_a.value.astype(BF16)[None]
    more = exchange(block, "seq", order[0])
    so_far = back_part(1, so_far)
    *so_far, over_c, over_d, more = join(*so_far, over_c, over_d, more)
    sum_c.add(over_c)
    sum_d_.add(over_d)
    over_d = sum_d_.send(y_step)
    block = widen(block, more, order[0])
    more = exchange(block, "seq", order[1])
    so_far = back_part(2, so_far)
    *so_far, over_d, more = join(*so_far, over_d, more)
    sum_d_.add(over_d)
    *so_far, block = join(*so_far, widen(block, more, order[1]))
    more = exchange(block, "seq", order[2])
    cols_c = sum_c.value.shape[-1]
    sum_c.value = jnp.concatenate([sum_c.value, sum_d_.value], axis=-1)
    over_c = sum_c.send(z_steps[0])
    so_far = back_part(3, so_far)
    *so_far, over_c = join(*so_far, over_c)
    sum_c.add(over_c)
    over_c = sum_c.send(z_steps[1])
    so_far = back_part(4, so_far)
    *so_far, over_c = join(*so_far, over_c)
    sum_c.add(over_c)
    for mark in z_steps[2:]:
        sum_c.add(sum_c.send(mark))
    small = sum_c.value.astype(BF16)[None]
    over_c = exchange(small, "seq", order[0])
    so_far = back_part(5, so_far)
    *so_far, over_c, more = join(*so_far, over_c, more)
    small = widen(small, over_c, order[0])
    block = widen(block, more, order[2])
    for step in order[3:]:
        block = widen(block, exchange(block, "seq", step), step)
    input_grad, late = so_far
    over_c = exchange(small, "seq", order[1])
    late = late.reshape(-1, n_wsh, D // n_wsh).transpose(1, 0, 2)
    sides = jnp.concatenate([early[:, k : k + D // n_wsh] for k in range(0, D, D // n_wsh)])
    late = jnp.concatenate([late, jnp.broadcast_to(sides, (n_wsh,) + sides.shape)], axis=1)
    late, over_c = join(sum_over_wsh(late), over_c)
    small = widen(small, over_c, order[1])
    over_c = exchange(small, "seq", order[2])
    late, over_c = join(sum_over_seq(late), over_c)
    small = widen(small, over_c, order[2])
    for step in order[3:]:
        small = widen(small, exchange(small, "seq", step), step)
    block, small = in_order(block), in_order(small)
    g_a, g_b = block[:, :rows_a].reshape(-1, D).astype(F32), block[:, rows_a:].reshape(-1, D).astype(F32)
    small = small.reshape(-1, small.shape[-1]).astype(F32)
    g_c, g_d = small[:, :cols_c], small[:, cols_c:]
    input_grad = input_grad.reshape(tokens.shape)

    FF = ffn_in.shape[1]
    sides = late[4 * H + 8 :].reshape(n_wsh, 16, -1)
    early = jnp.concatenate([sides[k] for k in range(n_wsh)], axis=1)
    spans = {}
    for name, start, row, col, size in sum_spots(D, Z, V, FF):
        spans[name, start] = early[row, col : col + size]

    def span_of(name):
        return jnp.concatenate([spans[key] for key in sorted(spans) if key[0] == name])

    j = lax.axis_index("wsh")
    qk_sums, row_sums = span_of("qk"), span_of("rows")
    smalls = []
    for part in (
        span_of("mix"), span_of("value"), span_of("ffn"), span_of("rel"),
        *(qk_sums[k * Z : k * Z + Z] for k in range(3)), *(row_sums[k * D : k * D + D] for k in range(5)),
    ):
        size = part.shape[0] // n_wsh
        smalls.append(lax.dynamic_slice(part, (j * size,), (size,)))
    (
        g_mix_bias, g_value_bias, g_ffn_in_bias, g_rel, g_gain_q, g_gain_k, g_shift, gain_1, gain_2, shift_1, shift_2,
        g_ffn_out_bias,
    ) = smalls
    late = late[: 4 * H + 1].T
    tall_rows, wide_rows = ffn_out.shape[0], ffn_in.shape[0]
    n_seq = lax.axis_size("seq")
    first_rows = tall_rows // n_seq

    def unmerge(merged):
        parts = merged.reshape(n_seq, -1, D)
        top = parts[:, :first_rows].reshape(tall_rows, D)
        sides = parts[:, first_rows:].reshape(n_seq, 2, wide_rows // n_seq, D)
        return top, jnp.concatenate([sides[:, k].reshape(wide_rows, D) for k in range(2)], axis=1)

    g_ffn_out, g_ffn_in = unmerge(g_a)
    g_out, g_edges = unmerge(g_b)
    g_mix = jnp.concatenate([g_edges[:, :D], g_c, g_edges[:, D:]], axis=1)
    return (
        output.reshape(tokens.shape), input_grad,
        late[:, 0:H], late[:, H : 2 * H], late[:, 2 * H : 3 * H], late[:, 3 * H : 4 * H], late[:, 4 * H],
        g_mix, g_mix_bias, g_d, g_value_bias,
        jnp.stack([g_gain_q, g_gain_k], axis=1), g_shift, g_rel, g_out,
        jnp.stack([gain_1, gain_2], axis=1), jnp.stack([shift_1, shift_2], axis=1),
        g_ffn_in, g_ffn_in_bias, g_ffn_out, g_ffn_out_bias,
    )


def solution(mesh):
    in_specs = (
        P(None, "wsh", "seq", None),
        P(None, "wsh", "seq", None),
        P(None, "wsh"),
        P("wsh", None),
        P("wsh", None),
        P("wsh", None),
        P("wsh", None),
        P("wsh"),
        P("wsh", None),
        P("wsh"),
        P("wsh", None),
        P("wsh"),
        P("wsh", None),
        P("wsh"),
        P("wsh"),
        P("wsh", None),
        P("wsh", None),
        P("wsh", None),
        P("wsh", None),
        P("wsh"),
        P("wsh", None),
        P("wsh"),
    )
    out_specs = (
        P(None, "wsh", "seq", None),
        P(None, "wsh", "seq", None),
        P("wsh", None),
        P("wsh", None),
        P("wsh", None),
        P("wsh", None),
        P("wsh"),
        P("wsh", None),
        P("wsh"),
        P("wsh", None),
        P("wsh"),
        P("wsh", None),
        P("wsh"),
        P("wsh"),
        P("wsh", None),
        P("wsh", None),
        P("wsh", None),
        P("wsh", None),
        P("wsh"),
        P("wsh", None),
        P("wsh"),
    )
    return jax.shard_map(body, mesh=mesh, in_specs=in_specs, out_specs=out_specs, check_vma=False)
```
